32 devices in a mesh: replica: 8 (over z, x), fsdp: 4 (over y, core).
Axes of the slice: x: 2, y: 2, z: 4, core: 2. Of those that a mesh axis runs over, the one named last changes fastest.
Arguments:
- hidden_in: bfloat16 [2, 32, 256, 2048], P(None, ('replica', 'fsdp')), may hold values from -6 to 6
- segment_ids: int32 [2, 32, 256], P(None, ('replica', 'fsdp')), may hold values from 0 to 15, never falling along the last dimension, each value on 1 to 128 neighbouring positions
- cotangent: bfloat16 [2, 32, 256, 2048], P(None, ('replica', 'fsdp')), may hold values from -6 to 6
- norm_gain: bfloat16 [2048], P('fsdp'), may hold values from 0.099609375 to 1.8984375
- w_in: bfloat16 [2048, 8512], P('fsdp'), may hold values from -0.125 to 0.125
- conv_weight: bfloat16 [4, 4352], P(None, 'fsdp'), may hold values from -3 to 3
- conv_bias: bfloat16 [4352], P('fsdp'), may hold values from -0.5 to 0.5
- dt_bias: bfloat16 [64], P('fsdp'), may hold values from -6 to -2
- a_log: bfloat16 [64], P('fsdp'), may hold values from 0 to 2
- skip_gain: bfloat16 [64], P('fsdp'), may hold values from 0.5 to 1.5
- gate_gain: bfloat16 [4096], P('fsdp'), may hold values from 0.099609375 to 1.8984375
- w_out: bfloat16 [4096, 2048], P('fsdp'), may hold values from -0.09375 to 0.09375
Outputs:
- block_out: bfloat16 [2, 32, 256, 2048], P(None, ('replica', 'fsdp'))
- grad_in: float32 [2, 32, 256, 2048], P(None, ('replica', 'fsdp'))
- grad_norm_gain: float32 [2048], P('fsdp')
- grad_w_in: float32 [2048, 8512], P('fsdp')
- grad_conv_weight: float32 [4, 4352], P(None, 'fsdp')
- grad_conv_bias: float32 [4352], P('fsdp')
- grad_dt_bias: float32 [64], P('fsdp')
- grad_a_log: float32 [64], P('fsdp')
- grad_skip_gain: float32 [64], P('fsdp')
- grad_gate_gain: float32 [4096], P('fsdp')
- grad_w_out: float32 [4096, 2048], P('fsdp')
The draws below stay inside these ranges and needn't reach their ends.
Inputs may be any that keep to these rules, and one draw needn't show every extreme that they name: `segment_ids`: along each sequence the numbers never fall; each document has 1 to 128 tokens.
All inputs are finite; a program needn't handle non-finite values.
Results may differ from the reference program's by a relative error of at most 0.0077.
Values may be sent and summed in bfloat16 or wider, within the bound.
A program may use at most 384 MiB of HBM per device.

```python
import math
import jax
import jax.numpy as jnp
import numpy as np
from jax import lax

D = 2048
HEADS = 64
KERNEL = 4
SEQ_LEN = 256
MICRO = 2
DOC_COUNT = 16
DOC_MOST = 128
INNER = 4096
CONV = 4352
PROJ = 8512
SEQS = 32


def block_levels(own_key, shape, shards, least, high):
    level, own = 1.0, jax.random.fold_in(own_key, 6)
    for dim, shards_of in shards:
        draws = jnp.exp(jax.random.uniform(jax.random.fold_in(own, dim), (shards_of,), jnp.float32, least / len(shards), high / len(shards)))
        level = level * jnp.repeat(draws, shape[dim] // shards_of).reshape([-1 if axis == dim else 1 for axis in range(len(shape))])
    return level


def split_up(number_of, total, bound, slope):
    weights = [(1 << 20) // math.isqrt(grade ** slope) + 1 for grade in range(2, number_of + 1)]
    surplus, counts = total - bound - (number_of - 1), [1] * (number_of - 1)
    while surplus > 0:
        free = [i for i in range(number_of - 1) if counts[i] < bound]
        whole, budget = sum([weights[i] for i in free]), surplus
        for i in free:
            extra = min(bound - counts[i], max(1, budget * weights[i] // whole), surplus)
            counts[i] = counts[i] + extra
            surplus = surplus - extra
    return np.array([bound] + counts)


def uneven_parts(rng, amount, total, reach, skew):
    if amount == 2:
        one = jax.random.randint(rng, (), max(1, total - reach), min(reach, total - 1) + 1)
        return jnp.stack([one, total - one])
    lengths = jnp.asarray(split_up(amount, total, reach, skew), jnp.int32)
    couples = (amount - 1) // 2
    giver, taker = lengths[1:1 + 2 * couples:2], lengths[2:2 + 2 * couples:2]
    slack = jnp.minimum(giver - 1, reach - taker)
    shifted = jax.random.randint(jax.random.fold_in(rng, 1), (couples,), 0, 1 << 20) % (slack + 1)
    lengths = lengths.at[1:1 + 2 * couples:2].set(giver - shifted).at[2:2 + 2 * couples:2].set(taker + shifted)
    return lengths[jax.random.permutation(jax.random.fold_in(rng, 2), amount)]


def centred(stream_key, shape, width, bound, shards=(), kind=jnp.bfloat16):
    values = jax.random.normal(stream_key, shape, jnp.float32) * width
    if len(shards) > 0:
        values = block_levels(stream_key, shape, shards, -0.22, 0.18) * values
    return jnp.clip(values, min=-bound, max=bound).astype(kind)


def setup_inputs(seed: int = 0) -> dict:
    streams_of = jax.random.split(jax.random.key(seed), 13)
    return {
        "hidden_in": centred(streams_of[0], (MICRO, SEQS, SEQ_LEN, D), 1.0, 6.0, ((1, 32),)),
        "segment_ids": jax.vmap(lambda own: jnp.searchsorted(jnp.cumsum(uneven_parts(own, DOC_COUNT, SEQ_LEN, DOC_MOST, 2)), jnp.arange(SEQ_LEN), side="right"))(jax.random.split(streams_of[1], MICRO * SEQS)).reshape((MICRO, SEQS, SEQ_LEN)).astype(jnp.int32),
        "cotangent": centred(streams_of[2], (MICRO, SEQS, SEQ_LEN, D), 1.0, 6.0, ((1, 32),)),
        "norm_gain": jnp.clip(1.0 + 0.18 * jax.random.normal(streams_of[3], (D,), jnp.float32), 0.099609375, 1.8984375).astype(jnp.bfloat16),
        "w_in": centred(streams_of[4], (D, PROJ), D ** -0.5, 0.125, ((0, 4),)),
        "conv_weight": centred(streams_of[5], (KERNEL, CONV), 0.5, 3.0, ((1, 4),)),
        "conv_bias": jnp.clip(jax.random.uniform(streams_of[6], (CONV,), jnp.float32, -0.5, 0.5) * block_levels(streams_of[6], (CONV,), ((0, 4),), -0.4, 0.0), -0.5, 0.5).astype(jnp.bfloat16),
        "dt_bias": jnp.clip(-6.0 + 4.0 * jax.random.uniform(streams_of[7], (HEADS,), jnp.float32) ** block_levels(streams_of[7], (HEADS,), ((0, 4),), -0.2, 0.2), -6.0, -2.0).astype(jnp.bfloat16),
        "a_log": jnp.clip(2.0 * jax.random.uniform(streams_of[8], (HEADS,), jnp.float32) ** block_levels(streams_of[8], (HEADS,), ((0, 4),), -0.2, 0.2), 0.0, 2.0).astype(jnp.bfloat16),
        "skip_gain": jnp.clip(0.5 + 1.0 * jax.random.uniform(streams_of[9], (HEADS,), jnp.float32) ** block_levels(streams_of[9], (HEADS,), ((0, 4),), -0.2, 0.2), 0.5, 1.5).astype(jnp.bfloat16),
        "gate_gain": jnp.clip(1.0 + 0.18 * jax.random.normal(streams_of[10], (INNER,), jnp.float32), 0.099609375, 1.8984375).astype(jnp.bfloat16),
        "w_out": centred(streams_of[11], (INNER, D), INNER ** -0.5, 0.09375, ((0, 4),)),
    }


EPS = 1e-05
HIGHEST = lax.Precision.HIGHEST

@jax.custom_vjp
def low(v):
    return lax.optimization_barrier(v.astype(jnp.bfloat16)).astype(jnp.float32)

@jax.custom_vjp
def low_back(v):
    return v

def low_keep(v):
    return (low(v), None)

def low_pass(kept, grad):
    return (grad,)

def back_keep(v):
    return (v, None)

def back_low(kept, grad):
    return (low(grad),)
low.defvjp(low_keep, low_pass)
low_back.defvjp(back_keep, back_low)

def pre_norm(inputs, gain):
    square_mean = lax.optimization_barrier(jnp.mean(inputs * inputs, -1, keepdims=True))
    return inputs * lax.rsqrt(square_mean + EPS) * gain

def mixer(projected, conv_weight, conv_bias, dt_bias, a_log, skip_gain, gate_gain, segments):
    length = projected.shape[0]
    inner_width = gate_gain.shape[0]
    head_count = dt_bias.shape[0]
    conv_width = conv_bias.shape[0]
    state_width = (conv_width - inner_width) // 2
    head_width = inner_width // head_count
    kernel_width = conv_weight.shape[0]
    gate_part = projected[:, :inner_width]
    conv_input = projected[:, inner_width:inner_width + conv_width]
    step_raw = projected[:, inner_width + conv_width:]
    convolved = conv_bias + conv_weight[0] * conv_input
    for offset in range(1, kernel_width):
        prior = jnp.concatenate([jnp.zeros((offset, conv_width), projected.dtype), conv_input[:-offset]], 0)
        same_doc = jnp.concatenate([jnp.zeros((offset,), projected.dtype), (segments[offset:] == segments[:-offset]).astype(projected.dtype)], 0)
        convolved = convolved + conv_weight[offset] * prior * same_doc[:, None]
    activated = jax.nn.silu(convolved)
    values_in = activated[:, :inner_width].reshape(length, head_count, head_width)
    state_in = activated[:, inner_width:inner_width + state_width]
    state_out = activated[:, inner_width + state_width:]
    step_size = jax.nn.softplus(step_raw + dt_bias)
    log_decay = -jnp.exp(a_log) * step_size
    cumulative = jnp.cumsum(log_decay, 0)
    position = jnp.arange(length)
    visible = (position[:, None] >= position[None, :]) & (segments[:, None] == segments[None, :])
    distance = jnp.where(visible[:, :, None], cumulative[:, None, :] - cumulative[None, :, :], 0.0)
    decays = jnp.where(visible[:, :, None], jnp.exp(distance), 0.0)
    affinity = jnp.dot(state_out, state_in.T, precision=HIGHEST)
    weights_ts = affinity[:, :, None] * decays * step_size[None, :, :]
    output_sum = jnp.einsum('tsh,shp->thp', weights_ts, values_in, precision=HIGHEST) + skip_gain[:, None] * values_in
    output_sum = output_sum.reshape(length, inner_width)
    gated_out = output_sum * jax.nn.silu(gate_part)
    square_mean = lax.optimization_barrier(jnp.mean(gated_out * gated_out, -1, keepdims=True))
    return gated_out * lax.rsqrt(square_mean + EPS) * gate_gain

def block_forward(inputs, norm_gain, w_in, conv_weight, conv_bias, dt_bias, a_log, skip_gain, gate_gain, w_out, segments):
    scaled = pre_norm(inputs, norm_gain)
    projected = low_back(jnp.dot(low(scaled), w_in, precision=HIGHEST))
    normed = mixer(projected, conv_weight, conv_bias, dt_bias, a_log, skip_gain, gate_gain, segments)
    return inputs + jnp.dot(low(normed), w_out, precision=HIGHEST)

def reference(hidden_in, segment_ids, cotangent, norm_gain, w_in, conv_weight, conv_bias, dt_bias, a_log, skip_gain, gate_gain, w_out):
    rows_in = hidden_in.reshape(-1, SEQ_LEN, D).astype(jnp.float32)
    rows_seg = segment_ids.reshape(-1, SEQ_LEN).astype(jnp.int32)
    rows_cot = cotangent.reshape(-1, SEQ_LEN, D).astype(jnp.float32)
    params = tuple((weight.astype(jnp.float32) for weight in (norm_gain, w_in, conv_weight, conv_bias, dt_bias, a_log, skip_gain, gate_gain, w_out)))

    def one_sequence(totals, packed):
        inputs, segments, cotan = packed

        def local_forward(inputs_now, *weights):
            return block_forward(inputs_now, *weights, segments)
        result, back_fn = jax.vjp(local_forward, inputs, *params)
        grads = back_fn(cotan)
        summed = tuple((carried + added for carried, added in zip(totals, grads[1:])))
        return (summed, (result.astype(jnp.bfloat16), grads[0]))
    start = tuple((jnp.zeros(weight.shape, jnp.float32) for weight in params))
    totals, (outputs, grad_rows) = lax.scan(one_sequence, start, (rows_in, rows_seg, rows_cot))
    return (outputs.reshape(hidden_in.shape), grad_rows.reshape(hidden_in.shape), totals[0], totals[1], totals[2], totals[3], totals[4], totals[5], totals[6], totals[7], totals[8])
```

```python
import functools

import jax
import jax.numpy as jnp
from jax import lax
from jax.experimental import pallas as pl
from jax.experimental.pallas import tpu as pltpu
from jax.sharding import PartitionSpec as P

EPS = 1e-05
HIGHEST = lax.Precision.HIGHEST
LANES = 128
F32 = jnp.float32
BF16 = jnp.bfloat16
LOG2E = 1.4426950408889634


def contract_rows(left, right, precision=None):
    return lax.dot_general(
        left, right, (((0,), (0,)), ((), ())), precision=precision, preferred_element_type=F32
    )


def contract_cols(left, right, precision=None):
    return lax.dot_general(
        left, right, (((1,), (1,)), ((), ())), precision=precision, preferred_element_type=F32
    )


def sigmoid(v):
    return 1.0 / (1.0 + jnp.exp(-v))


def convolve(conv_input, taps, bias, mask_refs):
    total = bias + taps[0] * conv_input
    shifted = []
    for offset in range(1, len(taps)):
        prior = pltpu.roll(conv_input, offset, 0) * mask_refs[offset - 1]
        shifted.append(prior)
        total = total + taps[offset] * prior
    return total, shifted


def prepare(dims, own_ref, proj_ref, seg_col_ref, seg_row_ref, mask_ref, head_ref, cw_ref,
            mask_wide, visible_bias, step_wide, cum_wide, cum_rows, state_act, affinity):
    tokens, inner, state2, heads, local_heads, taps = dims
    for offset in range(taps - 1):
        mask_wide[offset] = jnp.broadcast_to(mask_ref[:, offset : offset + 1], (tokens, LANES))
    rows = lax.broadcasted_iota(jnp.int32, (tokens, tokens), 0)
    cols = lax.broadcasted_iota(jnp.int32, (tokens, tokens), 1)
    visible = (rows >= cols) & (seg_col_ref[...] == seg_row_ref[...])
    visible_bias[...] = jnp.where(visible, 0.0, -1e30)
    common = 2 * inner
    raw = proj_ref[:, common + state2 : common + state2 + heads]
    raw = jnp.concatenate([raw, jnp.zeros((tokens, LANES - heads), F32)], 1)
    raw = pltpu.roll(raw, LANES - own_ref[0] * local_heads, 1)
    raw = raw + head_ref[0:1, :]
    step = jnp.maximum(raw, 0.0) + jnp.log1p(jnp.exp(-jnp.abs(raw)))
    log_decay = head_ref[1:2, :] * step
    lower = jnp.where(rows >= cols, 1.0, 0.0).astype(F32)
    cumulative = jnp.dot(lower, log_decay, precision=HIGHEST, preferred_element_type=F32)
    scaled_cum = cumulative * LOG2E
    flipped = scaled_cum.T
    lane = lax.broadcasted_iota(jnp.int32, (tokens, LANES), 1)
    for head in range(local_heads):
        cum_wide[head] = jnp.broadcast_to(scaled_cum[:, head : head + 1], (tokens, LANES))
        cum_rows[head] = flipped[head : head + 1, :]
    for pair in range(local_heads // 2):
        step_wide[pair] = jnp.where(
            lane < LANES // 2, step[:, 2 * pair : 2 * pair + 1], step[:, 2 * pair + 1 : 2 * pair + 2]
        )
    for part in range(state2 // LANES):
        at = inner + part * LANES
        conv, _ = convolve(
            proj_ref[:, common + part * LANES : common + (part + 1) * LANES],
            [cw_ref[j : j + 1, at : at + LANES] for j in range(taps)],
            cw_ref[taps : taps + 1, at : at + LANES],
            mask_wide,
        )
        state_act[part] = conv * sigmoid(conv)
    affinity[...] = contract_cols(state_act[1], state_act[0], HIGHEST)
    return raw, step, log_decay, rows, cols


def forward_kernel(dims, own_ref, proj_ref, seg_col_ref, seg_row_ref, mask_ref, head_ref, cw_ref, chan_ref,
                   gated_ref, square_ref,
                   mask_wide, visible_bias, step_wide, cum_wide, cum_rows, state_act, affinity):
    tokens, inner, state2, heads, local_heads, taps = dims
    prepare(dims, own_ref, proj_ref, seg_col_ref, seg_row_ref, mask_ref, head_ref, cw_ref,
            mask_wide, visible_bias, step_wide, cum_wide, cum_rows, state_act, affinity)
    lane = lax.broadcasted_iota(jnp.int32, (tokens, LANES), 1)
    first = lane < LANES // 2
    blocks = tokens // LANES

    def pair_step(pair, squares):
        here = pl.ds(pl.multiple_of(pair * LANES, LANES), LANES)
        conv, _ = convolve(
            proj_ref[:, here], [cw_ref[j : j + 1, here] for j in range(taps)],
            cw_ref[taps : taps + 1, here], mask_wide,
        )
        values = conv * sigmoid(conv)
        weighted = values * step_wide[pair]
        out = chan_ref[0:1, here] * values
        parts = [out[b * LANES : (b + 1) * LANES] for b in range(blocks)]
        for which in range(2):
            head = 2 * pair + which
            mine = jnp.where(first == (which == 0), weighted, 0.0).astype(BF16)
            for tb in range(blocks):
                t_rows = slice(tb * LANES, (tb + 1) * LANES)
                pieces = []
                for sb in range(tb + 1):
                    s_cols = slice(sb * LANES, (sb + 1) * LANES)
                    distance = (cum_wide[head, t_rows, :] - cum_rows[head, :, s_cols]) + visible_bias[t_rows, s_cols]
                    pieces.append((affinity[t_rows, s_cols] * jnp.exp2(distance)).astype(BF16))
                weights = jnp.concatenate(pieces, 1) if tb > 0 else pieces[0]
                parts[tb] = parts[tb] + jnp.dot(
                    weights, mine[: (tb + 1) * LANES], preferred_element_type=F32
                )
        out = jnp.concatenate(parts, 0)
        gate = proj_ref[:, pl.ds(pl.multiple_of(inner + pair * LANES, LANES), LANES)]
        gated = out * (gate * sigmoid(gate))
        gated_ref[:, here] = (gated * chan_ref[1:2, here]).astype(BF16)
        return squares + gated * gated

    squares = lax.fori_loop(0, local_heads // 2, pair_step, jnp.zeros((tokens, LANES), F32))
    square_ref[...] = jnp.sum(squares, 1, keepdims=True)


def backward_kernel(dims, own_ref, proj_ref, seg_col_ref, seg_row_ref, mask_ref, head_ref, cw_ref, chan_ref,
                    stats_ref, gn_ref,
                    gp_ref, grad_cw_ref, grad_chan_ref, grad_head_ref,
                    mask_wide, visible_bias, step_wide, cum_wide, cum_rows, state_act, affinity,
                    grad_affinity, row_sums, col_sums, wide_stats):
    tokens, inner, state2, heads, local_heads, taps = dims

    @pl.when(pl.program_id(0) == 0)
    def _():
        grad_cw_ref[...] = jnp.zeros_like(grad_cw_ref)
        grad_chan_ref[...] = jnp.zeros_like(grad_chan_ref)
        grad_head_ref[...] = jnp.zeros_like(grad_head_ref)

    raw, step, log_decay, rows, cols = prepare(
        dims, own_ref, proj_ref, seg_col_ref, seg_row_ref, mask_ref, head_ref, cw_ref,
        mask_wide, visible_bias, step_wide, cum_wide, cum_rows, state_act, affinity)
    grad_affinity[...] = jnp.zeros_like(grad_affinity)
    row_sums[...] = jnp.zeros_like(row_sums)
    col_sums[...] = jnp.zeros_like(col_sums)
    wide_stats[0] = jnp.broadcast_to(stats_ref[:, 0:1], (tokens, LANES))
    wide_stats[1] = jnp.broadcast_to(stats_ref[:, 1:2], (tokens, LANES))
    lane = lax.broadcasted_iota(jnp.int32, (tokens, LANES), 1)
    block_lane = lax.broadcasted_iota(jnp.int32, (LANES, LANES), 1)
    first = lane < LANES // 2
    blocks = tokens // LANES

    def conv_back(grad_conv, shifted, conv_input, here):
        grad_cw_ref[0:1, here] += jnp.sum(grad_conv * conv_input, 0, keepdims=True)
        grad_cw_ref[taps : taps + 1, here] += jnp.sum(grad_conv, 0, keepdims=True)
        back = cw_ref[0:1, here] * grad_conv
        for offset in range(1, taps):
            grad_cw_ref[offset : offset + 1, here] += jnp.sum(grad_conv * shifted[offset - 1], 0, keepdims=True)
            term = (cw_ref[offset : offset + 1, here] * grad_conv) * mask_wide[offset - 1]
            back = back + pltpu.roll(term, tokens - offset, 0)
        return back

    def pair_step(pair, carry):
        here = pl.ds(pl.multiple_of(pair * LANES, LANES), LANES)
        there = pl.ds(pl.multiple_of(inner + pair * LANES, LANES), LANES)
        conv_input = proj_ref[:, here]
        conv, shifted = convolve(
            conv_input, [cw_ref[j : j + 1, here] for j in range(taps)],
            cw_ref[taps : taps + 1, here], mask_wide,
        )
        conv_sig = sigmoid(conv)
        values = conv * conv_sig
        weighted = values * step_wide[pair]
        skip = chan_ref[0:1, here]
        halves = [jnp.where(first == (which == 0), weighted, 0.0).astype(BF16) for which in range(2)]
        out_parts = [(skip * values)[b * LANES : (b + 1) * LANES] for b in range(blocks)]
        for which in range(2):
            head = 2 * pair + which
            for tb in range(blocks):
                t_rows = slice(tb * LANES, (tb + 1) * LANES)
                pieces = []
                for sb in range(tb + 1):
                    s_cols = slice(sb * LANES, (sb + 1) * LANES)
                    distance = (cum_wide[head, t_rows, :] - cum_rows[head, :, s_cols]) + visible_bias[t_rows, s_cols]
                    pieces.append((affinity[t_rows, s_cols] * jnp.exp2(distance)).astype(BF16))
                weights = jnp.concatenate(pieces, 1) if tb > 0 else pieces[0]
                out_parts[tb] = out_parts[tb] + jnp.dot(
                    weights, halves[which][: (tb + 1) * LANES], preferred_element_type=F32
                )
        out = jnp.concatenate(out_parts, 0)
        gate = proj_ref[:, there]
        gate_sig = sigmoid(gate)
        gate_silu = gate * gate_sig
        gated = out * gate_silu
        gn = gn_ref[:, here]
        gain = chan_ref[1:2, here]
        root = wide_stats[0]
        grad_chan_ref[1:2, here] += jnp.sum(gn * gated * root, 0, keepdims=True)
        grad_gated = root * (gn * gain) - gated * wide_stats[1]
        grad_out = grad_gated * gate_silu
        gp_ref[:, there] = (grad_gated * out * (gate_sig * (1.0 + gate * (1.0 - gate_sig)))).astype(BF16)
        grad_chan_ref[0:1, here] += jnp.sum(grad_out * values, 0, keepdims=True)
        back_parts = [jnp.zeros((LANES, LANES), F32) for _ in range(blocks)]
        for which in range(2):
            head = 2 * pair + which
            mine = jnp.where(first == (which == 0), grad_out, 0.0).astype(BF16)
            for tb in range(blocks):
                t_rows = slice(tb * LANES, (tb + 1) * LANES)
                sums = None
                for sb in range(tb + 1):
                    s_cols = slice(sb * LANES, (sb + 1) * LANES)
                    distance = (cum_wide[head, t_rows, :] - cum_rows[head, :, s_cols]) + visible_bias[t_rows, s_cols]
                    decay = jnp.exp2(distance)
                    weights = affinity[t_rows, s_cols] * decay
                    cross = contract_cols(mine[t_rows], halves[which][s_cols])
                    grad_affinity[t_rows, s_cols] += cross * decay
                    energy = cross * weights
                    col_sums[head, :, s_cols] += jnp.sum(energy, 0, keepdims=True)
                    sums = energy if sums is None else sums + energy
                    back_parts[sb] = back_parts[sb] + contract_rows(weights.astype(BF16), mine[t_rows])
                row_sums[t_rows, :] += jnp.where(
                    block_lane == head, jnp.sum(sums, 1, keepdims=True), 0.0
                )
        grad_values = jnp.concatenate(back_parts, 0) * step_wide[pair] + skip * grad_out
        grad_conv = grad_values * (conv_sig * (1.0 + conv * (1.0 - conv_sig)))
        gp_ref[:, here] = conv_back(grad_conv, shifted, conv_input, here).astype(BF16)
        return carry

    lax.fori_loop(0, local_heads // 2, pair_step, 0)

    common = 2 * inner
    grad_states = [
        contract_rows(grad_affinity[...], state_act[1], HIGHEST),
        jnp.dot(grad_affinity[...], state_act[0], precision=HIGHEST, preferred_element_type=F32),
    ]
    for part in range(state2 // LANES):
        at = slice(inner + part * LANES, inner + (part + 1) * LANES)
        spot = slice(common + part * LANES, common + (part + 1) * LANES)
        conv_input = proj_ref[:, spot]
        conv, shifted = convolve(
            conv_input, [cw_ref[j : j + 1, at] for j in range(taps)], cw_ref[taps : taps + 1, at], mask_wide
        )
        conv_sig = sigmoid(conv)
        grad_conv = grad_states[part] * (conv_sig * (1.0 + conv * (1.0 - conv_sig)))
        gp_ref[:, spot] = conv_back(grad_conv, shifted, conv_input, at).astype(BF16)

    col_rows = [col_sums[head] for head in range(local_heads)]
    col_rows.append(jnp.zeros((LANES - local_heads, tokens), F32))
    col_energy = jnp.concatenate(col_rows, 0).T
    upper = jnp.where(cols >= rows, 1.0, 0.0).astype(F32)
    grad_decay = jnp.dot(upper, row_sums[...] - col_energy, precision=HIGHEST, preferred_element_type=F32)
    step_sig = sigmoid(raw)
    ratio = jnp.where(raw < -20.0, 1.0, step_sig / jnp.maximum(step, 1e-30))
    grad_raw = col_energy * ratio + (head_ref[1:2, :] * grad_decay) * step_sig
    grad_head_ref[0:1, :] += jnp.sum(grad_raw, 0, keepdims=True)
    grad_head_ref[1:2, :] += jnp.sum(grad_decay * log_decay, 0, keepdims=True)
    placed = pltpu.roll(grad_raw, own_ref[0] * local_heads, 1)
    gp_ref[:, common + state2 : common + state2 + heads] = placed[:, :heads].astype(BF16)


def mixer_specs(dims, width):
    tokens, inner, state2, heads, local_heads, taps = dims
    fixed = lambda shape: pl.BlockSpec(shape, lambda s: (0,) * len(shape))
    in_specs = [
        pl.BlockSpec(memory_space=pltpu.SMEM),
        pl.BlockSpec((tokens, width), lambda s: (s, 0)),
        pl.BlockSpec((None, tokens, 1), lambda s: (s, 0, 0)),
        pl.BlockSpec((None, 1, tokens), lambda s: (s, 0, 0)),
        pl.BlockSpec((None, tokens, 8), lambda s: (s, 0, 0)),
        fixed((8, LANES)),
        fixed((8, inner + state2)),
        fixed((8, inner)),
    ]
    scratch = [
        pltpu.VMEM((taps - 1, tokens, LANES), F32),
        pltpu.VMEM((tokens, tokens), F32),
        pltpu.VMEM((local_heads // 2, tokens, LANES), F32),
        pltpu.VMEM((local_heads, tokens, LANES), F32),
        pltpu.VMEM((local_heads, 1, tokens), F32),
        pltpu.VMEM((state2 // LANES, tokens, LANES), F32),
        pltpu.VMEM((tokens, tokens), F32),
    ]
    return in_specs, scratch


def mix_forward(dims, operands):
    tokens, inner, state2, heads, local_heads, taps = dims
    total, width = operands[1].shape
    in_specs, scratch = mixer_specs(dims, width)
    return pl.pallas_call(
        functools.partial(forward_kernel, dims),
        grid=(total // tokens,),
        in_specs=in_specs,
        out_specs=[
            pl.BlockSpec((tokens, inner), lambda s: (s, 0)),
            pl.BlockSpec((tokens, 1), lambda s: (s, 0)),
        ],
        out_shape=[
            jax.ShapeDtypeStruct((total, inner), BF16),
            jax.ShapeDtypeStruct((total, 1), F32),
        ],
        scratch_shapes=scratch,
        compiler_params=pltpu.CompilerParams(vmem_limit_bytes=48 << 20),
        cost_estimate=pl.CostEstimate(
            flops=total * local_heads * tokens * 4 * 64,
            bytes_accessed=total * width * 4,
            transcendentals=total * local_heads * tokens,
        ),
        name="mix_forward",
    )(*operands)


def mix_backward(dims, operands, stats, grad_normed):
    tokens, inner, state2, heads, local_heads, taps = dims
    total, width = operands[1].shape
    in_specs, scratch = mixer_specs(dims, width)
    fixed = lambda shape: pl.BlockSpec(shape, lambda s: (0,) * len(shape))
    return pl.pallas_call(
        functools.partial(backward_kernel, dims),
        grid=(total // tokens,),
        in_specs=in_specs + [
            pl.BlockSpec((tokens, 2), lambda s: (s, 0)),
            pl.BlockSpec((tokens, inner), lambda s: (s, 0)),
        ],
        out_specs=[
            pl.BlockSpec((tokens, width), lambda s: (s, 0)),
            fixed((8, inner + state2)),
            fixed((8, inner)),
            fixed((8, LANES)),
        ],
        out_shape=[
            jax.ShapeDtypeStruct((total, width), BF16),
            jax.ShapeDtypeStruct((8, inner + state2), F32),
            jax.ShapeDtypeStruct((8, inner), F32),
            jax.ShapeDtypeStruct((8, LANES), F32),
        ],
        scratch_shapes=scratch + [
            pltpu.VMEM((tokens, tokens), F32),
            pltpu.VMEM((tokens, LANES), F32),
            pltpu.VMEM((local_heads, 1, tokens), F32),
            pltpu.VMEM((2, tokens, LANES), F32),
        ],
        compiler_params=pltpu.CompilerParams(vmem_limit_bytes=48 << 20),
        cost_estimate=pl.CostEstimate(
            flops=total * local_heads * tokens * 12 * 64,
            bytes_accessed=total * width * 6,
            transcendentals=2 * total * local_heads * tokens,
        ),
        name="mix_backward",
    )(*operands, stats, grad_normed)


def swap(array, axis, size, bit):
    return lax.ppermute(array, axis, [(i, i ^ bit) for i in range(size)])


def axis_bits(size):
    bits = []
    bit = 1
    while bit < size:
        bits.append(bit)
        bit *= 2
    return bits


def gather_relative(array, axis, size):
    held = array[None]
    for bit in reversed(axis_bits(size)):
        held = jnp.concatenate([held, swap(held, axis, size, bit)], 0)
    return held


def scatter_relative(array, axis, size):
    total = array
    for bit in axis_bits(size):
        half = total.shape[0] // 2
        received = swap(total[half:].astype(BF16), axis, size, bit)
        total = total[:half].astype(F32) + received.astype(F32)
    return total[0]


def sum_tokens(array, axis, size):
    kinds, tokens = array.shape
    for bit in axis_bits(size):
        stride = tokens // (2 * bit)
        received = swap(array, axis, size, bit).reshape(kinds, bit, 2, stride)
        array = array + received[:, :, ::-1].reshape(kinds, tokens)
    return array


def halve_sum(array, order, replica, size):
    total = array
    for bit in order:
        blocks, rows, columns = total.shape
        mine = (replica // bit) % 2
        halves = total.reshape(blocks, 2, rows // 2, columns)
        kept = lax.dynamic_index_in_dim(halves, mine, 1, keepdims=False)
        sent = lax.dynamic_index_in_dim(halves, 1 - mine, 1, keepdims=False)
        received = swap(sent.astype(BF16), "replica", size, bit)
        total = kept + received.astype(F32)
    return total


def double_gather(array, order, replica, size):
    held = array
    for bit in reversed(order):
        received = swap(held, "replica", size, bit)
        upper = (replica // bit) % 2 == 1
        held = jnp.where(
            upper,
            jnp.concatenate([received, held], 1),
            jnp.concatenate([held, received], 1),
        )
    return held


def flip(index, bit):
    return index + bit * (1 - 2 * ((index // bit) % 2))


def reduce_chunks(size, copies, depth, inner, common, out_rows, width):
    bits = axis_bits(copies)
    first, second = bits, bits[1:] + bits[:1]
    chunks = []
    for index in range(out_rows // OUT_CHUNK):
        chunks.append(("out", index, second if index % 2 else first))
    for index in range(2 * inner // COL_CHUNK):
        chunks.append(("in", index, second if index % 2 else first))
    chunks.append(("shared", 0, first))
    return chunks


COL_CHUNK = 256
OUT_CHUNK = 256
STAGES = ("keep", "got0", "sent1", "got1", "sent2", "got2", "final")


def reduce_kernel(plan, in_ref, out_ref, sum_in_ref, sum_shared_ref, sum_out_ref, *scratch):
    size, copies, chunks, shapes = plan
    groups = {}
    position = 0
    for name in shapes:
        groups[name] = dict(zip(STAGES, scratch[position : position + len(STAGES)]))
        position += len(STAGES)
    shared_in, shared_sum = scratch[position], scratch[position + 1]
    send_sems, recv_sems, local_sems = scratch[position + 2 :]
    me = lax.axis_index("fsdp")
    replica = lax.axis_index("replica")
    levels = len(axis_bits(copies))
    MESH = pl.DeviceIdType.MESH

    def replica_peer(bit):
        return (flip(replica, bit), me)

    def copy_peer(offset):
        other = me
        for bit in axis_bits(size):
            if offset & bit:
                other = flip(other, bit)
        return other

    barrier = pltpu.get_barrier_semaphore()
    peers = [replica_peer(bit) for bit in axis_bits(copies)]
    peers += [(replica, copy_peer(offset)) for offset in range(1, size)]
    for peer in peers:
        pl.semaphore_signal(barrier, inc=1, device_id=peer, device_id_type=MESH)
    pl.semaphore_wait(barrier, len(peers))

    def run(number, group, index, order):
        blocks, rows, columns = shapes[group]
        if group == "in":
            source, target = in_ref, sum_in_ref
            cut = lambda ref, at, count: ref.at[:, pl.ds(at, count), pl.ds(index * columns, columns)]
        elif group == "shared":
            source, target = in_ref, sum_shared_ref
            cut = lambda ref, at, count: ref.at[:, pl.ds(at, count), pl.ds(in_ref.shape[2] - columns, columns)]
        else:
            source, target = out_ref, sum_out_ref
            cut = lambda ref, at, count: ref.at[pl.ds(index, 1), pl.ds(at, count)]
        if group == "shared":
            place = lambda at, count: target.at[pl.ds(at, count)]
        else:
            place = lambda at, count: cut(target, at, count)
        held = {name: groups[group][name].at[index] for name in STAGES}
        sizes = [rows >> (level + 1) for level in range(levels)]
        upper = [(replica // bit) % 2 for bit in order]
        starts = [0]
        for level in range(levels):
            starts.append(pl.multiple_of(starts[-1] + upper[level] * sizes[level], sizes[-1]))
        sem = 0
        pending = []

        def send(from_ref, to_ref, device, slot):
            copy = pltpu.make_async_remote_copy(
                src_ref=from_ref, dst_ref=to_ref, send_sem=send_sems.at[number, slot],
                recv_sem=recv_sems.at[number, slot], device_id=device, device_id_type=MESH,
            )
            copy.start()
            pending.append(copy)
            return copy

        other = pl.multiple_of((1 - upper[0]) * sizes[0], sizes[0])
        keep_copy = pltpu.make_async_copy(cut(source, starts[1], sizes[0]), held["keep"], local_sems.at[number, 0])
        keep_copy.start()
        copy = send(cut(source, other, sizes[0]), held["got0"], replica_peer(order[0]), 0)
        yield
        keep_copy.wait()

        def summed(level, at, count):
            total = None
            for name, base in [("keep", 1)] + [("got%d" % l, l + 1) for l in range(level)]:
                local = pl.multiple_of(at - starts[base], count)
                part = held[name][:, pl.ds(local, count), :].astype(F32)
                total = part if total is None else total + part
            return total

        for level in range(1, levels):
            copy.wait_recv()
            there = starts[level] + (1 - upper[level]) * sizes[level]
            held["sent%d" % level][...] = summed(level, there, sizes[level]).astype(BF16)
            copy = send(held["sent%d" % level], held["got%d" % level], replica_peer(order[level]), level)
            yield
        copy.wait_recv()
        held["final"][...] = summed(levels, starts[levels], sizes[-1]).astype(BF16)
        final = held["final"]
        here, count = starts[levels], sizes[-1]
        slot = levels
        if group == "out":
            own = pltpu.make_async_copy(final, place(here, count), local_sems.at[number, 1])
            own.start()
            own.wait()
        else:
            landing = shared_in if group == "shared" else None
            arrivals = []
            for offset in range(1, size):
                peer = copy_peer(offset)
                if group == "shared":
                    to_ref = shared_in.at[offset - 1]
                else:
                    to_ref = target.at[me, pl.ds(here, count), pl.ds(index * columns, columns)]
                arrivals.append(send(final.at[peer], to_ref, (replica, peer), slot))
                slot += 1
            if group == "shared":
                yield
                total = final[me].astype(F32)
                for offset in range(1, size):
                    arrivals[offset - 1].wait_recv()
                    total = total + shared_in[offset - 1].astype(F32)
                shared_sum[...] = total.astype(BF16)
                own = pltpu.make_async_copy(shared_sum, place(here, count), local_sems.at[number, 1])
                own.start()
                own.wait()
            else:
                own = pltpu.make_async_copy(
                    final.at[me], target.at[me, pl.ds(here, count), pl.ds(index * columns, columns)],
                    local_sems.at[number, 1],
                )
                own.start()
                yield
                own.wait()
                for arrival in arrivals:
                    arrival.wait_recv()
        for level in range(levels - 1, -1, -1):
            region = place(starts[level + 1], sizes[level])
            copy = send(region, region, replica_peer(order[level]), slot)
            slot += 1
            yield
            copy.wait_recv()
        for copy in pending:
            copy.wait_send()

    waiting = [run(number, *chunk) for number, chunk in enumerate(chunks)]
    active = []
    while waiting or active:
        active += waiting[:PER_TICK]
        waiting = waiting[PER_TICK:]
        still = []
        for steps in active:
            try:
                next(steps)
                still.append(steps)
            except StopIteration:
                pass
        active = still


PER_TICK = 2


def reduce_gradients(size, copies, depth, inner, common, grad_in, grad_out):
    width = grad_out.shape[2]
    chunks = reduce_chunks(size, copies, depth, inner, common, grad_out.shape[0] * OUT_CHUNK, width)
    shapes = {"out": (1, OUT_CHUNK, width), "in": (size, depth, COL_CHUNK), "shared": (size, depth, common)}
    counts = {name: sum(1 for chunk in chunks if chunk[0] == name) for name in shapes}
    scratch = []
    for name, (blocks, rows, columns) in shapes.items():
        fraction = {"keep": 2, "got0": 2, "sent1": 4, "got1": 4, "sent2": 8, "got2": 8, "final": 8}
        for stage in STAGES:
            scratch.append(pltpu.VMEM((counts[name], blocks, rows // fraction[stage], columns), BF16))
    scratch.append(pltpu.VMEM((size - 1, depth // copies, common), BF16))
    scratch.append(pltpu.VMEM((depth // copies, common), BF16))
    slots = 2 * len(axis_bits(copies)) + size - 1
    scratch.append(pltpu.SemaphoreType.DMA((len(chunks), slots)))
    scratch.append(pltpu.SemaphoreType.DMA((len(chunks), slots)))
    scratch.append(pltpu.SemaphoreType.DMA((len(chunks), 2)))
    anywhere = pl.BlockSpec(memory_space=pl.ANY)
    return pl.pallas_call(
        functools.partial(reduce_kernel, (size, copies, chunks, shapes)),
        in_specs=[anywhere] * 2,
        out_specs=[anywhere] * 3,
        out_shape=[
            jax.ShapeDtypeStruct((size, depth, 2 * inner), BF16),
            jax.ShapeDtypeStruct((depth, common), BF16),
            jax.ShapeDtypeStruct(grad_out.shape, BF16),
        ],
        scratch_shapes=scratch,
        compiler_params=pltpu.CompilerParams(
            collective_id=0, has_side_effects=True, vmem_limit_bytes=56 << 20
        ),
        cost_estimate=pl.CostEstimate(flops=0, bytes_accessed=700 << 20, transcendentals=0),
        name="reduce_gradients",
    )(grad_in, grad_out)


def small_pieces(size, copies, depth, inner, columns, me, replica, scaled_low, gp, normed_low, cot_all):
    replica_bits = axis_bits(copies)
    orders = [replica_bits, replica_bits[1:] + replica_bits[:1]]
    pieces = []
    part_rows = inner // 2
    for part in range(2):
        grad = contract_rows(normed_low[:, part * part_rows : (part + 1) * part_rows], cot_all)
        order = orders[part % 2]
        mine = halve_sum(grad[None], order, replica, copies)
        pieces.append(double_gather(mine.astype(BF16), order, replica, copies)[0])
    grad_w_out = jnp.concatenate(pieces, 0).astype(F32)


    def columns_sum(start, stop, order, shared):
        grad = contract_rows(scaled_low, gp[:, start:stop])
        mine = halve_sum(grad.reshape(size, depth, stop - start), order, replica, copies)
        own = lax.dynamic_index_in_dim(mine, me, 0, keepdims=False)
        got = [own]
        for offset in range(1, size):
            there = lax.dynamic_index_in_dim(mine, me ^ offset, 0, keepdims=False)
            got.append(swap(there.astype(BF16), "fsdp", size, offset))
        if shared:
            held = sum(block.astype(F32) for block in got)[None].astype(BF16)
        else:
            held = jnp.stack([block.astype(BF16) for block in got])
        return double_gather(held, order, replica, copies)

    halves = inner // 2
    value_parts = [columns_sum(c * halves, (c + 1) * halves, orders[c % 2], False) for c in range(2)]
    gate_parts = [
        columns_sum(inner + c * halves, inner + (c + 1) * halves, orders[c % 2], False) for c in range(2)
    ]
    shared_part = columns_sum(2 * inner, columns, orders[0], True)[0]

    def in_place(parts):
        placed = []
        for device in range(size):
            for part in parts:
                placed.append(lax.dynamic_index_in_dim(part, me ^ device, 0, keepdims=False))
        return placed

    grad_w_in = jnp.concatenate(in_place(gate_parts) + in_place(value_parts) + [shared_part], 1).astype(F32)
    return grad_w_in, grad_w_out


def on_device(copies, size, hidden_in, segment_ids, cotangent, norm_gain, w_in, conv_weight, conv_bias,
              dt_bias, a_log, skip_gain, gate_gain, w_out):
    micro_count, seq_count, tokens, width = hidden_in.shape
    own_rows = micro_count * seq_count * tokens
    total = size * own_rows
    inner = gate_gain.shape[0]
    local_heads = dt_bias.shape[0]
    heads = local_heads * size
    channel = inner // local_heads
    full_inner = inner * size
    taps, own_conv = conv_weight.shape
    conv_width = own_conv * size
    state2 = conv_width - full_inner
    depth = w_in.shape[0]
    common = state2 + heads
    columns = 2 * inner + common
    dims = (tokens, inner, state2, heads, local_heads, taps)
    me = lax.axis_index("fsdp")
    replica = lax.axis_index("replica")

    own_x = hidden_in.reshape(own_rows, width)
    own_cot = cotangent.reshape(own_rows, width)
    x_all = gather_relative(own_x, "fsdp", size).reshape(total, width)
    small = jnp.concatenate([norm_gain, conv_weight.reshape(-1), conv_bias])
    small = lax.all_gather(small, "fsdp", axis=0, tiled=False).astype(F32)
    full_norm = small[:, :depth].reshape(1, width)
    full_cw = small[:, depth : depth + taps * own_conv].reshape(size, taps, own_conv)
    full_cw = full_cw.transpose(1, 0, 2).reshape(taps, conv_width)
    full_cb = small[:, depth + taps * own_conv :].reshape(1, conv_width)
    seg_all = gather_relative(segment_ids.reshape(micro_count * seq_count, tokens), "fsdp", size)
    seg_all = seg_all.reshape(total // tokens, tokens)

    def columns_of(device):
        return jnp.concatenate(
            [
                lax.dynamic_slice(w_in, (0, full_inner + device * inner), (depth, inner)),
                lax.dynamic_slice(w_in, (0, device * inner), (depth, inner)),
                w_in[:, 2 * full_inner :],
            ],
            1,
        )

    w_cols = jnp.zeros((size * depth, columns), BF16)
    w_cols = lax.dynamic_update_slice(w_cols, columns_of(me), (me * depth, 0))
    for offset in range(1, size):
        received = swap(columns_of(me ^ offset), "fsdp", size, offset)
        w_cols = lax.dynamic_update_slice(w_cols, received, ((me ^ offset) * depth, 0))
    cot_all = gather_relative(own_cot, "fsdp", size).reshape(total, width)

    def normalise(inputs):
        wide = inputs.astype(F32)
        return lax.rsqrt(jnp.mean(wide * wide, -1, keepdims=True) + EPS)

    scaled_low = (x_all.astype(F32) * normalise(x_all) * full_norm).astype(BF16)
    projected = jnp.dot(scaled_low, w_cols, preferred_element_type=F32)

    conv_all = jnp.concatenate([full_cw, full_cb, jnp.zeros((7 - taps, conv_width), F32)], 0)
    conv_own = jnp.concatenate(
        [lax.dynamic_slice(conv_all, (0, me * inner), (8, inner)), conv_all[:, full_inner:]], 1
    )
    pad_heads = lambda row: jnp.pad(row.astype(F32), (0, LANES - local_heads))
    head_rows = jnp.stack([pad_heads(dt_bias), pad_heads(-jnp.exp(a_log.astype(F32)))])
    head_rows = jnp.pad(head_rows, ((0, 6), (0, 0)))
    chan_rows = jnp.stack([jnp.repeat(skip_gain.astype(F32), channel), gate_gain.astype(F32)])
    chan_rows = jnp.pad(chan_rows, ((0, 6), (0, 0)))
    same = []
    for offset in range(1, taps):
        equal = (seg_all[:, offset:] == seg_all[:, :-offset]).astype(F32)
        same.append(jnp.pad(equal, ((0, 0), (offset, 0))))
    same = jnp.pad(jnp.stack(same, 2), ((0, 0), (0, 0), (0, 9 - taps)))
    operands = (
        me.astype(jnp.int32).reshape(1), projected, seg_all[:, :, None], seg_all[:, None, :], same,
        head_rows, conv_own, chan_rows,
    )
    gated, squares = mix_forward(dims, operands)
    grad_normed = contract_cols(cot_all, w_out)
    cross = jnp.sum(gated.astype(F32) * grad_normed, 1)
    stats = sum_tokens(jnp.stack([squares[:, 0], cross]), "fsdp", size)
    root = lax.rsqrt(stats[0] / full_inner + EPS)
    pull = root * root * root * stats[1] / full_inner

    out_part = jnp.dot(gated, w_out, preferred_element_type=F32).astype(BF16)
    out_sum = scatter_relative(out_part.reshape(size, own_rows, width), "fsdp", size)
    block_out = (own_x.astype(F32) + root[:own_rows, None] * out_sum).astype(BF16)
    block_out = block_out.reshape(hidden_in.shape)

    normed_low = (gated.astype(F32) * root[:, None]).astype(BF16)
    gp, grad_conv, grad_chan, grad_head = mix_backward(
        dims, operands, jnp.stack([root, pull], 1), grad_normed
    )

    full_levels = copies == 8 and depth % (16 * copies) == 0 and inner % COL_CHUNK == 0
    if full_levels:
        grad_out = contract_rows(normed_low, cot_all).astype(BF16)
        grad_cols = contract_rows(scaled_low, gp).astype(BF16)
        sum_in, sum_shared, sum_out = reduce_gradients(
            size, copies, depth, inner, common,
            grad_cols.reshape(size, depth, columns), grad_out.reshape(inner // OUT_CHUNK, OUT_CHUNK, width),
        )
        grad_w_out = sum_out.reshape(inner, width).astype(F32)
        by_kind = [sum_in[device, :, inner:] for device in range(size)]
        by_kind += [sum_in[device, :, :inner] for device in range(size)]
        grad_w_in = jnp.concatenate(by_kind + [sum_shared], 1).astype(F32)
    else:
        grad_w_in, grad_w_out = small_pieces(
            size, copies, depth, inner, columns, me, replica, scaled_low, gp, normed_low, cot_all
        )

    scaled_part = contract_cols(gp, w_cols).astype(BF16)
    grad_scaled = scatter_relative(scaled_part.reshape(size, own_rows, width), "fsdp", size)
    own_wide = own_x.astype(F32)
    own_root = normalise(own_x)
    gained = grad_scaled * full_norm
    inner_mean = jnp.mean(gained * own_wide, -1, keepdims=True)
    grad_in = own_cot.astype(F32) + own_root * gained - own_wide * (own_root * own_root * own_root * inner_mean)
    grad_in = grad_in.reshape(hidden_in.shape)
    grad_norm = jnp.sum(grad_scaled * own_wide * own_root, 0)

    conv_full = jnp.zeros((8, conv_width), F32)
    conv_full = lax.dynamic_update_slice(conv_full, grad_conv[:, inner:], (0, full_inner))
    conv_full = lax.dynamic_update_slice(conv_full, grad_conv[:, :inner], (0, me * inner))
    conv_full = conv_full[: taps + 1].reshape(-1)
    skip_grad = grad_chan[0].reshape(local_heads, channel).sum(1)
    own_small = jnp.concatenate(
        [grad_head[0, :local_heads], grad_head[1, :local_heads], skip_grad, grad_chan[1]]
    )
    conv_full, grad_norm = lax.psum((conv_full, grad_norm), ("replica", "fsdp"))
    own_small = lax.psum(own_small, "replica")
    conv_full = lax.dynamic_slice(conv_full.reshape(taps + 1, conv_width), (0, me * own_conv), (taps + 1, own_conv))
    grad_norm = lax.dynamic_slice(grad_norm, (me * depth,), (depth,))
    return (
        block_out,
        grad_in,
        grad_norm,
        grad_w_in,
        conv_full[:taps],
        conv_full[taps],
        own_small[:local_heads],
        own_small[local_heads : 2 * local_heads],
        own_small[2 * local_heads : 3 * local_heads],
        own_small[3 * local_heads :],
        grad_w_out,
    )


def solution(mesh):
    rows = ("replica", "fsdp")
    placed = (
        P(None, rows, None, None),
        P(None, rows, None),
        P(None, rows, None, None),
        P("fsdp"),
        P("fsdp", None),
        P(None, "fsdp"),
        P("fsdp"),
        P("fsdp"),
        P("fsdp"),
        P("fsdp"),
        P("fsdp"),
        P("fsdp", None),
    )
    return jax.shard_map(
        functools.partial(on_device, mesh.shape["replica"], mesh.shape["fsdp"]),
        mesh=mesh,
        in_specs=placed,
        out_specs=(
            P(None, rows, None, None),
            P(None, rows, None, None),
            P("fsdp"),
            P("fsdp", None),
            P(None, "fsdp"),
            P("fsdp"),
            P("fsdp"),
            P("fsdp"),
            P("fsdp"),
            P("fsdp"),
            P("fsdp", None),
        ),
        check_vma=False,
    )
```

```python
import functools

import jax
import jax.numpy as jnp
from jax import lax
from jax.experimental import pallas as pl
from jax.experimental.pallas import tpu as pltpu
from jax.sharding import PartitionSpec as P

EPS = 1e-05
HIGHEST = lax.Precision.HIGHEST
LANES = 128
F32 = jnp.float32
BF16 = jnp.bfloat16
LOG2E = 1.4426950408889634


def contract_rows(left, right, precision=None):
    return lax.dot_general(
        left, right, (((0,), (0,)), ((), ())), precision=precision, preferred_element_type=F32
    )


def contract_cols(left, right, precision=None):
    return lax.dot_general(
        left, right, (((1,), (1,)), ((), ())), precision=precision, preferred_element_type=F32
    )


def sigmoid(v):
    return 1.0 / (1.0 + jnp.exp(-v))


def convolve(conv_input, taps, bias, mask_refs):
    total = bias + taps[0] * conv_input
    shifted = []
    for offset in range(1, len(taps)):
        prior = pltpu.roll(conv_input, offset, 0) * mask_refs[offset - 1]
        shifted.append(prior)
        total = total + taps[offset] * prior
    return total, shifted


def prepare(dims, own_ref, proj_ref, seg_col_ref, seg_row_ref, mask_ref, head_ref, cw_ref,
            mask_wide, visible_bias, step_wide, cum_wide, cum_rows, state_act, affinity):
    tokens, inner, state2, heads, local_heads, taps = dims
    for offset in range(taps - 1):
        mask_wide[offset] = jnp.broadcast_to(mask_ref[:, offset : offset + 1], (tokens, LANES))
    rows = lax.broadcasted_iota(jnp.int32, (tokens, tokens), 0)
    cols = lax.broadcasted_iota(jnp.int32, (tokens, tokens), 1)
    visible = (rows >= cols) & (seg_col_ref[...] == seg_row_ref[...])
    visible_bias[...] = jnp.where(visible, 0.0, -1e30)
    common = 2 * inner
    raw = proj_ref[:, common + state2 : common + state2 + heads]
    raw = jnp.concatenate([raw, jnp.zeros((tokens, LANES - heads), F32)], 1)
    raw = pltpu.roll(raw, LANES - own_ref[0] * local_heads, 1)
    raw = raw + head_ref[0:1, :]
    step = jnp.maximum(raw, 0.0) + jnp.log1p(jnp.exp(-jnp.abs(raw)))
    log_decay = head_ref[1:2, :] * step
    lower = jnp.where(rows >= cols, 1.0, 0.0).astype(F32)
    cumulative = jnp.dot(lower, log_decay, precision=HIGHEST, preferred_element_type=F32)
    scaled_cum = cumulative * LOG2E
    flipped = scaled_cum.T
    lane = lax.broadcasted_iota(jnp.int32, (tokens, LANES), 1)
    for head in range(local_heads):
        cum_wide[head] = jnp.broadcast_to(scaled_cum[:, head : head + 1], (tokens, LANES))
        cum_rows[head] = flipped[head : head + 1, :]
    for pair in range(local_heads // 2):
        step_wide[pair] = jnp.where(
            lane < LANES // 2, step[:, 2 * pair : 2 * pair + 1], step[:, 2 * pair + 1 : 2 * pair + 2]
        )
    for part in range(state2 // LANES):
        at = inner + part * LANES
        conv, _ = convolve(
            proj_ref[:, common + part * LANES : common + (part + 1) * LANES],
            [cw_ref[j : j + 1, at : at + LANES] for j in range(taps)],
            cw_ref[taps : taps + 1, at : at + LANES],
            mask_wide,
        )
        state_act[part] = conv * sigmoid(conv)
    affinity[...] = contract_cols(state_act[1], state_act[0], HIGHEST)
    return raw, step, log_decay, rows, cols


def forward_kernel(dims, own_ref, proj_ref, seg_col_ref, seg_row_ref, mask_ref, head_ref, cw_ref, chan_ref,
                   gated_ref, square_ref,
                   mask_wide, visible_bias, step_wide, cum_wide, cum_rows, state_act, affinity):
    tokens, inner, state2, heads, local_heads, taps = dims
    prepare(dims, own_ref, proj_ref, seg_col_ref, seg_row_ref, mask_ref, head_ref, cw_ref,
            mask_wide, visible_bias, step_wide, cum_wide, cum_rows, state_act, affinity)
    lane = lax.broadcasted_iota(jnp.int32, (tokens, LANES), 1)
    first = lane < LANES // 2
    blocks = tokens // LANES

    def pair_step(pair, squares):
        here = pl.ds(pl.multiple_of(pair * LANES, LANES), LANES)
        conv, _ = convolve(
            proj_ref[:, here], [cw_ref[j : j + 1, here] for j in range(taps)],
            cw_ref[taps : taps + 1, here], mask_wide,
        )
        values = conv * sigmoid(conv)
        weighted = values * step_wide[pair]
        out = chan_ref[0:1, here] * values
        parts = [out[b * LANES : (b + 1) * LANES] for b in range(blocks)]
        for which in range(2):
            head = 2 * pair + which
            mine = jnp.where(first == (which == 0), weighted, 0.0).astype(BF16)
            for tb in range(blocks):
                t_rows = slice(tb * LANES, (tb + 1) * LANES)
                pieces = []
                for sb in range(tb + 1):
                    s_cols = slice(sb * LANES, (sb + 1) * LANES)
                    distance = (cum_wide[head, t_rows, :] - cum_rows[head, :, s_cols]) + visible_bias[t_rows, s_cols]
                    pieces.append((affinity[t_rows, s_cols] * jnp.exp2(distance)).astype(BF16))
                weights = jnp.concatenate(pieces, 1) if tb > 0 else pieces[0]
                parts[tb] = parts[tb] + jnp.dot(
                    weights, mine[: (tb + 1) * LANES], preferred_element_type=F32
                )
        out = jnp.concatenate(parts, 0)
        gate = proj_ref[:, pl.ds(pl.multiple_of(inner + pair * LANES, LANES), LANES)]
        gated = out * (gate * sigmoid(gate))
        gated_ref[:, here] = (gated * chan_ref[1:2, here]).astype(BF16)
        return squares + gated * gated

    squares = lax.fori_loop(0, local_heads // 2, pair_step, jnp.zeros((tokens, LANES), F32))
    square_ref[...] = jnp.sum(squares, 1, keepdims=True)


def backward_kernel(dims, own_ref, proj_ref, seg_col_ref, seg_row_ref, mask_ref, head_ref, cw_ref, chan_ref,
                    stats_ref, gn_ref,
                    gp_ref, grad_cw_ref, grad_chan_ref, grad_head_ref,
                    mask_wide, visible_bias, step_wide, cum_wide, cum_rows, state_act, affinity,
                    grad_affinity, row_sums, col_sums, wide_stats):
    tokens, inner, state2, heads, local_heads, taps = dims

    @pl.when(pl.program_id(0) == 0)
    def _():
        grad_cw_ref[...] = jnp.zeros_like(grad_cw_ref)
        grad_chan_ref[...] = jnp.zeros_like(grad_chan_ref)
        grad_head_ref[...] = jnp.zeros_like(grad_head_ref)

    raw, step, log_decay, rows, cols = prepare(
        dims, own_ref, proj_ref, seg_col_ref, seg_row_ref, mask_ref, head_ref, cw_ref,
        mask_wide, visible_bias, step_wide, cum_wide, cum_rows, state_act, affinity)
    grad_affinity[...] = jnp.zeros_like(grad_affinity)
    row_sums[...] = jnp.zeros_like(row_sums)
    col_sums[...] = jnp.zeros_like(col_sums)
    wide_stats[0] = jnp.broadcast_to(stats_ref[:, 0:1], (tokens, LANES))
    wide_stats[1] = jnp.broadcast_to(stats_ref[:, 1:2], (tokens, LANES))
    lane = lax.broadcasted_iota(jnp.int32, (tokens, LANES), 1)
    block_lane = lax.broadcasted_iota(jnp.int32, (LANES, LANES), 1)
    first = lane < LANES // 2
    blocks = tokens // LANES

    def conv_back(grad_conv, shifted, conv_input, here):
        grad_cw_ref[0:1, here] += jnp.sum(grad_conv * conv_input, 0, keepdims=True)
        grad_cw_ref[taps : taps + 1, here] += jnp.sum(grad_conv, 0, keepdims=True)
        back = cw_ref[0:1, here] * grad_conv
        for offset in range(1, taps):
            grad_cw_ref[offset : offset + 1, here] += jnp.sum(grad_conv * shifted[offset - 1], 0, keepdims=True)
            term = (cw_ref[offset : offset + 1, here] * grad_conv) * mask_wide[offset - 1]
            back = back + pltpu.roll(term, tokens - offset, 0)
        return back

    def pair_step(pair, carry):
        here = pl.ds(pl.multiple_of(pair * LANES, LANES), LANES)
        there = pl.ds(pl.multiple_of(inner + pair * LANES, LANES), LANES)
        conv_input = proj_ref[:, here]
        conv, shifted = convolve(
            conv_input, [cw_ref[j : j + 1, here] for j in range(taps)],
            cw_ref[taps : taps + 1, here], mask_wide,
        )
        conv_sig = sigmoid(conv)
        values = conv * conv_sig
        weighted = values * step_wide[pair]
        skip = chan_ref[0:1, here]
        halves = [jnp.where(first == (which == 0), weighted, 0.0).astype(BF16) for which in range(2)]
        out_parts = [(skip * values)[b * LANES : (b + 1) * LANES] for b in range(blocks)]
        for which in range(2):
            head = 2 * pair + which
            for tb in range(blocks):
                t_rows = slice(tb * LANES, (tb + 1) * LANES)
                pieces = []
                for sb in range(tb + 1):
                    s_cols = slice(sb * LANES, (sb + 1) * LANES)
                    distance = (cum_wide[head, t_rows, :] - cum_rows[head, :, s_cols]) + visible_bias[t_rows, s_cols]
                    pieces.append((affinity[t_rows, s_cols] * jnp.exp2(distance)).astype(BF16))
                weights = jnp.concatenate(pieces, 1) if tb > 0 else pieces[0]
                out_parts[tb] = out_parts[tb] + jnp.dot(
                    weights, halves[which][: (tb + 1) * LANES], preferred_element_type=F32
                )
        out = jnp.concatenate(out_parts, 0)
        gate = proj_ref[:, there]
        gate_sig = sigmoid(gate)
        gate_silu = gate * gate_sig
        gated = out * gate_silu
        gn = gn_ref[:, here]
        gain = chan_ref[1:2, here]
        root = wide_stats[0]
        grad_chan_ref[1:2, here] += jnp.sum(gn * gated * root, 0, keepdims=True)
        grad_gated = root * (gn * gain) - gated * wide_stats[1]
        grad_out = grad_gated * gate_silu
        gp_ref[:, there] = (grad_gated * out * (gate_sig * (1.0 + gate * (1.0 - gate_sig)))).astype(BF16)
        grad_chan_ref[0:1, here] += jnp.sum(grad_out * values, 0, keepdims=True)
        back_parts = [jnp.zeros((LANES, LANES), F32) for _ in range(blocks)]
        for which in range(2):
            head = 2 * pair + which
            mine = jnp.where(first == (which == 0), grad_out, 0.0).astype(BF16)
            for tb in range(blocks):
                t_rows = slice(tb * LANES, (tb + 1) * LANES)
                sums = None
                for sb in range(tb + 1):
                    s_cols = slice(sb * LANES, (sb + 1) * LANES)
                    distance = (cum_wide[head, t_rows, :] - cum_rows[head, :, s_cols]) + visible_bias[t_rows, s_cols]
                    decay = jnp.exp2(distance)
                    weights = affinity[t_rows, s_cols] * decay
                    cross = contract_cols(mine[t_rows], halves[which][s_cols])
                    grad_affinity[t_rows, s_cols] += cross * decay
                    energy = cross * weights
                    col_sums[head, :, s_cols] += jnp.sum(energy, 0, keepdims=True)
                    sums = energy if sums is None else sums + energy
                    back_parts[sb] = back_parts[sb] + contract_rows(weights.astype(BF16), mine[t_rows])
                row_sums[t_rows, :] += jnp.where(
                    block_lane == head, jnp.sum(sums, 1, keepdims=True), 0.0
                )
        grad_values = jnp.concatenate(back_parts, 0) * step_wide[pair] + skip * grad_out
        grad_conv = grad_values * (conv_sig * (1.0 + conv * (1.0 - conv_sig)))
        gp_ref[:, here] = conv_back(grad_conv, shifted, conv_input, here).astype(BF16)
        return carry

    lax.fori_loop(0, local_heads // 2, pair_step, 0)

    common = 2 * inner
    grad_states = [
        contract_rows(grad_affinity[...], state_act[1], HIGHEST),
        jnp.dot(grad_affinity[...], state_act[0], precision=HIGHEST, preferred_element_type=F32),
    ]
    for part in range(state2 // LANES):
        at = slice(inner + part * LANES, inner + (part + 1) * LANES)
        spot = slice(common + part * LANES, common + (part + 1) * LANES)
        conv_input = proj_ref[:, spot]
        conv, shifted = convolve(
            conv_input, [cw_ref[j : j + 1, at] for j in range(taps)], cw_ref[taps : taps + 1, at], mask_wide
        )
        conv_sig = sigmoid(conv)
        grad_conv = grad_states[part] * (conv_sig * (1.0 + conv * (1.0 - conv_sig)))
        gp_ref[:, spot] = conv_back(grad_conv, shifted, conv_input, at).astype(BF16)

    col_rows = [col_sums[head] for head in range(local_heads)]
    col_rows.append(jnp.zeros((LANES - local_heads, tokens), F32))
    col_energy = jnp.concatenate(col_rows, 0).T
    upper = jnp.where(cols >= rows, 1.0, 0.0).astype(F32)
    grad_decay = jnp.dot(upper, row_sums[...] - col_energy, precision=HIGHEST, preferred_element_type=F32)
    step_sig = sigmoid(raw)
    ratio = jnp.where(raw < -20.0, 1.0, step_sig / jnp.maximum(step, 1e-30))
    grad_raw = col_energy * ratio + (head_ref[1:2, :] * grad_decay) * step_sig
    grad_head_ref[0:1, :] += jnp.sum(grad_raw, 0, keepdims=True)
    grad_head_ref[1:2, :] += jnp.sum(grad_decay * log_decay, 0, keepdims=True)
    placed = pltpu.roll(grad_raw, own_ref[0] * local_heads, 1)
    gp_ref[:, common + state2 : common + state2 + heads] = placed[:, :heads].astype(BF16)


def mixer_specs(dims, width):
    tokens, inner, state2, heads, local_heads, taps = dims
    fixed = lambda shape: pl.BlockSpec(shape, lambda s: (0,) * len(shape))
    in_specs = [
        pl.BlockSpec(memory_space=pltpu.SMEM),
        pl.BlockSpec((tokens, width), lambda s: (s, 0)),
        pl.BlockSpec((None, tokens, 1), lambda s: (s, 0, 0)),
        pl.BlockSpec((None, 1, tokens), lambda s: (s, 0, 0)),
        pl.BlockSpec((None, tokens, 8), lambda s: (s, 0, 0)),
        fixed((8, LANES)),
        fixed((8, inner + state2)),
        fixed((8, inner)),
    ]
    scratch = [
        pltpu.VMEM((taps - 1, tokens, LANES), F32),
        pltpu.VMEM((tokens, tokens), F32),
        pltpu.VMEM((local_heads // 2, tokens, LANES), F32),
        pltpu.VMEM((local_heads, tokens, LANES), F32),
        pltpu.VMEM((local_heads, 1, tokens), F32),
        pltpu.VMEM((state2 // LANES, tokens, LANES), F32),
        pltpu.VMEM((tokens, tokens), F32),
    ]
    return in_specs, scratch


def mix_forward(dims, operands):
    tokens, inner, state2, heads, local_heads, taps = dims
    total, width = operands[1].shape
    in_specs, scratch = mixer_specs(dims, width)
    return pl.pallas_call(
        functools.partial(forward_kernel, dims),
        grid=(total // tokens,),
        in_specs=in_specs,
        out_specs=[
            pl.BlockSpec((tokens, inner), lambda s: (s, 0)),
            pl.BlockSpec((tokens, 1), lambda s: (s, 0)),
        ],
        out_shape=[
            jax.ShapeDtypeStruct((total, inner), BF16),
            jax.ShapeDtypeStruct((total, 1), F32),
        ],
        scratch_shapes=scratch,
        compiler_params=pltpu.CompilerParams(vmem_limit_bytes=48 << 20),
        cost_estimate=pl.CostEstimate(
            flops=total * local_heads * tokens * 4 * 64,
            bytes_accessed=total * width * 4,
            transcendentals=total * local_heads * tokens,
        ),
        name="mix_forward",
    )(*operands)


def mix_backward(dims, operands, stats, grad_normed):
    tokens, inner, state2, heads, local_heads, taps = dims
    total, width = operands[1].shape
    in_specs, scratch = mixer_specs(dims, width)
    fixed = lambda shape: pl.BlockSpec(shape, lambda s: (0,) * len(shape))
    return pl.pallas_call(
        functools.partial(backward_kernel, dims),
        grid=(total // tokens,),
        in_specs=in_specs + [
            pl.BlockSpec((tokens, 2), lambda s: (s, 0)),
            pl.BlockSpec((tokens, inner), lambda s: (s, 0)),
        ],
        out_specs=[
            pl.BlockSpec((tokens, width), lambda s: (s, 0)),
            fixed((8, inner + state2)),
            fixed((8, inner)),
            fixed((8, LANES)),
        ],
        out_shape=[
            jax.ShapeDtypeStruct((total, width), BF16),
            jax.ShapeDtypeStruct((8, inner + state2), F32),
            jax.ShapeDtypeStruct((8, inner), F32),
            jax.ShapeDtypeStruct((8, LANES), F32),
        ],
        scratch_shapes=scratch + [
            pltpu.VMEM((tokens, tokens), F32),
            pltpu.VMEM((tokens, LANES), F32),
            pltpu.VMEM((local_heads, 1, tokens), F32),
            pltpu.VMEM((2, tokens, LANES), F32),
        ],
        compiler_params=pltpu.CompilerParams(vmem_limit_bytes=48 << 20),
        cost_estimate=pl.CostEstimate(
            flops=total * local_heads * tokens * 12 * 64,
            bytes_accessed=total * width * 6,
            transcendentals=2 * total * local_heads * tokens,
        ),
        name="mix_backward",
    )(*operands, stats, grad_normed)


def swap(array, axis, size, bit):
    return lax.ppermute(array, axis, [(i, i ^ bit) for i in range(size)])


def axis_bits(size):
    bits = []
    bit = 1
    while bit < size:
        bits.append(bit)
        bit *= 2
    return bits


def gather_relative(array, axis, size):
    held = array[None]
    for bit in reversed(axis_bits(size)):
        held = jnp.concatenate([held, swap(held, axis, size, bit)], 0)
    return held


def scatter_relative(array, axis, size):
    total = array
    for bit in axis_bits(size):
        half = total.shape[0] // 2
        received = swap(total[half:].astype(BF16), axis, size, bit)
        total = total[:half].astype(F32) + received.astype(F32)
    return total[0]


def sum_tokens(array, axis, size):
    kinds, tokens = array.shape
    for bit in axis_bits(size):
        stride = tokens // (2 * bit)
        received = swap(array, axis, size, bit).reshape(kinds, bit, 2, stride)
        array = array + received[:, :, ::-1].reshape(kinds, tokens)
    return array


def halve_sum(array, order, replica, size):
    total = array
    for bit in order:
        blocks, rows, columns = total.shape
        mine = (replica // bit) % 2
        halves = total.reshape(blocks, 2, rows // 2, columns)
        kept = lax.dynamic_index_in_dim(halves, mine, 1, keepdims=False)
        sent = lax.dynamic_index_in_dim(halves, 1 - mine, 1, keepdims=False)
        received = swap(sent.astype(BF16), "replica", size, bit)
        total = kept + received.astype(F32)
    return total


def double_gather(array, order, replica, size):
    held = array
    for bit in reversed(order):
        received = swap(held, "replica", size, bit)
        upper = (replica // bit) % 2 == 1
        held = jnp.where(
            upper,
            jnp.concatenate([received, held], 1),
            jnp.concatenate([held, received], 1),
        )
    return held


def flip(index, bit):
    return index + bit * (1 - 2 * ((index // bit) % 2))


MESH = pl.DeviceIdType.MESH


def greet(peers):
    barrier = pltpu.get_barrier_semaphore()
    for peer in peers:
        pl.semaphore_signal(barrier, inc=1, device_id=peer, device_id_type=MESH)
    pl.semaphore_wait(barrier, len(peers))


def copy_peers(me):
    return [flip(me, 1), flip(me, 2), flip(flip(me, 1), 2)]


def gather_kernel(full_inner, inner, x_ref, seg_ref, small_ref, w_ref,
                  x_all_ref, seg_all_ref, small_all_ref, cols_ref,
                  x_held, cols_held, send_sems, recv_sems, local_sems, store_sems):
    me = lax.axis_index("fsdp")
    replica = lax.axis_index("replica")
    depth, common = w_ref.shape[1], w_ref.shape[0] - 2 * full_inner
    peers = [(replica, peer) for peer in copy_peers(me)]
    beside, above = (flip(replica, 1), me), (flip(replica, 2), me)
    greet(peers + [beside, above])
    number = [0]
    started = []

    def send(from_ref, to_ref, device):
        slot = number[0]
        number[0] += 1
        copy = pltpu.make_async_remote_copy(
            src_ref=from_ref, dst_ref=to_ref, send_sem=send_sems.at[slot], recv_sem=recv_sems.at[slot],
            device_id=device, device_id_type=MESH,
        )
        copy.start()
        started.append(copy)
        return copy

    parts = [(0, inner), (inner, inner), (2 * inner, common)]

    def targets(owner, first, count):
        lanes = pl.ds(pl.multiple_of(owner * depth, depth), depth)
        return [
            cols_ref.at[pl.ds(pl.multiple_of(base + first * (length // 4), 16), count * (length // 4)), lanes]
            for base, length in parts
        ]

    def sources(device, first, count):
        bases = [full_inner + device * inner, device * inner, 2 * full_inner]
        return [
            w_ref.at[pl.ds(pl.multiple_of(base + first * (length // 4), 16), count * (length // 4))]
            for base, (_, length) in zip(bases, parts)
        ]

    def send_parts(from_refs, to_refs, device):
        return [send(source, target, device) for source, target in zip(from_refs, to_refs)]

    spot = replica % 4
    across = [send_parts(sources(peers[which][1], spot, 1), targets(me, spot, 1), peers[which]) for which in (1, 2)]
    x_y = send(x_ref, x_all_ref.at[1], peers[1])
    smalls = [send(small_ref, small_all_ref.at[me], peer) for peer in peers]
    smalls += [send(seg_ref, seg_all_ref.at[slot], peer) for peer, slot in zip(peers, (2, 1, 3))]
    near = send_parts(sources(peers[0][1], 0, 4), targets(me, 0, 4), peers[0])
    x_near = send(x_ref, x_all_ref.at[2], peers[0])
    held = [cols_held.at[pl.ds(base, length)] for base, length in parts] + [x_held]
    own = list(zip(sources(me, 0, 4) + [x_ref], held, targets(me, 0, 4) + [x_all_ref.at[0]]))
    loads = [pltpu.make_async_copy(source, held, local_sems.at[i]) for i, (source, held, _) in enumerate(own)]
    stores = [pltpu.make_async_copy(held, target, store_sems.at[i]) for i, (_, held, target) in enumerate(own)]
    stores += [
        pltpu.make_async_copy(small_ref, small_all_ref.at[me], local_sems.at[4]),
        pltpu.make_async_copy(seg_ref, seg_all_ref.at[0], local_sems.at[5]),
    ]
    for copy in loads + stores[4:]:
        copy.start()
    for load, store in zip(loads, stores):
        load.wait()
        store.start()

    def relay(which, first, count, device):
        refs = targets(peers[which][1], first, count)
        return send_parts(refs, refs, device)

    for copy in across[0]:
        copy.wait_recv()
    first_beside = relay(1, spot, 1, beside)
    for copy in across[1]:
        copy.wait_recv()
    first_above = relay(2, spot, 1, above)
    for copy in first_beside:
        copy.wait_recv()
    last = relay(1, (spot // 2) * 2, 2, above)
    for copy in first_above:
        copy.wait_recv()
    last += relay(2, spot, 1, beside)
    last += relay(2, flip(spot, 2), 1, beside)
    x_y.wait_recv()
    last.append(send(x_all_ref.at[1], x_all_ref.at[3], peers[0]))
    for copy in last + smalls + near + [x_near]:
        copy.wait_recv()
    for copy in stores:
        copy.wait()
    for copy in started:
        copy.wait_send()


GATHER_COPIES = 34


def gather_inputs(size, inner, x, segments, small, w_flipped):
    full, depth = w_flipped.shape
    full_inner = inner * size
    columns = 2 * inner + full - 2 * full_inner
    anywhere = pl.BlockSpec(memory_space=pl.ANY)
    return pl.pallas_call(
        functools.partial(gather_kernel, full_inner, inner),
        in_specs=[anywhere] * 4,
        out_specs=[anywhere] * 4,
        out_shape=[
            jax.ShapeDtypeStruct((size,) + x.shape, BF16),
            jax.ShapeDtypeStruct((size,) + segments.shape, jnp.int32),
            jax.ShapeDtypeStruct((size,) + small.shape, F32),
            jax.ShapeDtypeStruct((columns, size * depth), BF16),
        ],
        scratch_shapes=[
            pltpu.VMEM(x.shape, BF16),
            pltpu.VMEM((columns, depth), BF16),
            pltpu.SemaphoreType.DMA((GATHER_COPIES,)),
            pltpu.SemaphoreType.DMA((GATHER_COPIES,)),
            pltpu.SemaphoreType.DMA((6,)),
            pltpu.SemaphoreType.DMA((4,)),
        ],
        compiler_params=pltpu.CompilerParams(
            collective_id=1, has_side_effects=True, vmem_limit_bytes=16 << 20
        ),
        cost_estimate=pl.CostEstimate(flops=0, bytes_accessed=200 << 20, transcendentals=0),
        name="gather_inputs",
    )(x, segments, small, w_flipped)


PARTS = {
    "side": {"keep": 2, "got": 2, "lift": 2, "sent": 4, "swapped": 4, "final": 4},
    "lift": {"keep": 1, "got": 1, "sent": 2, "swapped": 2, "sent_side": 4, "got_side": 4, "final": 4},
}
SLOTS = 9
OUT_ROWS = (64,) * 16
IN_ROWS = (64,) * 32
PER_TICK = 3
TOKEN_PIECES = 16


def reduce_chunks(inner, common):
    pieces = []
    start = 0
    for rows in OUT_ROWS:
        pieces.append(("out", start, rows))
        start += rows
    start = 0
    for rows in IN_ROWS:
        pieces.append(("in", start, rows))
        start += rows
    pieces.insert(len(OUT_ROWS), ("shared", 0, common))
    counts = {}
    placed = []
    for number, (kind, start, rows) in enumerate(pieces):
        order = "lift" if number % 3 == 2 else "side"
        key = (kind == "shared", rows, order)
        where = counts.get(key, 0)
        counts[key] = where + 1
        placed.append((kind, start, rows, order, where))
    return placed, counts


def reduce_kernel(plan, in_ref, out_ref, tok_out_ref, tok_grad_ref, small_ref,
                  sum_in_ref, sum_shared_ref, sum_out_ref, got_out_ref, got_grad_ref, small_sum_ref, *scratch):
    chunks, counts, inner, depth = plan
    groups = {}
    position = 0
    for key in counts:
        names = list(PARTS[key[2]])
        groups[key] = dict(zip(names, scratch[position : position + len(names)]))
        position += len(names)
    (shared_in, shared_sum, small_got, send_sems, recv_sems, local_sems, tok_send, tok_recv,
     small_send, small_recv, shared_send, shared_recv) = scratch[position:]
    me = lax.axis_index("fsdp")
    replica = lax.axis_index("replica")
    up = replica // 2
    inside = (up == 1) | (up == 2)
    outside = (up == 0) | (up == 3)
    half = up // 2
    aside = replica % 2
    beside = (flip(replica, 1), me)
    partner = (flip(replica, 2), me)
    middle = (flip(flip(replica, 2), 4), me)
    peers = [(replica, peer) for peer in copy_peers(me)]
    greet(peers + [beside, partner, middle])

    def remote(from_ref, to_ref, device, sends, recvs):
        return pltpu.make_async_remote_copy(
            src_ref=from_ref, dst_ref=to_ref, send_sem=sends, recv_sem=recvs, device_id=device, device_id_type=MESH
        )

    def lanes_of(device):
        return pl.ds(pl.multiple_of(device * depth, depth), depth)

    def activations():
        rows = got_out_ref.shape[0] // TOKEN_PIECES
        copies = []
        for piece in range(TOKEN_PIECES):
            at = pl.ds(piece * rows, rows)
            for which, (source, target) in enumerate([(tok_out_ref, got_out_ref), (tok_grad_ref, got_grad_ref)]):
                copy = remote(
                    source.at[1, at], target.at[at], peers[1], tok_send.at[which, piece], tok_recv.at[which, piece]
                )
                copy.start()
                copies.append(copy)
            yield
        for copy in copies:
            copy.wait()

    def smalls():
        small_sum_ref[...] = small_ref[...]
        for level, peer in enumerate([peers[0], peers[1], beside, partner, middle]):
            copy = remote(small_sum_ref, small_got.at[level], peer, small_send.at[level], small_recv.at[level])
            copy.start()
            yield
            copy.wait()
            small_sum_ref[...] += small_got[level]

    def run(number, kind, start, rows, order, where):
        held = {name: ref.at[where] for name, ref in groups[kind == "shared", rows, order].items()}
        if kind == "in":
            group = 0 if start >= inner else 4
            local_start = start % inner
            source = lambda at, count: in_ref.at[pl.ds(pl.multiple_of(start + at, 16), count)]
            place = lambda at, count: sum_in_ref.at[pl.ds(group, 4), pl.ds(pl.multiple_of(local_start + at, 16), count)]
        elif kind == "out":
            source = lambda at, count: out_ref.at[pl.ds(pl.multiple_of(start + at, 16), count)]
            place = lambda at, count: sum_out_ref.at[pl.ds(pl.multiple_of(start + at, 16), count)]
        else:
            source = lambda at, count: shared_sum.at[pl.ds(at, count)]
            place = lambda at, count: sum_shared_ref.at[pl.ds(at, count)]
            copies = []
            for offset in range(3):
                copy = remote(
                    in_ref.at[pl.ds(2 * inner, rows), lanes_of(peers[offset][1])],
                    shared_in.at[offset], peers[offset], shared_send.at[offset], shared_recv.at[offset],
                )
                copy.start()
                copies.append(copy)
            own = pltpu.make_async_copy(
                in_ref.at[pl.ds(2 * inner, rows), lanes_of(me)], shared_in.at[3], local_sems.at[number, 1]
            )
            own.start()
            yield
            own.wait()
            total = shared_in[3].astype(F32)
            for offset in range(3):
                copies[offset].wait_recv()
                total = total + shared_in[offset].astype(F32)
            shared_sum[...] = total.astype(BF16)

        def link(from_ref, to_ref, device, slot):
            return remote(from_ref, to_ref, device, send_sems.at[number, slot], recv_sems.at[number, slot])

        def added(names_at, at, count):
            total = None
            for name, base in names_at:
                local = pl.multiple_of(at - base, count)
                part = held[name][pl.ds(local, count), :].astype(F32)
                total = part if total is None else total + part
            return total

        two, four = rows // 2, rows // 4
        if order == "side":
            mine, other = pl.multiple_of(aside * two, two), pl.multiple_of((1 - aside) * two, two)
            low, high = pl.multiple_of(mine + half * four, four), pl.multiple_of(mine + (1 - half) * four, four)
            keep = pltpu.make_async_copy(source(mine, two), held["keep"], local_sems.at[number, 0])
            keep.start()
            side = link(source(other, two), held["got"], beside, 0)
            side.start()
            yield
            keep.wait()
            side.wait_recv()
            lift = link(held["lift"], held["lift"], partner, 1)

            @pl.when(outside)
            def _():
                held["lift"][...] = added([("keep", mine), ("got", mine)], mine, two).astype(BF16)
                lift.start()

            yield
            bases = [("keep", mine), ("got", mine), ("lift", mine)]
            across = link(held["sent"], held["swapped"], middle, 2)

            @pl.when(inside)
            def _():
                lift.wait_recv()
                held["sent"][...] = added(bases, high, four).astype(BF16)
                across.start()

            yield
            bases = bases + [("swapped", low)]
        else:
            mine, other = pl.multiple_of(half * two, two), pl.multiple_of((1 - half) * two, two)
            low, high = pl.multiple_of(mine + aside * four, four), pl.multiple_of(mine + (1 - aside) * four, four)
            keep = pltpu.make_async_copy(source(0, rows), held["keep"], local_sems.at[number, 0])
            lift = link(source(0, rows), held["got"], partner, 1)

            @pl.when(outside)
            def _():
                lift.start()

            @pl.when(inside)
            def _():
                keep.start()

            yield
            bases = [("keep", 0), ("got", 0)]
            across = link(held["sent"], held["swapped"], middle, 2)

            @pl.when(inside)
            def _():
                keep.wait()
                lift.wait_recv()
                held["sent"][...] = added(bases, other, two).astype(BF16)
                across.start()

            yield
            bases = bases + [("swapped", mine)]
            side = link(held["sent_side"], held["got_side"], beside, 0)

            @pl.when(inside)
            def _():
                across.wait_recv()
                held["sent_side"][...] = added(bases, high, four).astype(BF16)
                side.start()

            yield
            bases = bases + [("got_side", low)]

        final = held["final"]
        trade = []
        if kind == "in":
            target = sum_in_ref.at[group + me, pl.ds(pl.multiple_of(local_start + low, 16), four)]
            trade = [
                link(final.at[:, lanes_of(peers[offset][1])], target, peers[offset], 3 + offset) for offset in range(3)
            ]
            own = pltpu.make_async_copy(final.at[:, lanes_of(me)], target, local_sems.at[number, 1])
        else:
            own = pltpu.make_async_copy(final, place(low, four), local_sems.at[number, 1])

        if order == "side":
            back = [
                link(place(low, four), place(low, four), middle, 6),
                link(place(mine, two), place(mine, two), partner, 7),
                link(place(mine, two), place(mine, two), beside, 8),
            ]
        else:
            back = [
                link(place(low, four), place(low, four), beside, 6),
                link(place(mine, two), place(mine, two), middle, 7),
                link(place(0, rows), place(0, rows), partner, 8),
            ]

        @pl.when(inside)
        def _():
            (across if order == "side" else side).wait_recv()
            final[...] = added(bases, low, four).astype(BF16)
            for copy in trade:
                copy.start()
            own.start()
            own.wait()
            for copy in trade:
                copy.wait_recv()
            back[0].start()

        yield

        @pl.when(inside)
        def _():
            back[0].wait_recv()
            back[1].start()
            if order == "side":
                back[2].start()

        yield
        if order == "side":

            @pl.when(outside)
            def _():
                back[1].wait_recv()
                back[2].start()

            yield
            back[2].wait_recv()
            side.wait_send()
            back[2].wait_send()

            @pl.when(outside)
            def _():
                lift.wait_send()

            @pl.when(inside)
            def _():
                across.wait_send()
                for copy in trade + back[:2]:
                    copy.wait_send()

        else:

            @pl.when(inside)
            def _():
                back[1].wait_recv()
                back[2].start()

            yield

            @pl.when(outside)
            def _():
                back[2].wait_recv()
                lift.wait_send()

            @pl.when(inside)
            def _():
                across.wait_send()
                side.wait_send()
                for copy in trade + back:
                    copy.wait_send()

        if kind == "shared":
            for copy in copies:
                copy.wait_send()

    waiting = [run(number, *chunk) for number, chunk in enumerate(chunks)]
    active, extra = [], [activations(), smalls()]

    def advance(running):
        still = []
        for steps in running:
            try:
                next(steps)
                still.append(steps)
            except StopIteration:
                pass
        return still

    while waiting or active:
        active = advance(active + waiting[:PER_TICK])
        waiting = waiting[PER_TICK:]
        extra = advance(extra)
    while extra:
        extra = advance(extra)


def reduce_gradients(size, depth, inner, common, grad_in, grad_out, tok_out, tok_grad, small):
    width = grad_out.shape[1]
    chunks, counts = reduce_chunks(inner, common)
    scratch = []
    for (shared, rows, order), count in counts.items():
        for fraction in PARTS[order].values():
            scratch.append(pltpu.VMEM((count, rows // fraction, depth if shared else width), BF16))
    sems = pltpu.SemaphoreType.DMA
    scratch += [
        pltpu.VMEM((4, common, depth), BF16),
        pltpu.VMEM((common, depth), BF16),
        pltpu.VMEM((5,) + small.shape, F32),
        sems((len(chunks), SLOTS)), sems((len(chunks), SLOTS)), sems((len(chunks), 2)),
        sems((2, TOKEN_PIECES)), sems((2, TOKEN_PIECES)), sems((5,)), sems((5,)), sems((3,)), sems((3,)),
    ]
    anywhere = pl.BlockSpec(memory_space=pl.ANY)
    local = pl.BlockSpec(memory_space=pltpu.VMEM)
    return pl.pallas_call(
        functools.partial(reduce_kernel, (chunks, counts, inner, depth)),
        in_specs=[anywhere] * 4 + [local],
        out_specs=[anywhere] * 5 + [local],
        out_shape=[
            jax.ShapeDtypeStruct((2 * size, inner, depth), BF16),
            jax.ShapeDtypeStruct((common, depth), BF16),
            jax.ShapeDtypeStruct(grad_out.shape, BF16),
            jax.ShapeDtypeStruct(tok_out.shape[1:], BF16),
            jax.ShapeDtypeStruct(tok_grad.shape[1:], BF16),
            jax.ShapeDtypeStruct(small.shape, F32),
        ],
        scratch_shapes=scratch,
        compiler_params=pltpu.CompilerParams(
            collective_id=0, has_side_effects=True, vmem_limit_bytes=58 << 20
        ),
        cost_estimate=pl.CostEstimate(flops=0, bytes_accessed=700 << 20, transcendentals=0),
        name="reduce_gradients",
    )(grad_in, grad_out, tok_out, tok_grad, small)


def small_pieces(size, copies, depth, inner, columns, me, replica, scaled_low, gp, normed_low, cot_all):
    replica_bits = axis_bits(copies)
    orders = [replica_bits, replica_bits[1:] + replica_bits[:1]]
    pieces = []
    part_rows = inner // 2
    for part in range(2):
        grad = contract_rows(normed_low[:, part * part_rows : (part + 1) * part_rows], cot_all)
        order = orders[part % 2]
        mine = halve_sum(grad[None], order, replica, copies)
        pieces.append(double_gather(mine.astype(BF16), order, replica, copies)[0])
    grad_w_out = jnp.concatenate(pieces, 0).astype(F32)


    def columns_sum(start, stop, order, shared):
        grad = contract_rows(scaled_low, gp[:, start:stop])
        mine = halve_sum(grad.reshape(size, depth, stop - start), order, replica, copies)
        own = lax.dynamic_index_in_dim(mine, me, 0, keepdims=False)
        got = [own]
        for offset in range(1, size):
            there = lax.dynamic_index_in_dim(mine, me ^ offset, 0, keepdims=False)
            got.append(swap(there.astype(BF16), "fsdp", size, offset))
        if shared:
            held = sum(block.astype(F32) for block in got)[None].astype(BF16)
        else:
            held = jnp.stack([block.astype(BF16) for block in got])
        return double_gather(held, order, replica, copies)

    halves = inner // 2
    value_parts = [columns_sum(c * halves, (c + 1) * halves, orders[c % 2], False) for c in range(2)]
    gate_parts = [
        columns_sum(inner + c * halves, inner + (c + 1) * halves, orders[c % 2], False) for c in range(2)
    ]
    shared_part = columns_sum(2 * inner, columns, orders[0], True)[0]

    def in_place(parts):
        placed = []
        for device in range(size):
            for part in parts:
                placed.append(lax.dynamic_index_in_dim(part, me ^ device, 0, keepdims=False))
        return placed

    grad_w_in = jnp.concatenate(in_place(gate_parts) + in_place(value_parts) + [shared_part], 1).astype(F32)
    return grad_w_in, grad_w_out


def recut(size, full_inner, inner, me, w_in):
    depth, full = w_in.shape

    def columns_of(device):
        return jnp.concatenate(
            [
                lax.dynamic_slice(w_in, (0, full_inner + device * inner), (depth, inner)),
                lax.dynamic_slice(w_in, (0, device * inner), (depth, inner)),
                w_in[:, 2 * full_inner :],
            ],
            1,
        )

    w_cols = jnp.zeros((size * depth, 2 * inner + full - 2 * full_inner), BF16)
    w_cols = lax.dynamic_update_slice(w_cols, columns_of(me), (me * depth, 0))
    for offset in range(1, size):
        received = swap(columns_of(me ^ offset), "fsdp", size, offset)
        w_cols = lax.dynamic_update_slice(w_cols, received, ((me ^ offset) * depth, 0))
    return w_cols


def on_device(copies, size, hidden_in, segment_ids, cotangent, norm_gain, w_in, conv_weight, conv_bias,
              dt_bias, a_log, skip_gain, gate_gain, w_out):
    micro_count, seq_count, tokens, width = hidden_in.shape
    own_rows = micro_count * seq_count * tokens
    total = size * own_rows
    inner = gate_gain.shape[0]
    local_heads = dt_bias.shape[0]
    heads = local_heads * size
    channel = inner // local_heads
    full_inner = inner * size
    taps, own_conv = conv_weight.shape
    conv_width = own_conv * size
    state2 = conv_width - full_inner
    depth = w_in.shape[0]
    common = state2 + heads
    columns = 2 * inner + common
    dims = (tokens, inner, state2, heads, local_heads, taps)
    me = lax.axis_index("fsdp")
    replica = lax.axis_index("replica")

    own_x = hidden_in.reshape(own_rows, width)
    own_cot = cotangent.reshape(own_rows, width)
    small = jnp.concatenate([norm_gain, conv_weight.reshape(-1), conv_bias])
    segments = segment_ids.reshape(micro_count * seq_count, tokens)
    fused = copies == 8 and size == 4 and sum(OUT_ROWS) == inner and sum(IN_ROWS) == 2 * inner
    if fused:
        padded = jnp.pad(small.astype(F32), (0, -small.shape[0] % (8 * LANES))).reshape(-1, LANES)
        x_all, seg_all, small, w_cols = gather_inputs(
            size, inner, own_x, segments.reshape(-1, LANES), padded, w_in.T
        )
        x_all = x_all.reshape(total, width)
        small = small.reshape(size, -1)
        own_cot_later, _ = lax.optimization_barrier((own_cot, seg_all))
        cot_across = swap(own_cot_later, "fsdp", size, 2)
    else:
        small = lax.all_gather(small, "fsdp", axis=0, tiled=False).astype(F32)
        x_all = gather_relative(own_x, "fsdp", size).reshape(total, width)
        seg_all = gather_relative(segments, "fsdp", size)
        w_cols = recut(size, full_inner, inner, me, w_in).T
        cot_all = gather_relative(own_cot, "fsdp", size).reshape(total, width)
    seg_all = seg_all.reshape(total // tokens, tokens)
    full_norm = small[:, :depth].reshape(1, width)
    full_cw = small[:, depth : depth + taps * own_conv].reshape(size, taps, own_conv)
    full_cw = full_cw.transpose(1, 0, 2).reshape(taps, conv_width)
    full_cb = small[:, depth + taps * own_conv : depth + (taps + 1) * own_conv].reshape(1, conv_width)

    def normalise(inputs):
        wide = inputs.astype(F32)
        return lax.rsqrt(jnp.mean(wide * wide, -1, keepdims=True) + EPS)

    scaled_low = (x_all.astype(F32) * normalise(x_all) * full_norm).astype(BF16)
    projected = contract_cols(scaled_low, w_cols)

    conv_all = jnp.concatenate([full_cw, full_cb, jnp.zeros((7 - taps, conv_width), F32)], 0)
    conv_own = jnp.concatenate(
        [lax.dynamic_slice(conv_all, (0, me * inner), (8, inner)), conv_all[:, full_inner:]], 1
    )
    pad_heads = lambda row: jnp.pad(row.astype(F32), (0, LANES - local_heads))
    head_rows = jnp.stack([pad_heads(dt_bias), pad_heads(-jnp.exp(a_log.astype(F32)))])
    head_rows = jnp.pad(head_rows, ((0, 6), (0, 0)))
    chan_rows = jnp.stack([jnp.repeat(skip_gain.astype(F32), channel), gate_gain.astype(F32)])
    chan_rows = jnp.pad(chan_rows, ((0, 6), (0, 0)))
    same = []
    for offset in range(1, taps):
        equal = (seg_all[:, offset:] == seg_all[:, :-offset]).astype(F32)
        same.append(jnp.pad(equal, ((0, 0), (offset, 0))))
    same = jnp.pad(jnp.stack(same, 2), ((0, 0), (0, 0), (0, 9 - taps)))
    operands = (
        me.astype(jnp.int32).reshape(1), projected, seg_all[:, :, None], seg_all[:, None, :], same,
        head_rows, conv_own, chan_rows,
    )
    gated, squares = mix_forward(dims, operands)
    if fused:
        cot_across, squares = lax.optimization_barrier((cot_across, squares))
        pair = jnp.stack([own_cot, cot_across])
        cot_all = jnp.concatenate([pair, swap(pair, "fsdp", size, 1)], 0).reshape(total, width)
    grad_normed = contract_cols(cot_all, w_out)
    cross = jnp.sum(gated.astype(F32) * grad_normed, 1)
    stats = sum_tokens(jnp.stack([squares[:, 0], cross]), "fsdp", size)
    root = lax.rsqrt(stats[0] / full_inner + EPS)
    pull = root * root * root * stats[1] / full_inner

    normed_low = (gated.astype(F32) * root[:, None]).astype(BF16)
    gp, grad_conv, grad_chan, grad_head = mix_backward(
        dims, operands, jnp.stack([root, pull], 1), grad_normed
    )
    own_wide = own_x.astype(F32)
    own_root = normalise(own_x)

    conv_full = jnp.zeros((8, conv_width), F32)
    conv_full = lax.dynamic_update_slice(conv_full, grad_conv[:, inner:], (0, full_inner))
    conv_full = lax.dynamic_update_slice(conv_full, grad_conv[:, :inner], (0, me * inner))
    conv_full = conv_full[: taps + 1].reshape(-1)
    skip_grad = grad_chan[0].reshape(local_heads, channel).sum(1)
    own_small = jnp.concatenate(
        [grad_head[0, :local_heads], grad_head[1, :local_heads], skip_grad, grad_chan[1]]
    )

    if fused:
        near = total // 2

        def halves(product):
            sent = swap(product(near, total).astype(BF16), "fsdp", size, 1)
            kept = product(0, near) + sent.astype(F32)
            return kept.astype(BF16).reshape(2, own_rows, width)

        tok_out = halves(lambda start, stop: jnp.dot(gated[start:stop], w_out, preferred_element_type=F32))
        far_grad = jnp.dot(gp[near:], w_cols, preferred_element_type=F32).astype(BF16)
        near_grad = jnp.dot(gp[:near], w_cols, preferred_element_type=F32).astype(BF16)
        tok_grad = (near_grad.astype(F32) + swap(far_grad, "fsdp", size, 1).astype(F32)).astype(BF16)
        tok_grad = tok_grad.reshape(2, own_rows, width)
        scaled_part = jnp.concatenate([near_grad, far_grad], 0)
        grad_norm = jnp.sum(scaled_part.astype(F32) * x_all.astype(F32) * normalise(x_all), 0)
        grad_out = contract_rows(normed_low, cot_all).astype(BF16)
        grad_cols = contract_rows(gp, scaled_low).astype(BF16)
        spread = lax.dynamic_update_slice(jnp.zeros((size, own_small.shape[0]), F32), own_small[None], (me, 0))
        vector = jnp.concatenate([conv_full, grad_norm, spread.reshape(-1)])
        vector = jnp.pad(vector, (0, -vector.shape[0] % (8 * LANES))).reshape(-1, LANES)
        sum_in, sum_shared, sum_out, got_out, got_grad, vector = reduce_gradients(
            size, depth, inner, common, grad_cols, grad_out, tok_out, tok_grad, vector
        )
        grad_w_out = sum_out.astype(F32)
        grad_w_in = jnp.concatenate([sum_in.reshape(2 * full_inner, depth), sum_shared], 0).astype(F32).T
        out_sum = tok_out[0].astype(F32) + got_out.astype(F32)
        grad_scaled = tok_grad[0].astype(F32) + got_grad.astype(F32)
        vector = vector.reshape(-1)
        conv_full = vector[: conv_full.shape[0]]
        grad_norm = vector[conv_full.shape[0] : conv_full.shape[0] + width]
        start = conv_full.shape[0] + width
        own_small = lax.dynamic_slice(vector, (start + me * own_small.shape[0],), own_small.shape)
    else:
        out_part = jnp.dot(gated, w_out, preferred_element_type=F32).astype(BF16)
        out_sum = scatter_relative(out_part.reshape(size, own_rows, width), "fsdp", size)
        grad_w_in, grad_w_out = small_pieces(
            size, copies, depth, inner, columns, me, replica, scaled_low, gp, normed_low, cot_all
        )
        scaled_part = jnp.dot(gp, w_cols, preferred_element_type=F32).astype(BF16)
        grad_scaled = scatter_relative(scaled_part.reshape(size, own_rows, width), "fsdp", size)
        grad_norm = jnp.sum(grad_scaled * own_wide * own_root, 0)
        conv_full, grad_norm = lax.psum((conv_full, grad_norm), ("replica", "fsdp"))
        own_small = lax.psum(own_small, "replica")

    block_out = (own_wide + root[:own_rows, None] * out_sum).astype(BF16).reshape(hidden_in.shape)
    gained = grad_scaled * full_norm
    inner_mean = jnp.mean(gained * own_wide, -1, keepdims=True)
    grad_in = own_cot.astype(F32) + own_root * gained - own_wide * (own_root * own_root * own_root * inner_mean)
    grad_in = grad_in.reshape(hidden_in.shape)
    conv_full = lax.dynamic_slice(conv_full.reshape(taps + 1, conv_width), (0, me * own_conv), (taps + 1, own_conv))
    grad_norm = lax.dynamic_slice(grad_norm, (me * depth,), (depth,))
    return (
        block_out,
        grad_in,
        grad_norm,
        grad_w_in,
        conv_full[:taps],
        conv_full[taps],
        own_small[:local_heads],
        own_small[local_heads : 2 * local_heads],
        own_small[2 * local_heads : 3 * local_heads],
        own_small[3 * local_heads :],
        grad_w_out,
    )


def solution(mesh):
    rows = ("replica", "fsdp")
    placed = (
        P(None, rows, None, None),
        P(None, rows, None),
        P(None, rows, None, None),
        P("fsdp"),
        P("fsdp", None),
        P(None, "fsdp"),
        P("fsdp"),
        P("fsdp"),
        P("fsdp"),
        P("fsdp"),
        P("fsdp"),
        P("fsdp", None),
    )
    return jax.shard_map(
        functools.partial(on_device, mesh.shape["replica"], mesh.shape["fsdp"]),
        mesh=mesh,
        in_specs=placed,
        out_specs=(
            P(None, rows, None, None),
            P(None, rows, None, None),
            P("fsdp"),
            P("fsdp", None),
            P(None, "fsdp"),
            P("fsdp"),
            P("fsdp"),
            P("fsdp"),
            P("fsdp"),
            P("fsdp"),
            P("fsdp", None),
        ),
        check_vma=False,
    )
```

```python
import functools

import jax
import jax.numpy as jnp
from jax import lax
from jax.experimental import pallas as pl
from jax.experimental.pallas import tpu as pltpu
from jax.sharding import PartitionSpec as P

EPS = 1e-05
HIGHEST = lax.Precision.HIGHEST
LANES = 128
F32 = jnp.float32
BF16 = jnp.bfloat16
LOG2E = 1.4426950408889634


def contract_rows(left, right, precision=None):
    return lax.dot_general(
        left, right, (((0,), (0,)), ((), ())), precision=precision, preferred_element_type=F32
    )


def contract_cols(left, right, precision=None):
    return lax.dot_general(
        left, right, (((1,), (1,)), ((), ())), precision=precision, preferred_element_type=F32
    )


def sigmoid(v):
    return 0.5 * jnp.tanh(0.5 * v) + 0.5


def convolve(conv_input, taps, bias, mask_refs):
    total = bias + taps[0] * conv_input
    shifted = []
    for offset in range(1, len(taps)):
        prior = pltpu.roll(conv_input, offset, 0) * mask_refs[offset - 1]
        shifted.append(prior)
        total = total + taps[offset] * prior
    return total, shifted


def prepare(dims, own_ref, proj_ref, seg_col_ref, seg_row_ref, mask_ref, head_ref, cw_ref,
            mask_wide, visible_bias, step_wide, cum_wide, cum_rows, state_act, affinity):
    tokens, inner, state2, heads, local_heads, taps = dims
    for offset in range(taps - 1):
        mask_wide[offset] = jnp.broadcast_to(mask_ref[:, offset : offset + 1], (tokens, LANES))
    rows = lax.broadcasted_iota(jnp.int32, (tokens, tokens), 0)
    cols = lax.broadcasted_iota(jnp.int32, (tokens, tokens), 1)
    visible = (rows >= cols) & (seg_col_ref[...] == seg_row_ref[...])
    visible_bias[...] = jnp.where(visible, 0.0, -1e30)
    common = 2 * inner
    raw = proj_ref[:, common + state2 : common + state2 + heads]
    raw = jnp.concatenate([raw, jnp.zeros((tokens, LANES - heads), F32)], 1)
    raw = pltpu.roll(raw, LANES - own_ref[0] * local_heads, 1)
    raw = raw + head_ref[0:1, :]
    step = jnp.maximum(raw, 0.0) + jnp.log1p(jnp.exp(-jnp.abs(raw)))
    log_decay = head_ref[1:2, :] * step
    lower = jnp.where(rows >= cols, 1.0, 0.0).astype(F32)
    cumulative = jnp.dot(lower, log_decay, precision=HIGHEST, preferred_element_type=F32)
    scaled_cum = cumulative * LOG2E
    flipped = scaled_cum.T
    lane = lax.broadcasted_iota(jnp.int32, (tokens, LANES), 1)
    for head in range(local_heads):
        cum_wide[head] = jnp.broadcast_to(scaled_cum[:, head : head + 1], (tokens, LANES))
        cum_rows[head] = flipped[head : head + 1, :]
    for pair in range(local_heads // 2):
        step_wide[pair] = jnp.where(
            lane < LANES // 2, step[:, 2 * pair : 2 * pair + 1], step[:, 2 * pair + 1 : 2 * pair + 2]
        )
    for part in range(state2 // LANES):
        at = inner + part * LANES
        conv, _ = convolve(
            proj_ref[:, common + part * LANES : common + (part + 1) * LANES],
            [cw_ref[j : j + 1, at : at + LANES] for j in range(taps)],
            cw_ref[taps : taps + 1, at : at + LANES],
            mask_wide,
        )
        state_act[part] = conv * sigmoid(conv)
    affinity[...] = contract_cols(state_act[1], state_act[0], HIGHEST)
    return raw, step, log_decay, rows, cols


def over_pairs(count, step, carry):
    group = 4 if count % 4 == 0 else 2

    def turn(index, carried):
        for inner in range(group):
            carried = step(index * group + inner, carried)
        return carried

    return lax.fori_loop(0, count // group, turn, carry)


def forward_kernel(dims, own_ref, proj_ref, seg_col_ref, seg_row_ref, mask_ref, head_ref, cw_ref, chan_ref,
                   gated_ref, square_ref,
                   mask_wide, visible_bias, step_wide, cum_wide, cum_rows, state_act, affinity):
    tokens, inner, state2, heads, local_heads, taps = dims
    prepare(dims, own_ref, proj_ref, seg_col_ref, seg_row_ref, mask_ref, head_ref, cw_ref,
            mask_wide, visible_bias, step_wide, cum_wide, cum_rows, state_act, affinity)
    lane = lax.broadcasted_iota(jnp.int32, (tokens, LANES), 1)
    first = lane < LANES // 2
    blocks = tokens // LANES

    def pair_step(pair, squares):
        here = pl.ds(pl.multiple_of(pair * LANES, LANES), LANES)
        conv, _ = convolve(
            proj_ref[:, here], [cw_ref[j : j + 1, here] for j in range(taps)],
            cw_ref[taps : taps + 1, here], mask_wide,
        )
        values = conv * sigmoid(conv)
        weighted = values * step_wide[pair]
        out = chan_ref[0:1, here] * values
        parts = [out[b * LANES : (b + 1) * LANES] for b in range(blocks)]
        for which in range(2):
            head = 2 * pair + which
            mine = jnp.where(first == (which == 0), weighted, 0.0).astype(BF16)
            for tb in range(blocks):
                t_rows = slice(tb * LANES, (tb + 1) * LANES)
                pieces = []
                for sb in range(tb + 1):
                    s_cols = slice(sb * LANES, (sb + 1) * LANES)
                    distance = (cum_wide[head, t_rows, :] - cum_rows[head, :, s_cols]) + visible_bias[t_rows, s_cols]
                    pieces.append((affinity[t_rows, s_cols] * jnp.exp2(distance)).astype(BF16))
                weights = jnp.concatenate(pieces, 1) if tb > 0 else pieces[0]
                parts[tb] = parts[tb] + jnp.dot(
                    weights, mine[: (tb + 1) * LANES], preferred_element_type=F32
                )
        out = jnp.concatenate(parts, 0)
        gate = proj_ref[:, pl.ds(pl.multiple_of(inner + pair * LANES, LANES), LANES)]
        gated = out * (gate * sigmoid(gate))
        gated_ref[:, here] = (gated * chan_ref[1:2, here]).astype(BF16)
        return squares + gated * gated

    squares = over_pairs(local_heads // 2, pair_step, jnp.zeros((tokens, LANES), F32))
    square_ref[...] = jnp.sum(squares, 1, keepdims=True)


def backward_kernel(dims, own_ref, proj_ref, seg_col_ref, seg_row_ref, mask_ref, head_ref, cw_ref, chan_ref,
                    stats_ref, gn_ref,
                    gp_ref, grad_cw_ref, grad_chan_ref, grad_head_ref,
                    mask_wide, visible_bias, step_wide, cum_wide, cum_rows, state_act, affinity,
                    grad_affinity, row_sums, col_sums, wide_stats):
    tokens, inner, state2, heads, local_heads, taps = dims

    @pl.when(pl.program_id(0) == 0)
    def _():
        grad_cw_ref[...] = jnp.zeros_like(grad_cw_ref)
        grad_chan_ref[...] = jnp.zeros_like(grad_chan_ref)
        grad_head_ref[...] = jnp.zeros_like(grad_head_ref)

    raw, step, log_decay, rows, cols = prepare(
        dims, own_ref, proj_ref, seg_col_ref, seg_row_ref, mask_ref, head_ref, cw_ref,
        mask_wide, visible_bias, step_wide, cum_wide, cum_rows, state_act, affinity)
    grad_affinity[...] = jnp.zeros_like(grad_affinity)
    row_sums[...] = jnp.zeros_like(row_sums)
    col_sums[...] = jnp.zeros_like(col_sums)
    wide_stats[0] = jnp.broadcast_to(stats_ref[:, 0:1], (tokens, LANES))
    wide_stats[1] = jnp.broadcast_to(stats_ref[:, 1:2], (tokens, LANES))
    lane = lax.broadcasted_iota(jnp.int32, (tokens, LANES), 1)
    block_lane = lax.broadcasted_iota(jnp.int32, (LANES, LANES), 1)
    first = lane < LANES // 2
    blocks = tokens // LANES

    def conv_back(grad_conv, shifted, conv_input, here):
        grad_cw_ref[0:1, here] += jnp.sum(grad_conv * conv_input, 0, keepdims=True)
        grad_cw_ref[taps : taps + 1, here] += jnp.sum(grad_conv, 0, keepdims=True)
        back = cw_ref[0:1, here] * grad_conv
        for offset in range(1, taps):
            grad_cw_ref[offset : offset + 1, here] += jnp.sum(grad_conv * shifted[offset - 1], 0, keepdims=True)
            term = (cw_ref[offset : offset + 1, here] * grad_conv) * mask_wide[offset - 1]
            back = back + pltpu.roll(term, tokens - offset, 0)
        return back

    def pair_step(pair, carry):
        here = pl.ds(pl.multiple_of(pair * LANES, LANES), LANES)
        there = pl.ds(pl.multiple_of(inner + pair * LANES, LANES), LANES)
        conv_input = proj_ref[:, here]
        conv, shifted = convolve(
            conv_input, [cw_ref[j : j + 1, here] for j in range(taps)],
            cw_ref[taps : taps + 1, here], mask_wide,
        )
        conv_sig = sigmoid(conv)
        values = conv * conv_sig
        weighted = values * step_wide[pair]
        skip = chan_ref[0:1, here]
        halves = [jnp.where(first == (which == 0), weighted, 0.0).astype(BF16) for which in range(2)]
        out_parts = [(skip * values)[b * LANES : (b + 1) * LANES] for b in range(blocks)]
        for which in range(2):
            head = 2 * pair + which
            for tb in range(blocks):
                t_rows = slice(tb * LANES, (tb + 1) * LANES)
                pieces = []
                for sb in range(tb + 1):
                    s_cols = slice(sb * LANES, (sb + 1) * LANES)
                    distance = (cum_wide[head, t_rows, :] - cum_rows[head, :, s_cols]) + visible_bias[t_rows, s_cols]
                    pieces.append((affinity[t_rows, s_cols] * jnp.exp2(distance)).astype(BF16))
                weights = jnp.concatenate(pieces, 1) if tb > 0 else pieces[0]
                out_parts[tb] = out_parts[tb] + jnp.dot(
                    weights, halves[which][: (tb + 1) * LANES], preferred_element_type=F32
                )
        out = jnp.concatenate(out_parts, 0)
        gate = proj_ref[:, there]
        gate_sig = sigmoid(gate)
        gate_silu = gate * gate_sig
        gated = out * gate_silu
        gn = gn_ref[:, here]
        gain = chan_ref[1:2, here]
        root = wide_stats[0]
        grad_chan_ref[1:2, here] += jnp.sum(gn * gated * root, 0, keepdims=True)
        grad_gated = root * (gn * gain) - gated * wide_stats[1]
        grad_out = grad_gated * gate_silu
        gp_ref[:, there] = (grad_gated * out * (gate_sig * (1.0 + gate * (1.0 - gate_sig)))).astype(BF16)
        grad_chan_ref[0:1, here] += jnp.sum(grad_out * values, 0, keepdims=True)
        back_parts = [jnp.zeros((LANES, LANES), F32) for _ in range(blocks)]
        for which in range(2):
            head = 2 * pair + which
            mine = jnp.where(first == (which == 0), grad_out, 0.0).astype(BF16)
            for tb in range(blocks):
                t_rows = slice(tb * LANES, (tb + 1) * LANES)
                sums = None
                for sb in range(tb + 1):
                    s_cols = slice(sb * LANES, (sb + 1) * LANES)
                    distance = (cum_wide[head, t_rows, :] - cum_rows[head, :, s_cols]) + visible_bias[t_rows, s_cols]
                    decay = jnp.exp2(distance)
                    weights = affinity[t_rows, s_cols] * decay
                    cross = contract_cols(mine[t_rows], halves[which][s_cols])
                    grad_affinity[t_rows, s_cols] += cross * decay
                    energy = cross * weights
                    col_sums[head, :, s_cols] += jnp.sum(energy, 0, keepdims=True)
                    sums = energy if sums is None else sums + energy
                    back_parts[sb] = back_parts[sb] + contract_rows(weights.astype(BF16), mine[t_rows])
                row_sums[t_rows, :] += jnp.where(
                    block_lane == head, jnp.sum(sums, 1, keepdims=True), 0.0
                )
        grad_values = jnp.concatenate(back_parts, 0) * step_wide[pair] + skip * grad_out
        grad_conv = grad_values * (conv_sig * (1.0 + conv * (1.0 - conv_sig)))
        gp_ref[:, here] = conv_back(grad_conv, shifted, conv_input, here).astype(BF16)
        return carry

    over_pairs(local_heads // 2, pair_step, 0)

    common = 2 * inner
    grad_states = [
        contract_rows(grad_affinity[...], state_act[1], HIGHEST),
        jnp.dot(grad_affinity[...], state_act[0], precision=HIGHEST, preferred_element_type=F32),
    ]
    for part in range(state2 // LANES):
        at = slice(inner + part * LANES, inner + (part + 1) * LANES)
        spot = slice(common + part * LANES, common + (part + 1) * LANES)
        conv_input = proj_ref[:, spot]
        conv, shifted = convolve(
            conv_input, [cw_ref[j : j + 1, at] for j in range(taps)], cw_ref[taps : taps + 1, at], mask_wide
        )
        conv_sig = sigmoid(conv)
        grad_conv = grad_states[part] * (conv_sig * (1.0 + conv * (1.0 - conv_sig)))
        gp_ref[:, spot] = conv_back(grad_conv, shifted, conv_input, at).astype(BF16)

    col_rows = [col_sums[head] for head in range(local_heads)]
    col_rows.append(jnp.zeros((LANES - local_heads, tokens), F32))
    col_energy = jnp.concatenate(col_rows, 0).T
    upper = jnp.where(cols >= rows, 1.0, 0.0).astype(F32)
    grad_decay = jnp.dot(upper, row_sums[...] - col_energy, precision=HIGHEST, preferred_element_type=F32)
    step_sig = sigmoid(raw)
    ratio = jnp.where(raw < -20.0, 1.0, step_sig / jnp.maximum(step, 1e-30))
    grad_raw = col_energy * ratio + (head_ref[1:2, :] * grad_decay) * step_sig
    grad_head_ref[0:1, :] += jnp.sum(grad_raw, 0, keepdims=True)
    grad_head_ref[1:2, :] += jnp.sum(grad_decay * log_decay, 0, keepdims=True)
    placed = pltpu.roll(grad_raw, own_ref[0] * local_heads, 1)
    gp_ref[:, common + state2 : common + state2 + heads] = placed[:, :heads].astype(BF16)


def mixer_specs(dims, width):
    tokens, inner, state2, heads, local_heads, taps = dims
    fixed = lambda shape: pl.BlockSpec(shape, lambda s: (0,) * len(shape))
    in_specs = [
        pl.BlockSpec(memory_space=pltpu.SMEM),
        pl.BlockSpec((tokens, width), lambda s: (s, 0)),
        pl.BlockSpec((None, tokens, 1), lambda s: (s, 0, 0)),
        pl.BlockSpec((None, 1, tokens), lambda s: (s, 0, 0)),
        pl.BlockSpec((None, tokens, 8), lambda s: (s, 0, 0)),
        fixed((8, LANES)),
        fixed((8, inner + state2)),
        fixed((8, inner)),
    ]
    scratch = [
        pltpu.VMEM((taps - 1, tokens, LANES), F32),
        pltpu.VMEM((tokens, tokens), F32),
        pltpu.VMEM((local_heads // 2, tokens, LANES), F32),
        pltpu.VMEM((local_heads, tokens, LANES), F32),
        pltpu.VMEM((local_heads, 1, tokens), F32),
        pltpu.VMEM((state2 // LANES, tokens, LANES), F32),
        pltpu.VMEM((tokens, tokens), F32),
    ]
    return in_specs, scratch


def mix_forward(dims, operands):
    tokens, inner, state2, heads, local_heads, taps = dims
    total, width = operands[1].shape
    in_specs, scratch = mixer_specs(dims, width)
    return pl.pallas_call(
        functools.partial(forward_kernel, dims),
        grid=(total // tokens,),
        in_specs=in_specs,
        out_specs=[
            pl.BlockSpec((tokens, inner), lambda s: (s, 0)),
            pl.BlockSpec((tokens, 1), lambda s: (s, 0)),
        ],
        out_shape=[
            jax.ShapeDtypeStruct((total, inner), BF16),
            jax.ShapeDtypeStruct((total, 1), F32),
        ],
        scratch_shapes=scratch,
        compiler_params=pltpu.CompilerParams(vmem_limit_bytes=48 << 20),
        cost_estimate=pl.CostEstimate(
            flops=total * local_heads * tokens * 4 * 64,
            bytes_accessed=total * width * 4,
            transcendentals=total * local_heads * tokens,
        ),
        name="mix_forward",
    )(*operands)


def mix_backward(dims, operands, stats, grad_normed):
    tokens, inner, state2, heads, local_heads, taps = dims
    total, width = operands[1].shape
    in_specs, scratch = mixer_specs(dims, width)
    fixed = lambda shape: pl.BlockSpec(shape, lambda s: (0,) * len(shape))
    return pl.pallas_call(
        functools.partial(backward_kernel, dims),
        grid=(total // tokens,),
        in_specs=in_specs + [
            pl.BlockSpec((tokens, 2), lambda s: (s, 0)),
            pl.BlockSpec((tokens, inner), lambda s: (s, 0)),
        ],
        out_specs=[
            pl.BlockSpec((tokens, width), lambda s: (s, 0)),
            fixed((8, inner + state2)),
            fixed((8, inner)),
            fixed((8, LANES)),
        ],
        out_shape=[
            jax.ShapeDtypeStruct((total, width), BF16),
            jax.ShapeDtypeStruct((8, inner + state2), F32),
            jax.ShapeDtypeStruct((8, inner), F32),
            jax.ShapeDtypeStruct((8, LANES), F32),
        ],
        scratch_shapes=scratch + [
            pltpu.VMEM((tokens, tokens), F32),
            pltpu.VMEM((tokens, LANES), F32),
            pltpu.VMEM((local_heads, 1, tokens), F32),
            pltpu.VMEM((2, tokens, LANES), F32),
        ],
        compiler_params=pltpu.CompilerParams(vmem_limit_bytes=48 << 20),
        cost_estimate=pl.CostEstimate(
            flops=total * local_heads * tokens * 12 * 64,
            bytes_accessed=total * width * 6,
            transcendentals=2 * total * local_heads * tokens,
        ),
        name="mix_backward",
    )(*operands, stats, grad_normed)


def swap(array, axis, size, bit):
    return lax.ppermute(array, axis, [(i, i ^ bit) for i in range(size)])


def axis_bits(size):
    bits = []
    bit = 1
    while bit < size:
        bits.append(bit)
        bit *= 2
    return bits


def gather_relative(array, axis, size):
    held = array[None]
    for bit in reversed(axis_bits(size)):
        held = jnp.concatenate([held, swap(held, axis, size, bit)], 0)
    return held


def scatter_relative(array, axis, size):
    total = array
    for bit in axis_bits(size):
        half = total.shape[0] // 2
        received = swap(total[half:].astype(BF16), axis, size, bit)
        total = total[:half].astype(F32) + received.astype(F32)
    return total[0]


def sum_tokens(array, axis, size):
    kinds, tokens = array.shape
    for bit in axis_bits(size):
        stride = tokens // (2 * bit)
        received = swap(array, axis, size, bit).reshape(kinds, bit, 2, stride)
        array = array + received[:, :, ::-1].reshape(kinds, tokens)
    return array


def halve_sum(array, order, replica, size):
    total = array
    for bit in order:
        blocks, rows, columns = total.shape
        mine = (replica // bit) % 2
        halves = total.reshape(blocks, 2, rows // 2, columns)
        kept = lax.dynamic_index_in_dim(halves, mine, 1, keepdims=False)
        sent = lax.dynamic_index_in_dim(halves, 1 - mine, 1, keepdims=False)
        received = swap(sent.astype(BF16), "replica", size, bit)
        total = kept + received.astype(F32)
    return total


def double_gather(array, order, replica, size):
    held = array
    for bit in reversed(order):
        received = swap(held, "replica", size, bit)
        upper = (replica // bit) % 2 == 1
        held = jnp.where(
            upper,
            jnp.concatenate([received, held], 1),
            jnp.concatenate([held, received], 1),
        )
    return held


def flip(index, bit):
    return index + bit * (1 - 2 * ((index // bit) % 2))


MESH = pl.DeviceIdType.MESH


def greet(peers):
    barrier = pltpu.get_barrier_semaphore()
    for peer in peers:
        pl.semaphore_signal(barrier, inc=1, device_id=peer, device_id_type=MESH)
    pl.semaphore_wait(barrier, len(peers))


def copy_peers(me):
    return [flip(me, 1), flip(me, 2), flip(flip(me, 1), 2)]


def gather_kernel(full_inner, inner, x_ref, seg_ref, small_ref, w_ref,
                  x_all_ref, seg_all_ref, small_all_ref, cols_ref,
                  x_held, cols_held, send_sems, recv_sems, local_sems, store_sems):
    me = lax.axis_index("fsdp")
    replica = lax.axis_index("replica")
    depth, common = w_ref.shape[1], w_ref.shape[0] - 2 * full_inner
    peers = [(replica, peer) for peer in copy_peers(me)]
    beside, above = (flip(replica, 1), me), (flip(replica, 2), me)
    greet(peers + [beside, above])
    number = [0]
    started = []

    def send(from_ref, to_ref, device):
        slot = number[0]
        number[0] += 1
        copy = pltpu.make_async_remote_copy(
            src_ref=from_ref, dst_ref=to_ref, send_sem=send_sems.at[slot], recv_sem=recv_sems.at[slot],
            device_id=device, device_id_type=MESH,
        )
        copy.start()
        started.append(copy)
        return copy

    parts = [(0, inner), (inner, inner), (2 * inner, common)]

    def targets(owner, first, count):
        lanes = pl.ds(pl.multiple_of(owner * depth, depth), depth)
        return [
            cols_ref.at[pl.ds(pl.multiple_of(base + first * (length // 4), 16), count * (length // 4)), lanes]
            for base, length in parts
        ]

    def sources(device, first, count):
        bases = [full_inner + device * inner, device * inner, 2 * full_inner]
        return [
            w_ref.at[pl.ds(pl.multiple_of(base + first * (length // 4), 16), count * (length // 4))]
            for base, (_, length) in zip(bases, parts)
        ]

    def send_parts(from_refs, to_refs, device):
        return [send(source, target, device) for source, target in zip(from_refs, to_refs)]

    spot = replica % 4
    across = [send_parts(sources(peers[which][1], spot, 1), targets(me, spot, 1), peers[which]) for which in (1, 2)]
    x_y = send(x_ref, x_all_ref.at[1], peers[1])
    smalls = [send(small_ref, small_all_ref.at[me], peer) for peer in peers]
    smalls += [send(seg_ref, seg_all_ref.at[slot], peer) for peer, slot in zip(peers, (2, 1, 3))]
    near = send_parts(sources(peers[0][1], 0, 4), targets(me, 0, 4), peers[0])
    x_near = send(x_ref, x_all_ref.at[2], peers[0])
    held = [cols_held.at[pl.ds(base, length)] for base, length in parts] + [x_held]
    own = list(zip(sources(me, 0, 4) + [x_ref], held, targets(me, 0, 4) + [x_all_ref.at[0]]))
    loads = [pltpu.make_async_copy(source, held, local_sems.at[i]) for i, (source, held, _) in enumerate(own)]
    stores = [pltpu.make_async_copy(held, target, store_sems.at[i]) for i, (_, held, target) in enumerate(own)]
    stores += [
        pltpu.make_async_copy(small_ref, small_all_ref.at[me], local_sems.at[4]),
        pltpu.make_async_copy(seg_ref, seg_all_ref.at[0], local_sems.at[5]),
    ]
    for copy in loads + stores[4:]:
        copy.start()
    for load, store in zip(loads, stores):
        load.wait()
        store.start()

    def relay(which, first, count, device):
        refs = targets(peers[which][1], first, count)
        return send_parts(refs, refs, device)

    for copy in across[0]:
        copy.wait_recv()
    first_beside = relay(1, spot, 1, beside)
    for copy in across[1]:
        copy.wait_recv()
    first_above = relay(2, spot, 1, above)
    for copy in first_beside:
        copy.wait_recv()
    last = relay(1, (spot // 2) * 2, 2, above)
    for copy in first_above:
        copy.wait_recv()
    last += relay(2, spot, 1, beside)
    last += relay(2, flip(spot, 2), 1, beside)
    x_y.wait_recv()
    last.append(send(x_all_ref.at[1], x_all_ref.at[3], peers[0]))
    for copy in last + smalls + near + [x_near]:
        copy.wait_recv()
    for copy in stores:
        copy.wait()
    for copy in started:
        copy.wait_send()


GATHER_COPIES = 34


def gather_inputs(size, inner, x, segments, small, w_flipped):
    full, depth = w_flipped.shape
    full_inner = inner * size
    columns = 2 * inner + full - 2 * full_inner
    anywhere = pl.BlockSpec(memory_space=pl.ANY)
    return pl.pallas_call(
        functools.partial(gather_kernel, full_inner, inner),
        in_specs=[anywhere] * 4,
        out_specs=[anywhere] * 4,
        out_shape=[
            jax.ShapeDtypeStruct((size,) + x.shape, BF16),
            jax.ShapeDtypeStruct((size,) + segments.shape, jnp.int32),
            jax.ShapeDtypeStruct((size,) + small.shape, F32),
            jax.ShapeDtypeStruct((columns, size * depth), BF16),
        ],
        scratch_shapes=[
            pltpu.VMEM(x.shape, BF16),
            pltpu.VMEM((columns, depth), BF16),
            pltpu.SemaphoreType.DMA((GATHER_COPIES,)),
            pltpu.SemaphoreType.DMA((GATHER_COPIES,)),
            pltpu.SemaphoreType.DMA((6,)),
            pltpu.SemaphoreType.DMA((4,)),
        ],
        compiler_params=pltpu.CompilerParams(
            collective_id=1, has_side_effects=True, vmem_limit_bytes=16 << 20
        ),
        cost_estimate=pl.CostEstimate(flops=0, bytes_accessed=200 << 20, transcendentals=0),
        name="gather_inputs",
    )(x, segments, small, w_flipped)


PARTS = {
    "side": {"got": 2, "lift": 2, "sent": 4, "swapped": 4, "final": 4},
    "lift": {"got": 1, "sent": 2, "swapped": 2, "sent_side": 4, "got_side": 4, "final": 4},
}
SLOTS = 9
IN_ROWS = (64,) * 32
SHARED_AT = 4
COLUMN_BLOCK = 256
ROW_BLOCK = 256
LANE_TILE = 256
PER_TURN = 3
TOKEN_PIECES = 8


def reduce_chunks(inner, common):
    pieces = []
    start = 0
    for rows in IN_ROWS:
        pieces.append(("in", start, rows))
        start += rows
    pieces.insert(SHARED_AT, ("shared", 0, common))
    counts = {}
    placed = []
    for number, (kind, start, rows) in enumerate(pieces):
        order = "lift" if number % 3 == 2 else "side"
        key = (kind == "shared", rows, order)
        where = counts.get(key, 0)
        counts[key] = where + 1
        placed.append((kind, start, rows, order, where))
    return placed, counts


def reduce_kernel(plan, gp_ref, scaled_ref, cols_ref, tok_out_ref, small_ref,
                  sum_in_ref, sum_shared_ref, got_out_ref, own_grad_ref, got_grad_ref, small_sum_ref,
                  far_land_ref, across_ref, *scratch):
    chunks, counts, inner, depth, common, norm_row = plan
    groups = {}
    position = 0
    for key in counts:
        names = list(PARTS[key[2]])
        groups[key] = dict(zip(names, scratch[position : position + len(names)]))
        position += len(names)
    (shared_in, shared_sum, small_got, scaled, cols, grads, gp_cols, gp_flipped, gp_rows, tiles, far_tile, norm_sum,
     send_sems, recv_sems, local_sems, tok_send, tok_recv,
     small_send, small_recv, shared_send, shared_recv, far_send, far_recv, load_sems, store_sems) = scratch[position:]
    whole_loads = [
        pltpu.make_async_copy(scaled_ref, scaled, load_sems.at[0]),
        pltpu.make_async_copy(cols_ref, cols, load_sems.at[1]),
    ]
    for copy in whole_loads:
        copy.start()
    loaded = [False, False]

    def need(which):
        if not loaded[which]:
            whole_loads[which].wait()
            loaded[which] = True

    column_blocks = [(start, COLUMN_BLOCK) for start in range(0, 2 * inner, COLUMN_BLOCK)]
    column_blocks.insert(1, (2 * inner, common))
    width = scaled.shape[1]
    rows_of_block = tiles.shape[1]
    lane_tiles = width // LANE_TILE
    column_loads = []
    columns_done = []

    def load_columns(number):
        if number < len(column_blocks):
            start, count = column_blocks[number]
            copy = pltpu.make_async_copy(
                gp_ref.at[:, pl.ds(start, count)], gp_cols.at[:, pl.ds(0, count)], load_sems.at[2]
            )
            copy.start()
            column_loads.append(copy)

    def next_columns():
        number = len(columns_done)
        if number == len(column_blocks):
            return
        start, count = column_blocks[number]
        need(0)
        column_loads[number].wait()
        gp_flipped[pl.ds(0, count), :] = gp_cols[:, pl.ds(0, count)].T
        load_columns(number + 1)

        def lanes_step(tile, carry):
            lanes = pl.ds(pl.multiple_of(tile * LANE_TILE, LANE_TILE), LANE_TILE)
            grads[pl.ds(start, count), lanes] = jnp.dot(
                gp_flipped[pl.ds(0, count), :], scaled[:, lanes], preferred_element_type=F32
            ).astype(BF16)
            return carry

        lax.fori_loop(0, lane_tiles, lanes_step, 0)
        columns_done.append(start)

    def ensure_columns(start):
        while start not in columns_done:
            next_columns()

    load_columns(0)
    me = lax.axis_index("fsdp")
    replica = lax.axis_index("replica")
    up = replica // 2
    inside = (up == 1) | (up == 2)
    outside = (up == 0) | (up == 3)
    half = up // 2
    aside = replica % 2
    beside = (flip(replica, 1), me)
    partner = (flip(replica, 2), me)
    middle = (flip(flip(replica, 2), 4), me)
    peers = [(replica, peer) for peer in copy_peers(me)]
    greet(peers + [beside, partner, middle])

    def remote(from_ref, to_ref, device, sends, recvs):
        return pltpu.make_async_remote_copy(
            src_ref=from_ref, dst_ref=to_ref, send_sem=sends, recv_sem=recvs, device_id=device, device_id_type=MESH
        )

    def lanes_of(device):
        return pl.ds(pl.multiple_of(device * depth, depth), depth)

    def activations():
        rows = got_out_ref.shape[0] // TOKEN_PIECES
        copies = []
        for piece in range(TOKEN_PIECES):
            at = pl.ds(piece * rows, rows)
            copy = remote(tok_out_ref.at[1, at], got_out_ref.at[at], peers[1], tok_send.at[0, piece], tok_recv.at[0, piece])
            copy.start()
            copies.append(copy)
            yield
        for piece in range(TOKEN_PIECES):
            at = pl.ds(piece * rows, rows)
            copy = remote(across_ref.at[at], got_grad_ref.at[at], peers[1], tok_send.at[1, piece], tok_recv.at[1, piece])
            copy.start()
            copies.append(copy)
            yield
        for copy in copies:
            copy.wait()

    def row_products():
        half_blocks = gp_ref.shape[0] // (2 * rows_of_block)
        quarter_blocks = half_blocks // 2
        later = list(range(quarter_blocks, half_blocks))
        sooner = list(range(quarter_blocks))
        order = [(True, i) for i in later] + [(False, i) for i in later]
        order += [(True, i) for i in sooner] + [(False, i) for i in sooner]
        norm_sum[...] = jnp.zeros_like(norm_sum)
        row_loads = []

        def load_rows(number):
            if number < len(order):
                far, block = order[number]
                at = (half_blocks + block if far else block) * rows_of_block
                copy = pltpu.make_async_copy(gp_ref.at[pl.ds(at, rows_of_block)], gp_rows, load_sems.at[3])
                copy.start()
                row_loads.append((copy, at))

        load_rows(0)
        need(0)
        need(1)
        arrivals = {}
        busy = [None, None]
        for number, (far, block) in enumerate(order):
            slot = number % 2
            if busy[slot] is not None:
                busy[slot]()
            if not far:
                arrivals[block].wait_recv()
                load = pltpu.make_async_copy(far_land_ref.at[block], far_tile, load_sems.at[4])
                load.start()
                load.wait()
            copy, at = row_loads[number]
            copy.wait()

            def lanes_step(tile, carry):
                lanes = pl.ds(pl.multiple_of(tile * LANE_TILE, LANE_TILE), LANE_TILE)
                part = jnp.dot(gp_rows[...], cols[:, lanes], preferred_element_type=F32)
                norm_sum[:, lanes] += jnp.sum(
                    part * scaled[pl.ds(at, rows_of_block), lanes].astype(F32), 0, keepdims=True
                )
                if not far:
                    part = part + far_tile[:, lanes].astype(F32)
                tiles[slot, :, lanes] = part.astype(BF16)
                return carry

            lax.fori_loop(0, lane_tiles, lanes_step, 0)
            load_rows(number + 1)
            if far:
                sent = remote(tiles.at[slot], far_land_ref.at[block], peers[0], far_send.at[block], far_recv.at[block])
                sent.start()
                arrivals[block] = sent
                busy[slot] = sent.wait_send
            else:
                target = own_grad_ref if block < quarter_blocks else across_ref
                place = pl.ds((block % quarter_blocks) * rows_of_block, rows_of_block)
                store = pltpu.make_async_copy(tiles.at[slot], target.at[place], store_sems.at[block])
                store.start()
                busy[slot] = store.wait
            yield
        for wait in busy:
            wait()
        for tile in range(width // LANES):
            small_sum_ref[norm_row + tile : norm_row + tile + 1, :] = norm_sum[:, tile * LANES : (tile + 1) * LANES]

    def smalls():
        small_sum_ref[...] = small_ref[...]
        yield from row_products()
        for level, peer in enumerate([peers[0], peers[1], beside, partner, middle]):
            copy = remote(small_sum_ref, small_got.at[level], peer, small_send.at[level], small_recv.at[level])
            copy.start()
            yield
            copy.wait()
            small_sum_ref[...] += small_got[level]

    def run(number, kind, start, rows, order, where):
        held = {name: ref.at[where] for name, ref in groups[kind == "shared", rows, order].items()}
        if kind == "in":
            group = 0 if start >= inner else 4
            local_start = start % inner
            ensure_columns(start // COLUMN_BLOCK * COLUMN_BLOCK)
            base_ref, base_start = grads, start
            place = lambda at, count: sum_in_ref.at[pl.ds(group, 4), pl.ds(pl.multiple_of(local_start + at, 16), count)]
        else:
            ensure_columns(2 * inner)
            base_ref, base_start = shared_sum, 0
            place = lambda at, count: sum_shared_ref.at[pl.ds(at, count)]
            copies = []
            for offset in range(3):
                copy = remote(
                    grads.at[pl.ds(2 * inner, rows), lanes_of(peers[offset][1])],
                    shared_in.at[offset], peers[offset], shared_send.at[offset], shared_recv.at[offset],
                )
                copy.start()
                copies.append(copy)
            yield
            total = grads[pl.ds(2 * inner, rows), lanes_of(me)].astype(F32)
            for offset in range(3):
                copies[offset].wait_recv()
                total = total + shared_in[offset].astype(F32)
            shared_sum[...] = total.astype(BF16)

        def source(at, count):
            return base_ref.at[pl.ds(pl.multiple_of(base_start + at, 16), count)]

        def link(from_ref, to_ref, device, slot):
            return remote(from_ref, to_ref, device, send_sems.at[number, slot], recv_sems.at[number, slot])

        def added(names_at, at, count):
            total = source(at, count)[...].astype(F32)
            for name, base in names_at:
                local = pl.multiple_of(at - base, count)
                total = total + held[name][pl.ds(local, count), :].astype(F32)
            return total

        two, four = rows // 2, rows // 4
        if order == "side":
            mine, other = pl.multiple_of(aside * two, two), pl.multiple_of((1 - aside) * two, two)
            low, high = pl.multiple_of(mine + half * four, four), pl.multiple_of(mine + (1 - half) * four, four)
            side = link(source(other, two), held["got"], beside, 0)
            side.start()
            yield
            side.wait_recv()
            lift = link(held["lift"], held["lift"], partner, 1)

            @pl.when(outside)
            def _():
                held["lift"][...] = added([("got", mine)], mine, two).astype(BF16)
                lift.start()

            yield
            bases = [("got", mine), ("lift", mine)]
            across = link(held["sent"], held["swapped"], middle, 2)

            @pl.when(inside)
            def _():
                lift.wait_recv()
                held["sent"][...] = added(bases, high, four).astype(BF16)
                across.start()

            yield
            bases = bases + [("swapped", low)]
        else:
            mine, other = pl.multiple_of(half * two, two), pl.multiple_of((1 - half) * two, two)
            low, high = pl.multiple_of(mine + aside * four, four), pl.multiple_of(mine + (1 - aside) * four, four)
            lift = link(source(0, rows), held["got"], partner, 1)

            @pl.when(outside)
            def _():
                lift.start()

            yield
            bases = [("got", 0)]
            across = link(held["sent"], held["swapped"], middle, 2)

            @pl.when(inside)
            def _():
                lift.wait_recv()
                held["sent"][...] = added(bases, other, two).astype(BF16)
                across.start()

            yield
            bases = bases + [("swapped", mine)]
            side = link(held["sent_side"], held["got_side"], beside, 0)

            @pl.when(inside)
            def _():
                across.wait_recv()
                held["sent_side"][...] = added(bases, high, four).astype(BF16)
                side.start()

            yield
            bases = bases + [("got_side", low)]

        final = held["final"]
        trade = []
        if kind == "in":
            target = sum_in_ref.at[group + me, pl.ds(pl.multiple_of(local_start + low, 16), four)]
            trade = [
                link(final.at[:, lanes_of(peers[offset][1])], target, peers[offset], 3 + offset) for offset in range(3)
            ]
            own = pltpu.make_async_copy(final.at[:, lanes_of(me)], target, local_sems.at[number])
        else:
            own = pltpu.make_async_copy(final, place(low, four), local_sems.at[number])

        if order == "side":
            back = [
                link(place(low, four), place(low, four), middle, 6),
                link(place(mine, two), place(mine, two), partner, 7),
                link(place(mine, two), place(mine, two), beside, 8),
            ]
        else:
            back = [
                link(place(low, four), place(low, four), beside, 6),
                link(place(mine, two), place(mine, two), middle, 7),
                link(place(0, rows), place(0, rows), partner, 8),
            ]

        @pl.when(inside)
        def _():
            (across if order == "side" else side).wait_recv()
            final[...] = added(bases, low, four).astype(BF16)
            for copy in trade:
                copy.start()
            own.start()
            own.wait()
            for copy in trade:
                copy.wait_recv()
            back[0].start()

        yield

        @pl.when(inside)
        def _():
            back[0].wait_recv()
            back[1].start()
            if order == "side":
                back[2].start()

        yield
        if order == "side":

            @pl.when(outside)
            def _():
                back[1].wait_recv()
                back[2].start()

            yield
            back[2].wait_recv()
            side.wait_send()
            back[2].wait_send()

            @pl.when(outside)
            def _():
                lift.wait_send()

            @pl.when(inside)
            def _():
                across.wait_send()
                for copy in trade + back[:2]:
                    copy.wait_send()

        else:

            @pl.when(inside)
            def _():
                back[1].wait_recv()
                back[2].start()

            yield

            @pl.when(outside)
            def _():
                back[2].wait_recv()
                lift.wait_send()

            @pl.when(inside)
            def _():
                across.wait_send()
                side.wait_send()
                for copy in trade + back:
                    copy.wait_send()

        if kind == "shared":
            for copy in copies:
                copy.wait_send()

    waiting = [run(number, *chunk) for number, chunk in enumerate(chunks)]
    active, extra = [], [smalls(), activations()]

    def advance(running):
        still = []
        for steps in running:
            try:
                next(steps)
                still.append(steps)
            except StopIteration:
                pass
        return still

    while waiting or active:
        active = advance(active + waiting[:PER_TURN])
        waiting = waiting[PER_TURN:]
        extra = advance(extra)
        next_columns()
    while extra:
        extra = advance(extra)


def reduce_gradients(size, depth, inner, common, norm_row, gp, scaled, cols, tok_out, small):
    total, width = scaled.shape
    own_rows = tok_out.shape[1]
    chunks, counts = reduce_chunks(inner, common)
    scratch = []
    for (shared, rows, order), count in counts.items():
        for fraction in PARTS[order].values():
            scratch.append(pltpu.VMEM((count, rows // fraction, depth if shared else width), BF16))
    sems = pltpu.SemaphoreType.DMA
    half_blocks = total // 2 // ROW_BLOCK
    scratch += [
        pltpu.VMEM((3, common, depth), BF16),
        pltpu.VMEM((common, depth), BF16),
        pltpu.VMEM((5,) + small.shape, F32),
        pltpu.VMEM(scaled.shape, BF16),
        pltpu.VMEM(cols.shape, BF16),
        pltpu.VMEM(cols.shape, BF16),
        pltpu.VMEM((total, max(common, COLUMN_BLOCK)), BF16),
        pltpu.VMEM((max(common, COLUMN_BLOCK), total), BF16),
        pltpu.VMEM((ROW_BLOCK, gp.shape[1]), BF16),
        pltpu.VMEM((2, ROW_BLOCK, width), BF16),
        pltpu.VMEM((ROW_BLOCK, width), BF16),
        pltpu.VMEM((1, width), F32),
        sems((len(chunks), SLOTS)), sems((len(chunks), SLOTS)), sems((len(chunks),)),
        sems((2, TOKEN_PIECES)), sems((2, TOKEN_PIECES)), sems((5,)), sems((5,)), sems((3,)), sems((3,)),
        sems((half_blocks,)), sems((half_blocks,)), sems((5,)), sems((half_blocks,)),
    ]
    anywhere = pl.BlockSpec(memory_space=pl.ANY)
    local = pl.BlockSpec(memory_space=pltpu.VMEM)
    own = jax.ShapeDtypeStruct((own_rows, width), BF16)
    return pl.pallas_call(
        functools.partial(reduce_kernel, (chunks, counts, inner, depth, common, norm_row)),
        in_specs=[anywhere] * 4 + [local],
        out_specs=[anywhere] * 5 + [local] + [anywhere] * 2,
        out_shape=[
            jax.ShapeDtypeStruct((2 * size, inner, depth), BF16),
            jax.ShapeDtypeStruct((common, depth), BF16),
            own, own, own,
            jax.ShapeDtypeStruct(small.shape, F32),
            jax.ShapeDtypeStruct((half_blocks, ROW_BLOCK, width), BF16),
            own,
        ],
        scratch_shapes=scratch,
        compiler_params=pltpu.CompilerParams(
            collective_id=0, has_side_effects=True, vmem_limit_bytes=60 << 20
        ),
        cost_estimate=pl.CostEstimate(
            flops=4 * total * gp.shape[1] * width, bytes_accessed=600 << 20, transcendentals=0
        ),
        name="reduce_gradients",
    )(gp, scaled, cols, tok_out, small)


def small_pieces(size, copies, depth, inner, columns, me, replica, scaled_low, gp, normed_low, cot_all):
    replica_bits = axis_bits(copies)
    orders = [replica_bits, replica_bits[1:] + replica_bits[:1]]
    pieces = []
    part_rows = inner // 2
    for part in range(2):
        grad = contract_rows(normed_low[:, part * part_rows : (part + 1) * part_rows], cot_all)
        order = orders[part % 2]
        mine = halve_sum(grad[None], order, replica, copies)
        pieces.append(double_gather(mine.astype(BF16), order, replica, copies)[0])
    grad_w_out = jnp.concatenate(pieces, 0).astype(F32)


    def columns_sum(start, stop, order, shared):
        grad = contract_rows(scaled_low, gp[:, start:stop])
        mine = halve_sum(grad.reshape(size, depth, stop - start), order, replica, copies)
        own = lax.dynamic_index_in_dim(mine, me, 0, keepdims=False)
        got = [own]
        for offset in range(1, size):
            there = lax.dynamic_index_in_dim(mine, me ^ offset, 0, keepdims=False)
            got.append(swap(there.astype(BF16), "fsdp", size, offset))
        if shared:
            held = sum(block.astype(F32) for block in got)[None].astype(BF16)
        else:
            held = jnp.stack([block.astype(BF16) for block in got])
        return double_gather(held, order, replica, copies)

    halves = inner // 2
    value_parts = [columns_sum(c * halves, (c + 1) * halves, orders[c % 2], False) for c in range(2)]
    gate_parts = [
        columns_sum(inner + c * halves, inner + (c + 1) * halves, orders[c % 2], False) for c in range(2)
    ]
    shared_part = columns_sum(2 * inner, columns, orders[0], True)[0]

    def in_place(parts):
        placed = []
        for device in range(size):
            for part in parts:
                placed.append(lax.dynamic_index_in_dim(part, me ^ device, 0, keepdims=False))
        return placed

    grad_w_in = jnp.concatenate(in_place(gate_parts) + in_place(value_parts) + [shared_part], 1).astype(F32)
    return grad_w_in, grad_w_out


def recut(size, full_inner, inner, me, w_in):
    depth, full = w_in.shape

    def columns_of(device):
        return jnp.concatenate(
            [
                lax.dynamic_slice(w_in, (0, full_inner + device * inner), (depth, inner)),
                lax.dynamic_slice(w_in, (0, device * inner), (depth, inner)),
                w_in[:, 2 * full_inner :],
            ],
            1,
        )

    w_cols = jnp.zeros((size * depth, 2 * inner + full - 2 * full_inner), BF16)
    w_cols = lax.dynamic_update_slice(w_cols, columns_of(me), (me * depth, 0))
    for offset in range(1, size):
        received = swap(columns_of(me ^ offset), "fsdp", size, offset)
        w_cols = lax.dynamic_update_slice(w_cols, received, ((me ^ offset) * depth, 0))
    return w_cols


def on_device(copies, size, hidden_in, segment_ids, cotangent, norm_gain, w_in, conv_weight, conv_bias,
              dt_bias, a_log, skip_gain, gate_gain, w_out):
    micro_count, seq_count, tokens, width = hidden_in.shape
    own_rows = micro_count * seq_count * tokens
    total = size * own_rows
    inner = gate_gain.shape[0]
    local_heads = dt_bias.shape[0]
    heads = local_heads * size
    channel = inner // local_heads
    full_inner = inner * size
    taps, own_conv = conv_weight.shape
    conv_width = own_conv * size
    state2 = conv_width - full_inner
    depth = w_in.shape[0]
    common = state2 + heads
    columns = 2 * inner + common
    dims = (tokens, inner, state2, heads, local_heads, taps)
    me = lax.axis_index("fsdp")
    replica = lax.axis_index("replica")

    own_x = hidden_in.reshape(own_rows, width)
    own_cot = cotangent.reshape(own_rows, width)
    small = jnp.concatenate([norm_gain, conv_weight.reshape(-1), conv_bias])
    segments = segment_ids.reshape(micro_count * seq_count, tokens)
    fused = copies == 8 and size == 4 and sum(IN_ROWS) == 2 * inner
    if fused:
        padded = jnp.pad(small.astype(F32), (0, -small.shape[0] % (8 * LANES))).reshape(-1, LANES)
        x_all, seg_all, small, w_cols = gather_inputs(
            size, inner, own_x, segments.reshape(-1, LANES), padded, w_in.T
        )
        x_all = x_all.reshape(total, width)
        small = small.reshape(size, -1)
        own_cot_later, _ = lax.optimization_barrier((own_cot, seg_all))
        cot_across = swap(own_cot_later, "fsdp", size, 2)
    else:
        small = lax.all_gather(small, "fsdp", axis=0, tiled=False).astype(F32)
        x_all = gather_relative(own_x, "fsdp", size).reshape(total, width)
        seg_all = gather_relative(segments, "fsdp", size)
        w_cols = recut(size, full_inner, inner, me, w_in).T
        cot_all = gather_relative(own_cot, "fsdp", size).reshape(total, width)
    seg_all = seg_all.reshape(total // tokens, tokens)
    full_norm = small[:, :depth].reshape(1, width)
    full_cw = small[:, depth : depth + taps * own_conv].reshape(size, taps, own_conv)
    full_cw = full_cw.transpose(1, 0, 2).reshape(taps, conv_width)
    full_cb = small[:, depth + taps * own_conv : depth + (taps + 1) * own_conv].reshape(1, conv_width)

    def normalise(inputs):
        wide = inputs.astype(F32)
        return lax.rsqrt(jnp.mean(wide * wide, -1, keepdims=True) + EPS)

    scaled_low = (x_all.astype(F32) * normalise(x_all) * full_norm).astype(BF16)
    projected = contract_cols(scaled_low, w_cols)

    conv_all = jnp.concatenate([full_cw, full_cb, jnp.zeros((7 - taps, conv_width), F32)], 0)
    conv_own = jnp.concatenate(
        [lax.dynamic_slice(conv_all, (0, me * inner), (8, inner)), conv_all[:, full_inner:]], 1
    )
    pad_heads = lambda row: jnp.pad(row.astype(F32), (0, LANES - local_heads))
    head_rows = jnp.stack([pad_heads(dt_bias), pad_heads(-jnp.exp(a_log.astype(F32)))])
    head_rows = jnp.pad(head_rows, ((0, 6), (0, 0)))
    chan_rows = jnp.stack([jnp.repeat(skip_gain.astype(F32), channel), gate_gain.astype(F32)])
    chan_rows = jnp.pad(chan_rows, ((0, 6), (0, 0)))
    same = []
    for offset in range(1, taps):
        equal = (seg_all[:, offset:] == seg_all[:, :-offset]).astype(F32)
        same.append(jnp.pad(equal, ((0, 0), (offset, 0))))
    same = jnp.pad(jnp.stack(same, 2), ((0, 0), (0, 0), (0, 9 - taps)))
    operands = (
        me.astype(jnp.int32).reshape(1), projected, seg_all[:, :, None], seg_all[:, None, :], same,
        head_rows, conv_own, chan_rows,
    )
    gated, squares = mix_forward(dims, operands)
    if fused:
        cot_across, squares = lax.optimization_barrier((cot_across, squares))
        pair = jnp.stack([own_cot, cot_across])
        cot_all = jnp.concatenate([pair, swap(pair, "fsdp", size, 1)], 0).reshape(total, width)
    grad_normed = contract_cols(cot_all, w_out)
    cross = jnp.sum(gated.astype(F32) * grad_normed, 1)
    stats = sum_tokens(jnp.stack([squares[:, 0], cross]), "fsdp", size)
    root = lax.rsqrt(stats[0] / full_inner + EPS)
    pull = root * root * root * stats[1] / full_inner

    normed_low = (gated.astype(F32) * root[:, None]).astype(BF16)
    if fused:
        grad_out = contract_rows(normed_low, cot_all).astype(BF16)
        head_rows, grad_out = lax.optimization_barrier((head_rows, grad_out))
        operands = operands[:5] + (head_rows,) + operands[6:]
        own_out = lax.psum_scatter(grad_out, "replica", scatter_dimension=0, tiled=True)
    gp, grad_conv, grad_chan, grad_head = mix_backward(
        dims, operands, jnp.stack([root, pull], 1), grad_normed
    )
    if fused:
        own_out, grad_head = lax.optimization_barrier((own_out, grad_head))
        grad_w_out = lax.all_gather(own_out, "replica", axis=0, tiled=True).astype(F32)
    own_wide = own_x.astype(F32)
    own_root = normalise(own_x)

    conv_full = jnp.zeros((8, conv_width), F32)
    conv_full = lax.dynamic_update_slice(conv_full, grad_conv[:, inner:], (0, full_inner))
    conv_full = lax.dynamic_update_slice(conv_full, grad_conv[:, :inner], (0, me * inner))
    conv_full = conv_full[: taps + 1].reshape(-1)
    skip_grad = grad_chan[0].reshape(local_heads, channel).sum(1)
    own_small = jnp.concatenate(
        [grad_head[0, :local_heads], grad_head[1, :local_heads], skip_grad, grad_chan[1]]
    )

    if fused:
        near = total // 2

        def halves(product):
            sent = swap(product(near, total).astype(BF16), "fsdp", size, 1)
            kept = product(0, near) + sent.astype(F32)
            return kept.astype(BF16).reshape(2, own_rows, width)

        tok_out = halves(lambda start, stop: jnp.dot(gated[start:stop], w_out, preferred_element_type=F32))
        spread = lax.dynamic_update_slice(jnp.zeros((size, own_small.shape[0]), F32), own_small[None], (me, 0))
        norm_row = -(-conv_full.shape[0] // LANES)
        conv_padded = jnp.pad(conv_full, (0, norm_row * LANES - conv_full.shape[0]))
        vector = jnp.concatenate([conv_padded, jnp.zeros((width,), F32), spread.reshape(-1)])
        vector = jnp.pad(vector, (0, -vector.shape[0] % (8 * LANES))).reshape(-1, LANES)
        sum_in, sum_shared, got_out, own_grad, got_grad, vector, _, _ = reduce_gradients(
            size, depth, inner, common, norm_row, gp, scaled_low, w_cols, tok_out, vector
        )
        grad_w_in = jnp.concatenate([sum_in.reshape(2 * full_inner, depth), sum_shared], 0).astype(F32).T
        out_sum = tok_out[0].astype(F32) + got_out.astype(F32)
        grad_scaled = own_grad.astype(F32) + got_grad.astype(F32)
        vector = vector.reshape(-1)
        conv_full = vector[: conv_full.shape[0]]
        start = norm_row * LANES
        grad_norm = vector[start : start + width] / full_norm[0]
        start = start + width
        own_small = lax.dynamic_slice(vector, (start + me * own_small.shape[0],), own_small.shape)
    else:
        out_part = jnp.dot(gated, w_out, preferred_element_type=F32).astype(BF16)
        out_sum = scatter_relative(out_part.reshape(size, own_rows, width), "fsdp", size)
        grad_w_in, grad_w_out = small_pieces(
            size, copies, depth, inner, columns, me, replica, scaled_low, gp, normed_low, cot_all
        )
        scaled_part = jnp.dot(gp, w_cols, preferred_element_type=F32).astype(BF16)
        grad_scaled = scatter_relative(scaled_part.reshape(size, own_rows, width), "fsdp", size)
        grad_norm = jnp.sum(grad_scaled * own_wide * own_root, 0)
        conv_full, grad_norm = lax.psum((conv_full, grad_norm), ("replica", "fsdp"))
        own_small = lax.psum(own_small, "replica")

    block_out = (own_wide + root[:own_rows, None] * out_sum).astype(BF16).reshape(hidden_in.shape)
    gained = grad_scaled * full_norm
    inner_mean = jnp.mean(gained * own_wide, -1, keepdims=True)
    grad_in = own_cot.astype(F32) + own_root * gained - own_wide * (own_root * own_root * own_root * inner_mean)
    grad_in = grad_in.reshape(hidden_in.shape)
    conv_full = lax.dynamic_slice(conv_full.reshape(taps + 1, conv_width), (0, me * own_conv), (taps + 1, own_conv))
    grad_norm = lax.dynamic_slice(grad_norm, (me * depth,), (depth,))
    return (
        block_out,
        grad_in,
        grad_norm,
        grad_w_in,
        conv_full[:taps],
        conv_full[taps],
        own_small[:local_heads],
        own_small[local_heads : 2 * local_heads],
        own_small[2 * local_heads : 3 * local_heads],
        own_small[3 * local_heads :],
        grad_w_out,
    )


def solution(mesh):
    rows = ("replica", "fsdp")
    placed = (
        P(None, rows, None, None),
        P(None, rows, None),
        P(None, rows, None, None),
        P("fsdp"),
        P("fsdp", None),
        P(None, "fsdp"),
        P("fsdp"),
        P("fsdp"),
        P("fsdp"),
        P("fsdp"),
        P("fsdp"),
        P("fsdp", None),
    )
    return jax.shard_map(
        functools.partial(on_device, mesh.shape["replica"], mesh.shape["fsdp"]),
        mesh=mesh,
        in_specs=placed,
        out_specs=(
            P(None, rows, None, None),
            P(None, rows, None, None),
            P("fsdp"),
            P("fsdp", None),
            P(None, "fsdp"),
            P("fsdp"),
            P("fsdp"),
            P("fsdp"),
            P("fsdp"),
            P("fsdp"),
            P("fsdp", None),
        ),
        check_vma=False,
    )
```

```python
import functools

import jax
import jax.numpy as jnp
from jax import lax
from jax.experimental import pallas as pl
from jax.experimental.pallas import tpu as pltpu
from jax.sharding import PartitionSpec as P

EPS = 1e-05
HIGHEST = lax.Precision.HIGHEST
LANES = 128
F32 = jnp.float32
BF16 = jnp.bfloat16
LOG2E = 1.4426950408889634
VMEM_LIMIT = 60 << 20


def contract_rows(left, right, precision=None):
    return lax.dot_general(
        left, right, (((0,), (0,)), ((), ())), precision=precision, preferred_element_type=F32
    )


def contract_cols(left, right, precision=None):
    return lax.dot_general(
        left, right, (((1,), (1,)), ((), ())), precision=precision, preferred_element_type=F32
    )


def sigmoid(v):
    return 0.5 * jnp.tanh(0.5 * v) + 0.5


def convolve(conv_input, taps, bias, mask_refs):
    total = bias + taps[0] * conv_input
    shifted = []
    for offset in range(1, len(taps)):
        prior = pltpu.roll(conv_input, offset, 0) * mask_refs[offset - 1]
        shifted.append(prior)
        total = total + taps[offset] * prior
    return total, shifted


def prepare(dims, own_ref, proj_ref, seg_col_ref, seg_row_ref, mask_ref, head_ref, cw_ref,
            mask_wide, visible_bias, step_wide, cum_wide, cum_rows, state_act, affinity):
    tokens, inner, state2, heads, local_heads, taps = dims
    for offset in range(taps - 1):
        mask_wide[offset] = jnp.broadcast_to(mask_ref[:, offset : offset + 1], (tokens, LANES))
    rows = lax.broadcasted_iota(jnp.int32, (tokens, tokens), 0)
    cols = lax.broadcasted_iota(jnp.int32, (tokens, tokens), 1)
    visible = (rows >= cols) & (seg_col_ref[...] == seg_row_ref[...])
    visible_bias[...] = jnp.where(visible, 0.0, -1e30)
    common = 2 * inner
    raw = proj_ref[:, common + state2 : common + state2 + heads]
    raw = jnp.concatenate([raw, jnp.zeros((tokens, LANES - heads), F32)], 1)
    raw = pltpu.roll(raw, LANES - own_ref[0] * local_heads, 1)
    raw = raw + head_ref[0:1, :]
    step = jnp.maximum(raw, 0.0) + jnp.log1p(jnp.exp(-jnp.abs(raw)))
    log_decay = head_ref[1:2, :] * step
    lower = jnp.where(rows >= cols, 1.0, 0.0).astype(F32)
    cumulative = jnp.dot(lower, log_decay, precision=HIGHEST, preferred_element_type=F32)
    scaled_cum = cumulative * LOG2E
    flipped = scaled_cum.T
    lane = lax.broadcasted_iota(jnp.int32, (tokens, LANES), 1)
    for head in range(local_heads):
        cum_wide[head] = jnp.broadcast_to(scaled_cum[:, head : head + 1], (tokens, LANES))
        cum_rows[head] = flipped[head : head + 1, :]
    for pair in range(local_heads // 2):
        step_wide[pair] = jnp.where(
            lane < LANES // 2, step[:, 2 * pair : 2 * pair + 1], step[:, 2 * pair + 1 : 2 * pair + 2]
        )
    for part in range(state2 // LANES):
        at = inner + part * LANES
        conv, _ = convolve(
            proj_ref[:, common + part * LANES : common + (part + 1) * LANES],
            [cw_ref[j : j + 1, at : at + LANES] for j in range(taps)],
            cw_ref[taps : taps + 1, at : at + LANES],
            mask_wide,
        )
        state_act[part] = conv * sigmoid(conv)
    affinity[...] = contract_cols(state_act[1], state_act[0], HIGHEST)
    return raw, step, log_decay, rows, cols


def over_pairs(count, step, carry):
    group = 4 if count % 4 == 0 else 2

    def turn(index, carried):
        for inner in range(group):
            carried = step(index * group + inner, carried)
        return carried

    return lax.fori_loop(0, count // group, turn, carry)


def forward_kernel(dims, own_ref, proj_ref, seg_col_ref, seg_row_ref, mask_ref, head_ref, cw_ref, chan_ref,
                   gated_ref, square_ref, out_ref,
                   mask_wide, visible_bias, step_wide, cum_wide, cum_rows, state_act, affinity):
    tokens, inner, state2, heads, local_heads, taps = dims
    prepare(dims, own_ref, proj_ref, seg_col_ref, seg_row_ref, mask_ref, head_ref, cw_ref,
            mask_wide, visible_bias, step_wide, cum_wide, cum_rows, state_act, affinity)
    lane = lax.broadcasted_iota(jnp.int32, (tokens, LANES), 1)
    first = lane < LANES // 2
    blocks = tokens // LANES

    def pair_step(pair, squares):
        here = pl.ds(pl.multiple_of(pair * LANES, LANES), LANES)
        conv, _ = convolve(
            proj_ref[:, here], [cw_ref[j : j + 1, here] for j in range(taps)],
            cw_ref[taps : taps + 1, here], mask_wide,
        )
        values = conv * sigmoid(conv)
        weighted = values * step_wide[pair]
        out = chan_ref[0:1, here] * values
        parts = [out[b * LANES : (b + 1) * LANES] for b in range(blocks)]
        for which in range(2):
            head = 2 * pair + which
            mine = jnp.where(first == (which == 0), weighted, 0.0).astype(BF16)
            for tb in range(blocks):
                t_rows = slice(tb * LANES, (tb + 1) * LANES)
                pieces = []
                for sb in range(tb + 1):
                    s_cols = slice(sb * LANES, (sb + 1) * LANES)
                    distance = (cum_wide[head, t_rows, :] - cum_rows[head, :, s_cols]) + visible_bias[t_rows, s_cols]
                    pieces.append((affinity[t_rows, s_cols] * jnp.exp2(distance)).astype(BF16))
                weights = jnp.concatenate(pieces, 1) if tb > 0 else pieces[0]
                parts[tb] = parts[tb] + jnp.dot(
                    weights, mine[: (tb + 1) * LANES], preferred_element_type=F32
                )
        out = jnp.concatenate(parts, 0)
        out_ref[:, here] = out.astype(BF16)
        gate = proj_ref[:, pl.ds(pl.multiple_of(inner + pair * LANES, LANES), LANES)]
        gated = out * (gate * sigmoid(gate))
        gated_ref[:, here] = (gated * chan_ref[1:2, here]).astype(BF16)
        return squares + gated * gated

    squares = over_pairs(local_heads // 2, pair_step, jnp.zeros((tokens, LANES), F32))
    square_ref[...] = jnp.sum(squares, 1, keepdims=True)


def backward_kernel(dims, own_ref, proj_ref, seg_col_ref, seg_row_ref, mask_ref, head_ref, cw_ref, chan_ref,
                    stats_ref, gn_ref, out_ref,
                    gp_ref, grad_cw_ref, grad_chan_ref, grad_head_ref,
                    mask_wide, visible_bias, step_wide, cum_wide, cum_rows, state_act, affinity,
                    grad_affinity, row_sums, col_sums, wide_stats):
    tokens, inner, state2, heads, local_heads, taps = dims

    @pl.when(pl.program_id(0) == 0)
    def _():
        grad_cw_ref[...] = jnp.zeros_like(grad_cw_ref)
        grad_chan_ref[...] = jnp.zeros_like(grad_chan_ref)
        grad_head_ref[...] = jnp.zeros_like(grad_head_ref)

    raw, step, log_decay, rows, cols = prepare(
        dims, own_ref, proj_ref, seg_col_ref, seg_row_ref, mask_ref, head_ref, cw_ref,
        mask_wide, visible_bias, step_wide, cum_wide, cum_rows, state_act, affinity)
    grad_affinity[...] = jnp.zeros_like(grad_affinity)
    row_sums[...] = jnp.zeros_like(row_sums)
    col_sums[...] = jnp.zeros_like(col_sums)
    wide_stats[0] = jnp.broadcast_to(stats_ref[:, 0:1], (tokens, LANES))
    wide_stats[1] = jnp.broadcast_to(stats_ref[:, 1:2], (tokens, LANES))
    lane = lax.broadcasted_iota(jnp.int32, (tokens, LANES), 1)
    block_lane = lax.broadcasted_iota(jnp.int32, (LANES, LANES), 1)
    first = lane < LANES // 2
    blocks = tokens // LANES

    def conv_back(grad_conv, shifted, conv_input, here):
        grad_cw_ref[0:1, here] += jnp.sum(grad_conv * conv_input, 0, keepdims=True)
        grad_cw_ref[taps : taps + 1, here] += jnp.sum(grad_conv, 0, keepdims=True)
        back = cw_ref[0:1, here] * grad_conv
        for offset in range(1, taps):
            grad_cw_ref[offset : offset + 1, here] += jnp.sum(grad_conv * shifted[offset - 1], 0, keepdims=True)
            term = (cw_ref[offset : offset + 1, here] * grad_conv) * mask_wide[offset - 1]
            back = back + pltpu.roll(term, tokens - offset, 0)
        return back

    def pair_step(pair, carry):
        here = pl.ds(pl.multiple_of(pair * LANES, LANES), LANES)
        there = pl.ds(pl.multiple_of(inner + pair * LANES, LANES), LANES)
        conv_input = proj_ref[:, here]
        conv, shifted = convolve(
            conv_input, [cw_ref[j : j + 1, here] for j in range(taps)],
            cw_ref[taps : taps + 1, here], mask_wide,
        )
        conv_sig = sigmoid(conv)
        values = conv * conv_sig
        weighted = values * step_wide[pair]
        skip = chan_ref[0:1, here]
        halves = [jnp.where(first == (which == 0), weighted, 0.0).astype(BF16) for which in range(2)]
        out = out_ref[:, here].astype(F32)
        gate = proj_ref[:, there]
        gate_sig = sigmoid(gate)
        gate_silu = gate * gate_sig
        gated = out * gate_silu
        gn = gn_ref[:, here]
        gain = chan_ref[1:2, here]
        root = wide_stats[0]
        grad_chan_ref[1:2, here] += jnp.sum(gn * gated * root, 0, keepdims=True)
        grad_gated = root * (gn * gain) - gated * wide_stats[1]
        grad_out = grad_gated * gate_silu
        gp_ref[:, there] = (grad_gated * out * (gate_sig * (1.0 + gate * (1.0 - gate_sig)))).astype(BF16)
        grad_chan_ref[0:1, here] += jnp.sum(grad_out * values, 0, keepdims=True)
        back_parts = [jnp.zeros((LANES, LANES), F32) for _ in range(blocks)]
        for which in range(2):
            head = 2 * pair + which
            mine = jnp.where(first == (which == 0), grad_out, 0.0).astype(BF16)
            for tb in range(blocks):
                t_rows = slice(tb * LANES, (tb + 1) * LANES)
                sums = None
                for sb in range(tb + 1):
                    s_cols = slice(sb * LANES, (sb + 1) * LANES)
                    distance = (cum_wide[head, t_rows, :] - cum_rows[head, :, s_cols]) + visible_bias[t_rows, s_cols]
                    decay = jnp.exp2(distance)
                    weights = affinity[t_rows, s_cols] * decay
                    cross = contract_cols(mine[t_rows], halves[which][s_cols])
                    grad_affinity[t_rows, s_cols] += cross * decay
                    energy = cross * weights
                    col_sums[head, :, s_cols] += jnp.sum(energy, 0, keepdims=True)
                    sums = energy if sums is None else sums + energy
                    back_parts[sb] = back_parts[sb] + contract_rows(weights.astype(BF16), mine[t_rows])
                row_sums[t_rows, :] += jnp.where(
                    block_lane == head, jnp.sum(sums, 1, keepdims=True), 0.0
                )
        grad_values = jnp.concatenate(back_parts, 0) * step_wide[pair] + skip * grad_out
        grad_conv = grad_values * (conv_sig * (1.0 + conv * (1.0 - conv_sig)))
        gp_ref[:, here] = conv_back(grad_conv, shifted, conv_input, here).astype(BF16)
        return carry

    over_pairs(local_heads // 2, pair_step, 0)

    common = 2 * inner
    grad_states = [
        contract_rows(grad_affinity[...], state_act[1], HIGHEST),
        jnp.dot(grad_affinity[...], state_act[0], precision=HIGHEST, preferred_element_type=F32),
    ]
    for part in range(state2 // LANES):
        at = slice(inner + part * LANES, inner + (part + 1) * LANES)
        spot = slice(common + part * LANES, common + (part + 1) * LANES)
        conv_input = proj_ref[:, spot]
        conv, shifted = convolve(
            conv_input, [cw_ref[j : j + 1, at] for j in range(taps)], cw_ref[taps : taps + 1, at], mask_wide
        )
        conv_sig = sigmoid(conv)
        grad_conv = grad_states[part] * (conv_sig * (1.0 + conv * (1.0 - conv_sig)))
        gp_ref[:, spot] = conv_back(grad_conv, shifted, conv_input, at).astype(BF16)

    col_rows = [col_sums[head] for head in range(local_heads)]
    col_rows.append(jnp.zeros((LANES - local_heads, tokens), F32))
    col_energy = jnp.concatenate(col_rows, 0).T
    upper = jnp.where(cols >= rows, 1.0, 0.0).astype(F32)
    grad_decay = jnp.dot(upper, row_sums[...] - col_energy, precision=HIGHEST, preferred_element_type=F32)
    step_sig = sigmoid(raw)
    ratio = jnp.where(raw < -20.0, 1.0, step_sig / jnp.maximum(step, 1e-30))
    grad_raw = col_energy * ratio + (head_ref[1:2, :] * grad_decay) * step_sig
    grad_head_ref[0:1, :] += jnp.sum(grad_raw, 0, keepdims=True)
    grad_head_ref[1:2, :] += jnp.sum(grad_decay * log_decay, 0, keepdims=True)
    placed = pltpu.roll(grad_raw, own_ref[0] * local_heads, 1)
    gp_ref[:, common + state2 : common + state2 + heads] = placed[:, :heads].astype(BF16)


def mixer_specs(dims, width):
    tokens, inner, state2, heads, local_heads, taps = dims
    fixed = lambda shape: pl.BlockSpec(shape, lambda s: (0,) * len(shape))
    in_specs = [
        pl.BlockSpec(memory_space=pltpu.SMEM),
        pl.BlockSpec((tokens, width), lambda s: (s, 0)),
        pl.BlockSpec((None, tokens, 1), lambda s: (s, 0, 0)),
        pl.BlockSpec((None, 1, tokens), lambda s: (s, 0, 0)),
        pl.BlockSpec((None, tokens, 8), lambda s: (s, 0, 0)),
        fixed((8, LANES)),
        fixed((8, inner + state2)),
        fixed((8, inner)),
    ]
    scratch = [
        pltpu.VMEM((taps - 1, tokens, LANES), F32),
        pltpu.VMEM((tokens, tokens), F32),
        pltpu.VMEM((local_heads // 2, tokens, LANES), F32),
        pltpu.VMEM((local_heads, tokens, LANES), F32),
        pltpu.VMEM((local_heads, 1, tokens), F32),
        pltpu.VMEM((state2 // LANES, tokens, LANES), F32),
        pltpu.VMEM((tokens, tokens), F32),
    ]
    return in_specs, scratch


def mix_forward(dims, operands):
    tokens, inner, state2, heads, local_heads, taps = dims
    total, width = operands[1].shape
    in_specs, scratch = mixer_specs(dims, width)
    return pl.pallas_call(
        functools.partial(forward_kernel, dims),
        grid=(total // tokens,),
        in_specs=in_specs,
        out_specs=[
            pl.BlockSpec((tokens, inner), lambda s: (s, 0)),
            pl.BlockSpec((tokens, 1), lambda s: (s, 0)),
            pl.BlockSpec((tokens, inner), lambda s: (s, 0)),
        ],
        out_shape=[
            jax.ShapeDtypeStruct((total, inner), BF16),
            jax.ShapeDtypeStruct((total, 1), F32),
            jax.ShapeDtypeStruct((total, inner), BF16),
        ],
        scratch_shapes=scratch,
        compiler_params=pltpu.CompilerParams(vmem_limit_bytes=VMEM_LIMIT),
        cost_estimate=pl.CostEstimate(
            flops=total * local_heads * tokens * 4 * 64,
            bytes_accessed=total * width * 4,
            transcendentals=total * local_heads * tokens,
        ),
        name="mix_forward",
    )(*operands)


def mix_backward(dims, operands, stats, grad_normed, scan_out):
    tokens, inner, state2, heads, local_heads, taps = dims
    total, width = operands[1].shape
    in_specs, scratch = mixer_specs(dims, width)
    fixed = lambda shape: pl.BlockSpec(shape, lambda s: (0,) * len(shape))
    return pl.pallas_call(
        functools.partial(backward_kernel, dims),
        grid=(total // tokens,),
        in_specs=in_specs + [
            pl.BlockSpec((tokens, 2), lambda s: (s, 0)),
            pl.BlockSpec((tokens, inner), lambda s: (s, 0)),
            pl.BlockSpec((tokens, inner), lambda s: (s, 0)),
        ],
        out_specs=[
            pl.BlockSpec((tokens, width), lambda s: (s, 0)),
            fixed((8, inner + state2)),
            fixed((8, inner)),
            fixed((8, LANES)),
        ],
        out_shape=[
            jax.ShapeDtypeStruct((total, width), BF16),
            jax.ShapeDtypeStruct((8, inner + state2), F32),
            jax.ShapeDtypeStruct((8, inner), F32),
            jax.ShapeDtypeStruct((8, LANES), F32),
        ],
        scratch_shapes=scratch + [
            pltpu.VMEM((tokens, tokens), F32),
            pltpu.VMEM((tokens, LANES), F32),
            pltpu.VMEM((local_heads, 1, tokens), F32),
            pltpu.VMEM((2, tokens, LANES), F32),
        ],
        compiler_params=pltpu.CompilerParams(vmem_limit_bytes=VMEM_LIMIT),
        cost_estimate=pl.CostEstimate(
            flops=total * local_heads * tokens * 12 * 64,
            bytes_accessed=total * width * 6,
            transcendentals=2 * total * local_heads * tokens,
        ),
        name="mix_backward",
    )(*operands, stats, grad_normed, scan_out)


def norm_kernel(x_ref, gain_ref, scaled_ref):
    wide = x_ref[...].astype(F32)
    root = lax.rsqrt(jnp.mean(wide * wide, 1, keepdims=True) + EPS)
    scaled_ref[...] = (wide * root * gain_ref[...]).astype(BF16)


def norm_rows(inputs, gain):
    rows, width = inputs.shape
    block = pl.BlockSpec((256, width), lambda s: (s, 0))
    return pl.pallas_call(
        norm_kernel,
        grid=(rows // 256,),
        in_specs=[block, pl.BlockSpec((1, width), lambda s: (0, 0))],
        out_specs=block,
        out_shape=jax.ShapeDtypeStruct(inputs.shape, BF16),
        compiler_params=pltpu.CompilerParams(vmem_limit_bytes=VMEM_LIMIT),
        cost_estimate=pl.CostEstimate(flops=4 * rows * width, bytes_accessed=4 * rows * width, transcendentals=rows),
        name="norm_rows",
    )(inputs, gain)


def swap(array, axis, size, bit):
    return lax.ppermute(array, axis, [(i, i ^ bit) for i in range(size)])


def axis_bits(size):
    bits = []
    bit = 1
    while bit < size:
        bits.append(bit)
        bit *= 2
    return bits


def gather_relative(array, axis, size):
    held = array[None]
    for bit in reversed(axis_bits(size)):
        held = jnp.concatenate([held, swap(held, axis, size, bit)], 0)
    return held


def scatter_relative(array, axis, size):
    total = array
    for bit in axis_bits(size):
        half = total.shape[0] // 2
        received = swap(total[half:].astype(BF16), axis, size, bit)
        total = total[:half].astype(F32) + received.astype(F32)
    return total[0]


def sum_tokens(array, axis, size):
    kinds, tokens = array.shape
    for bit in axis_bits(size):
        stride = tokens // (2 * bit)
        received = swap(array, axis, size, bit).reshape(kinds, bit, 2, stride)
        array = array + received[:, :, ::-1].reshape(kinds, tokens)
    return array


def halve_sum(array, order, replica, size):
    total = array
    for bit in order:
        blocks, rows, columns = total.shape
        mine = (replica // bit) % 2
        halves = total.reshape(blocks, 2, rows // 2, columns)
        kept = lax.dynamic_index_in_dim(halves, mine, 1, keepdims=False)
        sent = lax.dynamic_index_in_dim(halves, 1 - mine, 1, keepdims=False)
        received = swap(sent.astype(BF16), "replica", size, bit)
        total = kept + received.astype(F32)
    return total


def double_gather(array, order, replica, size):
    held = array
    for bit in reversed(order):
        received = swap(held, "replica", size, bit)
        upper = (replica // bit) % 2 == 1
        held = jnp.where(
            upper,
            jnp.concatenate([received, held], 1),
            jnp.concatenate([held, received], 1),
        )
    return held


def flip(index, bit):
    return index + bit * (1 - 2 * ((index // bit) % 2))


MESH = pl.DeviceIdType.MESH


def greet(peers):
    barrier = pltpu.get_barrier_semaphore()
    for peer in peers:
        pl.semaphore_signal(barrier, inc=1, device_id=peer, device_id_type=MESH)
    pl.semaphore_wait(barrier, len(peers))


def copy_peers(me):
    return [flip(me, 1), flip(me, 2), flip(flip(me, 1), 2)]


def gather_kernel(full_inner, inner, x_ref, seg_ref, small_ref, w_ref,
                  scaled_ref, seg_all_ref, small_all_ref, cols_ref,
                  x_all_ref, scaled, gain, cols_held, send_sems, recv_sems, local_sems, store_sems, norm_sems):
    me = lax.axis_index("fsdp")
    replica = lax.axis_index("replica")
    depth, common = w_ref.shape[1], w_ref.shape[0] - 2 * full_inner
    peers = [(replica, peer) for peer in copy_peers(me)]
    beside, above = (flip(replica, 1), me), (flip(replica, 2), me)
    greet(peers + [beside, above])
    number = [0]
    started = []

    def send(from_ref, to_ref, device):
        slot = number[0]
        number[0] += 1
        copy = pltpu.make_async_remote_copy(
            src_ref=from_ref, dst_ref=to_ref, send_sem=send_sems.at[slot], recv_sem=recv_sems.at[slot],
            device_id=device, device_id_type=MESH,
        )
        copy.start()
        started.append(copy)
        return copy

    parts = [(0, inner), (inner, inner), (2 * inner, common)]

    def targets(owner, first, count):
        lanes = pl.ds(pl.multiple_of(owner * depth, depth), depth)
        return [
            cols_ref.at[pl.ds(pl.multiple_of(base + first * (length // 4), 16), count * (length // 4)), lanes]
            for base, length in parts
        ]

    def sources(device, first, count):
        bases = [full_inner + device * inner, device * inner, 2 * full_inner]
        return [
            w_ref.at[pl.ds(pl.multiple_of(base + first * (length // 4), 16), count * (length // 4))]
            for base, (_, length) in zip(bases, parts)
        ]

    def send_parts(from_refs, to_refs, device):
        return [send(source, target, device) for source, target in zip(from_refs, to_refs)]

    spot = replica % 4
    smalls = [send(small_ref, small_all_ref.at[me], peer) for peer in peers]
    smalls += [send(seg_ref, seg_all_ref.at[slot], peer) for peer, slot in zip(peers, (2, 1, 3))]
    across = [send_parts(sources(peers[which][1], spot, 1), targets(me, spot, 1), peers[which]) for which in (1, 2)]
    x_y = send(x_ref, x_all_ref.at[1], peers[1])
    near = send_parts(sources(peers[0][1], 0, 4), targets(me, 0, 4), peers[0])
    x_near = send(x_ref, x_all_ref.at[2], peers[0])
    held = [cols_held.at[pl.ds(base, length)] for base, length in parts]
    own = list(zip(sources(me, 0, 4), held, targets(me, 0, 4)))
    loads = [pltpu.make_async_copy(source, held, local_sems.at[i]) for i, (source, held, _) in enumerate(own)]
    stores = [pltpu.make_async_copy(held, target, store_sems.at[i]) for i, (_, held, target) in enumerate(own)]
    x_own = pltpu.make_async_copy(x_ref, x_all_ref.at[0], local_sems.at[3])
    small_own = pltpu.make_async_copy(small_ref, small_all_ref.at[me], local_sems.at[4])
    stores.append(pltpu.make_async_copy(seg_ref, seg_all_ref.at[0], local_sems.at[5]))
    for copy in loads + [x_own, small_own, stores[-1]]:
        copy.start()
    for load, store in zip(loads, stores):
        load.wait()
        store.start()

    rows_at_once = 128
    block_rows, width = scaled.shape[1:]
    tiles_of_owner = depth // LANES

    def normalise(block):
        def step(piece, carry):
            rows = pl.ds(pl.multiple_of(piece * rows_at_once, rows_at_once), rows_at_once)
            wide = x_all_ref[block, rows, :].astype(F32)
            root = lax.rsqrt(jnp.mean(wide * wide, 1, keepdims=True) + EPS)
            scaled[block, rows, :] = (wide * root * gain[...]).astype(BF16)
            return carry

        lax.fori_loop(0, block_rows // rows_at_once, step, 0)
        store = pltpu.make_async_copy(
            scaled.at[block], scaled_ref.at[pl.ds(block * block_rows, block_rows)], norm_sems.at[block]
        )
        store.start()
        stores.append(store)

    small_own.wait()
    for copy in smalls:
        copy.wait_recv()
    for tile in range(width // LANES):
        gain[:, tile * LANES : (tile + 1) * LANES] = small_all_ref[
            tile // tiles_of_owner, tile % tiles_of_owner : tile % tiles_of_owner + 1, :
        ]
    x_own.wait()
    normalise(0)

    def relay(which, first, count, device):
        refs = targets(peers[which][1], first, count)
        return send_parts(refs, refs, device)

    for copy in across[0]:
        copy.wait_recv()
    first_beside = relay(1, spot, 1, beside)
    for copy in across[1]:
        copy.wait_recv()
    first_above = relay(2, spot, 1, above)
    for copy in first_beside:
        copy.wait_recv()
    last = relay(1, (spot // 2) * 2, 2, above)
    for copy in first_above:
        copy.wait_recv()
    last += relay(2, spot, 1, beside)
    last += relay(2, flip(spot, 2), 1, beside)
    x_near.wait_recv()
    normalise(2)
    x_y.wait_recv()
    x_last = send(x_all_ref.at[1], x_all_ref.at[3], peers[0])
    normalise(1)
    x_last.wait_recv()
    normalise(3)
    for copy in last + near:
        copy.wait_recv()
    for copy in stores:
        copy.wait()
    for copy in started:
        copy.wait_send()


GATHER_COPIES = 34


def gather_inputs(size, inner, x, segments, small, w_flipped):
    full, depth = w_flipped.shape
    full_inner = inner * size
    columns = 2 * inner + full - 2 * full_inner
    anywhere = pl.BlockSpec(memory_space=pltpu.HBM)
    return pl.pallas_call(
        functools.partial(gather_kernel, full_inner, inner),
        in_specs=[anywhere] * 4,
        out_specs=[anywhere] * 2 + [pl.BlockSpec(memory_space=pltpu.VMEM), anywhere],
        out_shape=[
            jax.ShapeDtypeStruct((size * x.shape[0], x.shape[1]), BF16),
            jax.ShapeDtypeStruct((size,) + segments.shape, jnp.int32),
            jax.ShapeDtypeStruct((size,) + small.shape, F32),
            jax.ShapeDtypeStruct((columns, size * depth), BF16),
        ],
        scratch_shapes=[
            pltpu.VMEM((size,) + x.shape, BF16),
            pltpu.VMEM((size,) + x.shape, BF16),
            pltpu.VMEM((1, x.shape[1]), F32),
            pltpu.VMEM((columns, depth), BF16),
            pltpu.SemaphoreType.DMA((GATHER_COPIES,)),
            pltpu.SemaphoreType.DMA((GATHER_COPIES,)),
            pltpu.SemaphoreType.DMA((6,)),
            pltpu.SemaphoreType.DMA((3,)),
            pltpu.SemaphoreType.DMA((4,)),
        ],
        compiler_params=pltpu.CompilerParams(
            collective_id=1, has_side_effects=True, vmem_limit_bytes=VMEM_LIMIT
        ),
        cost_estimate=pl.CostEstimate(flops=0, bytes_accessed=200 << 20, transcendentals=0),
        name="gather_inputs",
    )(x, segments, small, w_flipped)


PARTS = {
    "side": {"got": 2, "lift": 2, "sent": 4, "swapped": 4, "final": 4},
    "lift": {"got": 1, "sent": 2, "swapped": 2, "sent_side": 4, "got_side": 4, "final": 4},
}
SLOTS = 9
IN_ROWS = (64,) * 32
SHARED_AT = 4
COLUMN_BLOCK = 256
ROW_BLOCK = 256
LANE_TILE = 1024
PER_TURN = 3
TOKEN_PIECES = 8


def reduce_chunks(inner, common):
    pieces = []
    start = 0
    for rows in IN_ROWS:
        pieces.append(("in", start, rows))
        start += rows
    pieces.insert(SHARED_AT, ("shared", 0, common))
    counts = {}
    placed = []
    for number, (kind, start, rows) in enumerate(pieces):
        order = "lift" if number % 4 == 2 else "side"
        key = (kind == "shared", rows, order)
        where = counts.get(key, 0)
        counts[key] = where + 1
        placed.append((kind, start, rows, order, where))
    return placed, counts


def reduce_kernel(plan, gp_ref, scaled_ref, cols_ref, tok_out_ref, small_ref,
                  sum_in_ref, sum_shared_ref, got_out_ref, own_grad_ref, got_grad_ref, small_sum_ref,
                  far_land_ref, across_ref, *scratch):
    chunks, counts, inner, depth, common, norm_row = plan
    groups = {}
    position = 0
    for key in counts:
        names = list(PARTS[key[2]])
        groups[key] = dict(zip(names, scratch[position : position + len(names)]))
        position += len(names)
    (shared_in, shared_sum, small_got, scaled, cols, grads, gp_cols, gp_flipped, gp_rows, tiles, far_tile, norm_sum,
     send_sems, recv_sems, local_sems, tok_send, tok_recv,
     small_send, small_recv, shared_send, shared_recv, far_send, far_recv, load_sems, store_sems) = scratch[position:]
    whole_loads = [
        pltpu.make_async_copy(scaled_ref, scaled, load_sems.at[0]),
        pltpu.make_async_copy(cols_ref, cols, load_sems.at[1]),
    ]
    for copy in whole_loads:
        copy.start()
    loaded = [False, False]

    def need(which):
        if not loaded[which]:
            whole_loads[which].wait()
            loaded[which] = True

    column_blocks = [(start, COLUMN_BLOCK) for start in range(0, 2 * inner, COLUMN_BLOCK)]
    column_blocks.insert(1, (2 * inner, common))
    width = scaled.shape[1]
    rows_of_block = tiles.shape[1]
    lane_tiles = width // LANE_TILE
    column_loads = []
    columns_done = []

    def load_columns(number):
        if number < len(column_blocks):
            start, count = column_blocks[number]
            copy = pltpu.make_async_copy(
                gp_ref.at[:, pl.ds(start, count)], gp_cols.at[:, pl.ds(0, count)], load_sems.at[2]
            )
            copy.start()
            column_loads.append(copy)

    def next_columns():
        number = len(columns_done)
        if number == len(column_blocks):
            return
        start, count = column_blocks[number]
        need(0)
        column_loads[number].wait()
        gp_flipped[pl.ds(0, count), :] = gp_cols[:, pl.ds(0, count)].T
        load_columns(number + 1)

        def lanes_step(tile, carry):
            lanes = pl.ds(pl.multiple_of(tile * LANE_TILE, LANE_TILE), LANE_TILE)
            grads[pl.ds(start, count), lanes] = jnp.dot(
                gp_flipped[pl.ds(0, count), :], scaled[:, lanes], preferred_element_type=F32
            ).astype(BF16)
            return carry

        lax.fori_loop(0, lane_tiles, lanes_step, 0)
        columns_done.append(start)

    def ensure_columns(start):
        while start not in columns_done:
            next_columns()

    load_columns(0)
    me = lax.axis_index("fsdp")
    replica = lax.axis_index("replica")
    up = replica // 2
    inside = (up == 1) | (up == 2)
    outside = (up == 0) | (up == 3)
    half = up // 2
    aside = replica % 2
    beside = (flip(replica, 1), me)
    partner = (flip(replica, 2), me)
    middle = (flip(flip(replica, 2), 4), me)
    peers = [(replica, peer) for peer in copy_peers(me)]
    greet(peers + [beside, partner, middle])

    def remote(from_ref, to_ref, device, sends, recvs):
        return pltpu.make_async_remote_copy(
            src_ref=from_ref, dst_ref=to_ref, send_sem=sends, recv_sem=recvs, device_id=device, device_id_type=MESH
        )

    def lanes_of(device):
        return pl.ds(pl.multiple_of(device * depth, depth), depth)

    def activations():
        rows = got_out_ref.shape[0] // TOKEN_PIECES
        copies = []
        for piece in range(TOKEN_PIECES):
            at = pl.ds(piece * rows, rows)
            copy = remote(tok_out_ref.at[1, at], got_out_ref.at[at], peers[1], tok_send.at[0, piece], tok_recv.at[0, piece])
            copy.start()
            copies.append(copy)
            yield
        for piece in range(TOKEN_PIECES):
            at = pl.ds(piece * rows, rows)
            copy = remote(across_ref.at[at], got_grad_ref.at[at], peers[1], tok_send.at[1, piece], tok_recv.at[1, piece])
            copy.start()
            copies.append(copy)
            yield
        for copy in copies:
            copy.wait()

    def row_products():
        half_blocks = gp_ref.shape[0] // (2 * rows_of_block)
        quarter_blocks = half_blocks // 2
        later = list(range(quarter_blocks, half_blocks))
        sooner = list(range(quarter_blocks))
        order = [(True, i) for i in later] + [(False, i) for i in later]
        order += [(True, i) for i in sooner] + [(False, i) for i in sooner]
        norm_sum[...] = jnp.zeros_like(norm_sum)
        row_loads = []

        def load_rows(number):
            if number < len(order):
                far, block = order[number]
                at = (half_blocks + block if far else block) * rows_of_block
                copy = pltpu.make_async_copy(gp_ref.at[pl.ds(at, rows_of_block)], gp_rows, load_sems.at[3])
                copy.start()
                row_loads.append((copy, at))

        load_rows(0)
        need(0)
        need(1)
        arrivals = {}
        busy = [None, None]
        for number, (far, block) in enumerate(order):
            slot = number % 2
            if busy[slot] is not None:
                busy[slot]()
            if not far:
                arrivals[block].wait_recv()
                load = pltpu.make_async_copy(far_land_ref.at[block], far_tile, load_sems.at[4])
                load.start()
                load.wait()
            copy, at = row_loads[number]
            copy.wait()

            def lanes_step(tile, carry):
                lanes = pl.ds(pl.multiple_of(tile * LANE_TILE, LANE_TILE), LANE_TILE)
                part = jnp.dot(gp_rows[...], cols[:, lanes], preferred_element_type=F32)
                norm_sum[:, lanes] += jnp.sum(
                    part * scaled[pl.ds(at, rows_of_block), lanes].astype(F32), 0, keepdims=True
                )
                if not far:
                    part = part + far_tile[:, lanes].astype(F32)
                tiles[slot, :, lanes] = part.astype(BF16)
                return carry

            lax.fori_loop(0, lane_tiles, lanes_step, 0)
            load_rows(number + 1)
            if far:
                sent = remote(tiles.at[slot], far_land_ref.at[block], peers[0], far_send.at[block], far_recv.at[block])
                sent.start()
                arrivals[block] = sent
                busy[slot] = sent.wait_send
            else:
                target = own_grad_ref if block < quarter_blocks else across_ref
                place = pl.ds((block % quarter_blocks) * rows_of_block, rows_of_block)
                store = pltpu.make_async_copy(tiles.at[slot], target.at[place], store_sems.at[block])
                store.start()
                busy[slot] = store.wait
            yield
        for wait in busy:
            wait()
        for tile in range(width // LANES):
            small_sum_ref[norm_row + tile : norm_row + tile + 1, :] = norm_sum[:, tile * LANES : (tile + 1) * LANES]

    def smalls():
        small_sum_ref[...] = small_ref[...]
        yield from row_products()
        for level, peer in enumerate([peers[0], peers[1], beside, partner, middle]):
            copy = remote(small_sum_ref, small_got.at[level], peer, small_send.at[level], small_recv.at[level])
            copy.start()
            yield
            copy.wait()
            small_sum_ref[...] += small_got[level]

    def run(number, kind, start, rows, order, where):
        held = {name: ref.at[where] for name, ref in groups[kind == "shared", rows, order].items()}
        if kind == "in":
            group = 0 if start >= inner else 4
            local_start = start % inner
            ensure_columns(start // COLUMN_BLOCK * COLUMN_BLOCK)
            base_ref, base_start = grads, start
            place = lambda at, count: sum_in_ref.at[pl.ds(group, 4), pl.ds(pl.multiple_of(local_start + at, 16), count)]
        else:
            ensure_columns(2 * inner)
            base_ref, base_start = shared_sum, 0
            place = lambda at, count: sum_shared_ref.at[pl.ds(at, count)]
            copies = []
            for offset in range(3):
                copy = remote(
                    grads.at[pl.ds(2 * inner, rows), lanes_of(peers[offset][1])],
                    shared_in.at[offset], peers[offset], shared_send.at[offset], shared_recv.at[offset],
                )
                copy.start()
                copies.append(copy)
            yield
            total = grads[pl.ds(2 * inner, rows), lanes_of(me)].astype(F32)
            for offset in range(3):
                copies[offset].wait_recv()
                total = total + shared_in[offset].astype(F32)
            shared_sum[...] = total.astype(BF16)

        def source(at, count):
            return base_ref.at[pl.ds(pl.multiple_of(base_start + at, 16), count)]

        def link(from_ref, to_ref, device, slot):
            return remote(from_ref, to_ref, device, send_sems.at[number, slot], recv_sems.at[number, slot])

        def added(names_at, at, count):
            total = source(at, count)[...].astype(F32)
            for name, base in names_at:
                local = pl.multiple_of(at - base, count)
                total = total + held[name][pl.ds(local, count), :].astype(F32)
            return total

        two, four = rows // 2, rows // 4
        if order == "side":
            mine, other = pl.multiple_of(aside * two, two), pl.multiple_of((1 - aside) * two, two)
            low, high = pl.multiple_of(mine + half * four, four), pl.multiple_of(mine + (1 - half) * four, four)
            side = link(source(other, two), held["got"], beside, 0)
            side.start()
            yield
            side.wait_recv()
            lift = link(held["lift"], held["lift"], partner, 1)

            @pl.when(outside)
            def _():
                held["lift"][...] = added([("got", mine)], mine, two).astype(BF16)
                lift.start()

            yield
            bases = [("got", mine), ("lift", mine)]
            across = link(held["sent"], held["swapped"], middle, 2)

            @pl.when(inside)
            def _():
                lift.wait_recv()
                held["sent"][...] = added(bases, high, four).astype(BF16)
                across.start()

            yield
            bases = bases + [("swapped", low)]
        else:
            mine, other = pl.multiple_of(half * two, two), pl.multiple_of((1 - half) * two, two)
            low, high = pl.multiple_of(mine + aside * four, four), pl.multiple_of(mine + (1 - aside) * four, four)
            lift = link(source(0, rows), held["got"], partner, 1)

            @pl.when(outside)
            def _():
                lift.start()

            yield
            bases = [("got", 0)]
            across = link(held["sent"], held["swapped"], middle, 2)

            @pl.when(inside)
            def _():
                lift.wait_recv()
                held["sent"][...] = added(bases, other, two).astype(BF16)
                across.start()

            yield
            bases = bases + [("swapped", mine)]
            side = link(held["sent_side"], held["got_side"], beside, 0)

            @pl.when(inside)
            def _():
                across.wait_recv()
                held["sent_side"][...] = added(bases, high, four).astype(BF16)
                side.start()

            yield
            bases = bases + [("got_side", low)]

        final = held["final"]
        trade = []
        if kind == "in":
            target = sum_in_ref.at[group + me, pl.ds(pl.multiple_of(local_start + low, 16), four)]
            trade = [
                link(final.at[:, lanes_of(peers[offset][1])], target, peers[offset], 3 + offset) for offset in range(3)
            ]
            own = pltpu.make_async_copy(final.at[:, lanes_of(me)], target, local_sems.at[number])
        else:
            own = pltpu.make_async_copy(final, place(low, four), local_sems.at[number])

        if order == "side":
            back = [
                link(place(low, four), place(low, four), middle, 6),
                link(place(mine, two), place(mine, two), partner, 7),
                link(place(mine, two), place(mine, two), beside, 8),
            ]
        else:
            back = [
                link(place(low, four), place(low, four), beside, 6),
                link(place(mine, two), place(mine, two), middle, 7),
                link(place(0, rows), place(0, rows), partner, 8),
            ]

        @pl.when(inside)
        def _():
            (across if order == "side" else side).wait_recv()
            final[...] = added(bases, low, four).astype(BF16)
            for copy in trade:
                copy.start()
            own.start()
            own.wait()
            for copy in trade:
                copy.wait_recv()
            back[0].start()

        yield

        @pl.when(inside)
        def _():
            back[0].wait_recv()
            back[1].start()
            if order == "side":
                back[2].start()

        yield
        if order == "side":

            @pl.when(outside)
            def _():
                back[1].wait_recv()
                back[2].start()

            yield
            back[2].wait_recv()
            side.wait_send()
            back[2].wait_send()

            @pl.when(outside)
            def _():
                lift.wait_send()

            @pl.when(inside)
            def _():
                across.wait_send()
                for copy in trade + back[:2]:
                    copy.wait_send()

        else:

            @pl.when(inside)
            def _():
                back[1].wait_recv()
                back[2].start()

            yield

            @pl.when(outside)
            def _():
                back[2].wait_recv()
                lift.wait_send()

            @pl.when(inside)
            def _():
                across.wait_send()
                side.wait_send()
                for copy in trade + back:
                    copy.wait_send()

        if kind == "shared":
            for copy in copies:
                copy.wait_send()

    waiting = [run(number, *chunk) for number, chunk in enumerate(chunks)]
    active, extra = [], [smalls(), activations()]

    def advance(running):
        still = []
        for steps in running:
            try:
                next(steps)
                still.append(steps)
            except StopIteration:
                pass
        return still

    while waiting or active:
        active = advance(active + waiting[:PER_TURN])
        waiting = waiting[PER_TURN:]
        extra = advance(extra)
        next_columns()
    while extra:
        extra = advance(extra)


def reduce_gradients(size, depth, inner, common, norm_row, gp, scaled, cols, tok_out, small):
    total, width = scaled.shape
    own_rows = tok_out.shape[1]
    chunks, counts = reduce_chunks(inner, common)
    scratch = []
    for (shared, rows, order), count in counts.items():
        for fraction in PARTS[order].values():
            scratch.append(pltpu.VMEM((count, rows // fraction, depth if shared else width), BF16))
    sems = pltpu.SemaphoreType.DMA
    half_blocks = total // 2 // ROW_BLOCK
    scratch += [
        pltpu.VMEM((3, common, depth), BF16),
        pltpu.VMEM((common, depth), BF16),
        pltpu.VMEM((5,) + small.shape, F32),
        pltpu.VMEM(scaled.shape, BF16),
        pltpu.VMEM(cols.shape, BF16),
        pltpu.VMEM(cols.shape, BF16),
        pltpu.VMEM((total, max(common, COLUMN_BLOCK)), BF16),
        pltpu.VMEM((max(common, COLUMN_BLOCK), total), BF16),
        pltpu.VMEM((ROW_BLOCK, gp.shape[1]), BF16),
        pltpu.VMEM((2, ROW_BLOCK, width), BF16),
        pltpu.VMEM((ROW_BLOCK, width), BF16),
        pltpu.VMEM((1, width), F32),
        sems((len(chunks), SLOTS)), sems((len(chunks), SLOTS)), sems((len(chunks),)),
        sems((2, TOKEN_PIECES)), sems((2, TOKEN_PIECES)), sems((5,)), sems((5,)), sems((3,)), sems((3,)),
        sems((half_blocks,)), sems((half_blocks,)), sems((5,)), sems((half_blocks,)),
    ]
    anywhere = pl.BlockSpec(memory_space=pltpu.HBM)
    local = pl.BlockSpec(memory_space=pltpu.VMEM)
    own = jax.ShapeDtypeStruct((own_rows, width), BF16)
    return pl.pallas_call(
        functools.partial(reduce_kernel, (chunks, counts, inner, depth, common, norm_row)),
        in_specs=[anywhere] * 4 + [local],
        out_specs=[anywhere] * 5 + [local] + [anywhere] * 2,
        out_shape=[
            jax.ShapeDtypeStruct((2 * size, inner, depth), BF16),
            jax.ShapeDtypeStruct((common, depth), BF16),
            own, own, own,
            jax.ShapeDtypeStruct(small.shape, F32),
            jax.ShapeDtypeStruct((half_blocks, ROW_BLOCK, width), BF16),
            own,
        ],
        scratch_shapes=scratch,
        compiler_params=pltpu.CompilerParams(
            collective_id=0, has_side_effects=True, vmem_limit_bytes=VMEM_LIMIT
        ),
        cost_estimate=pl.CostEstimate(
            flops=4 * total * gp.shape[1] * width, bytes_accessed=600 << 20, transcendentals=0
        ),
        name="reduce_gradients",
    )(gp, scaled, cols, tok_out, small)


def small_pieces(size, copies, depth, inner, columns, me, replica, scaled_low, gp, normed_low, cot_all):
    replica_bits = axis_bits(copies)
    orders = [replica_bits, replica_bits[1:] + replica_bits[:1]]
    pieces = []
    part_rows = inner // 2
    for part in range(2):
        grad = contract_rows(normed_low[:, part * part_rows : (part + 1) * part_rows], cot_all)
        order = orders[part % 2]
        mine = halve_sum(grad[None], order, replica, copies)
        pieces.append(double_gather(mine.astype(BF16), order, replica, copies)[0])
    grad_w_out = jnp.concatenate(pieces, 0).astype(F32)


    def columns_sum(start, stop, order, shared):
        grad = contract_rows(scaled_low, gp[:, start:stop])
        mine = halve_sum(grad.reshape(size, depth, stop - start), order, replica, copies)
        own = lax.dynamic_index_in_dim(mine, me, 0, keepdims=False)
        got = [own]
        for offset in range(1, size):
            there = lax.dynamic_index_in_dim(mine, me ^ offset, 0, keepdims=False)
            got.append(swap(there.astype(BF16), "fsdp", size, offset))
        if shared:
            held = sum(block.astype(F32) for block in got)[None].astype(BF16)
        else:
            held = jnp.stack([block.astype(BF16) for block in got])
        return double_gather(held, order, replica, copies)

    halves = inner // 2
    value_parts = [columns_sum(c * halves, (c + 1) * halves, orders[c % 2], False) for c in range(2)]
    gate_parts = [
        columns_sum(inner + c * halves, inner + (c + 1) * halves, orders[c % 2], False) for c in range(2)
    ]
    shared_part = columns_sum(2 * inner, columns, orders[0], True)[0]

    def in_place(parts):
        placed = []
        for device in range(size):
            for part in parts:
                placed.append(lax.dynamic_index_in_dim(part, me ^ device, 0, keepdims=False))
        return placed

    grad_w_in = jnp.concatenate(in_place(gate_parts) + in_place(value_parts) + [shared_part], 1).astype(F32)
    return grad_w_in, grad_w_out


def recut(size, full_inner, inner, me, w_in):
    depth, full = w_in.shape

    def columns_of(device):
        return jnp.concatenate(
            [
                lax.dynamic_slice(w_in, (0, full_inner + device * inner), (depth, inner)),
                lax.dynamic_slice(w_in, (0, device * inner), (depth, inner)),
                w_in[:, 2 * full_inner :],
            ],
            1,
        )

    w_cols = jnp.zeros((size * depth, 2 * inner + full - 2 * full_inner), BF16)
    w_cols = lax.dynamic_update_slice(w_cols, columns_of(me), (me * depth, 0))
    for offset in range(1, size):
        received = swap(columns_of(me ^ offset), "fsdp", size, offset)
        w_cols = lax.dynamic_update_slice(w_cols, received, ((me ^ offset) * depth, 0))
    return w_cols


def on_device(copies, size, hidden_in, segment_ids, cotangent, norm_gain, w_in, conv_weight, conv_bias,
              dt_bias, a_log, skip_gain, gate_gain, w_out):
    micro_count, seq_count, tokens, width = hidden_in.shape
    own_rows = micro_count * seq_count * tokens
    total = size * own_rows
    inner = gate_gain.shape[0]
    local_heads = dt_bias.shape[0]
    heads = local_heads * size
    channel = inner // local_heads
    full_inner = inner * size
    taps, own_conv = conv_weight.shape
    conv_width = own_conv * size
    state2 = conv_width - full_inner
    depth = w_in.shape[0]
    common = state2 + heads
    columns = 2 * inner + common
    dims = (tokens, inner, state2, heads, local_heads, taps)
    me = lax.axis_index("fsdp")
    replica = lax.axis_index("replica")

    own_x = hidden_in.reshape(own_rows, width)
    own_cot = cotangent.reshape(own_rows, width)
    small = jnp.concatenate([norm_gain, conv_weight.reshape(-1), conv_bias])
    segments = segment_ids.reshape(micro_count * seq_count, tokens)
    fused = copies == 8 and size == 4 and sum(IN_ROWS) == 2 * inner
    if fused:
        padded = jnp.pad(small.astype(F32), (0, -small.shape[0] % (8 * LANES))).reshape(-1, LANES)
        scaled_low, seg_all, small, w_cols = gather_inputs(
            size, inner, own_x, segments.reshape(-1, LANES), padded, w_in.T
        )
        small = small.reshape(size, -1)
        own_cot_later, _ = lax.optimization_barrier((own_cot, seg_all))
        cot_across = swap(own_cot_later, "fsdp", size, 2)
        cot_beside = swap(own_cot_later, "fsdp", size, 1)
    else:
        small = lax.all_gather(small, "fsdp", axis=0, tiled=False).astype(F32)
        x_all = gather_relative(own_x, "fsdp", size).reshape(total, width)
        seg_all = gather_relative(segments, "fsdp", size)
        w_cols = recut(size, full_inner, inner, me, w_in).T
        cot_all = gather_relative(own_cot, "fsdp", size).reshape(total, width)
    seg_all = seg_all.reshape(total // tokens, tokens)
    full_norm = small[:, :depth].reshape(1, width)
    full_cw = small[:, depth : depth + taps * own_conv].reshape(size, taps, own_conv)
    full_cw = full_cw.transpose(1, 0, 2).reshape(taps, conv_width)
    full_cb = small[:, depth + taps * own_conv : depth + (taps + 1) * own_conv].reshape(1, conv_width)

    def normalise(inputs):
        wide = inputs.astype(F32)
        return lax.rsqrt(jnp.mean(wide * wide, -1, keepdims=True) + EPS)

    if not fused:
        scaled_low = norm_rows(x_all, full_norm)
    projected = contract_cols(scaled_low, w_cols)

    conv_all = jnp.concatenate([full_cw, full_cb, jnp.zeros((7 - taps, conv_width), F32)], 0)
    conv_own = jnp.concatenate(
        [lax.dynamic_slice(conv_all, (0, me * inner), (8, inner)), conv_all[:, full_inner:]], 1
    )
    pad_heads = lambda row: jnp.pad(row.astype(F32), (0, LANES - local_heads))
    head_rows = jnp.stack([pad_heads(dt_bias), pad_heads(-jnp.exp(a_log.astype(F32)))])
    head_rows = jnp.pad(head_rows, ((0, 6), (0, 0)))
    chan_rows = jnp.stack([jnp.repeat(skip_gain.astype(F32), channel), gate_gain.astype(F32)])
    chan_rows = jnp.pad(chan_rows, ((0, 6), (0, 0)))
    same = []
    for offset in range(1, taps):
        equal = (seg_all[:, offset:] == seg_all[:, :-offset]).astype(F32)
        same.append(jnp.pad(equal, ((0, 0), (offset, 0))))
    same = jnp.pad(jnp.stack(same, 2), ((0, 0), (0, 0), (0, 9 - taps)))
    operands = (
        me.astype(jnp.int32).reshape(1), projected, seg_all[:, :, None], seg_all[:, None, :], same,
        head_rows, conv_own, chan_rows,
    )
    gated, squares, scan_out = mix_forward(dims, operands)
    if fused:
        cot_across, squares = lax.optimization_barrier((cot_across, squares))
        cot_all = jnp.concatenate([own_cot, cot_across, cot_beside, swap(cot_across, "fsdp", size, 1)], 0)
    grad_normed = contract_cols(cot_all, w_out)
    cross = jnp.sum(gated.astype(F32) * grad_normed, 1)
    stats = sum_tokens(jnp.stack([squares[:, 0], cross]), "fsdp", size)
    root = lax.rsqrt(stats[0] / full_inner + EPS)
    pull = root * root * root * stats[1] / full_inner

    normed_low = (gated.astype(F32) * root[:, None]).astype(BF16)
    if fused:
        near = total // 2
        far_out = jnp.dot(gated[near:], w_out, preferred_element_type=F32).astype(BF16)
        normed_low, far_out = lax.optimization_barrier((normed_low, far_out))
        far_out = swap(far_out, "fsdp", size, 1)
        grad_out = contract_rows(normed_low, cot_all).astype(BF16)
        head_rows, grad_out = lax.optimization_barrier((head_rows, grad_out))
        operands = operands[:5] + (head_rows,) + operands[6:]
        own_out = lax.psum_scatter(grad_out, "replica", scatter_dimension=0, tiled=True)
        tok_out = jnp.dot(gated[:near], w_out, preferred_element_type=F32) + far_out.astype(F32)
        tok_out = tok_out.astype(BF16).reshape(2, own_rows, width)
    gp, grad_conv, grad_chan, grad_head = mix_backward(
        dims, operands, jnp.stack([root, pull], 1), grad_normed, scan_out
    )
    if fused:
        own_out, grad_head, tok_out = lax.optimization_barrier((own_out, grad_head, tok_out))
        grad_w_out = lax.all_gather(own_out, "replica", axis=0, tiled=True).astype(F32)
    own_wide = own_x.astype(F32)
    own_root = normalise(own_x)

    conv_full = jnp.zeros((8, conv_width), F32)
    conv_full = lax.dynamic_update_slice(conv_full, grad_conv[:, inner:], (0, full_inner))
    conv_full = lax.dynamic_update_slice(conv_full, grad_conv[:, :inner], (0, me * inner))
    conv_full = conv_full[: taps + 1].reshape(-1)
    skip_grad = grad_chan[0].reshape(local_heads, channel).sum(1)
    own_small = jnp.concatenate(
        [grad_head[0, :local_heads], grad_head[1, :local_heads], skip_grad, grad_chan[1]]
    )

    if fused:
        spread = lax.dynamic_update_slice(jnp.zeros((size, own_small.shape[0]), F32), own_small[None], (me, 0))
        norm_row = -(-conv_full.shape[0] // LANES)
        conv_padded = jnp.pad(conv_full, (0, norm_row * LANES - conv_full.shape[0]))
        vector = jnp.concatenate([conv_padded, jnp.zeros((width,), F32), spread.reshape(-1)])
        vector = jnp.pad(vector, (0, -vector.shape[0] % (8 * LANES))).reshape(-1, LANES)
        sum_in, sum_shared, got_out, own_grad, got_grad, vector, _, _ = reduce_gradients(
            size, depth, inner, common, norm_row, gp, scaled_low, w_cols, tok_out, vector
        )
        grad_w_in = jnp.concatenate([sum_in.reshape(2 * full_inner, depth), sum_shared], 0).astype(F32).T
        out_sum = tok_out[0].astype(F32) + got_out.astype(F32)
        grad_scaled = own_grad.astype(F32) + got_grad.astype(F32)
        vector = vector.reshape(-1)
        conv_full = vector[: conv_full.shape[0]]
        start = norm_row * LANES
        grad_norm = vector[start : start + width] / full_norm[0]
        start = start + width
        own_small = lax.dynamic_slice(vector, (start + me * own_small.shape[0],), own_small.shape)
    else:
        out_part = jnp.dot(gated, w_out, preferred_element_type=F32).astype(BF16)
        out_sum = scatter_relative(out_part.reshape(size, own_rows, width), "fsdp", size)
        grad_w_in, grad_w_out = small_pieces(
            size, copies, depth, inner, columns, me, replica, scaled_low, gp, normed_low, cot_all
        )
        scaled_part = jnp.dot(gp, w_cols, preferred_element_type=F32).astype(BF16)
        grad_scaled = scatter_relative(scaled_part.reshape(size, own_rows, width), "fsdp", size)
        grad_norm = jnp.sum(grad_scaled * own_wide * own_root, 0)
        conv_full, grad_norm = lax.psum((conv_full, grad_norm), ("replica", "fsdp"))
        own_small = lax.psum(own_small, "replica")

    block_out = (own_wide + root[:own_rows, None] * out_sum).astype(BF16).reshape(hidden_in.shape)
    gained = grad_scaled * full_norm
    inner_mean = jnp.mean(gained * own_wide, -1, keepdims=True)
    grad_in = own_cot.astype(F32) + own_root * gained - own_wide * (own_root * own_root * own_root * inner_mean)
    grad_in = grad_in.reshape(hidden_in.shape)
    conv_full = lax.dynamic_slice(conv_full.reshape(taps + 1, conv_width), (0, me * own_conv), (taps + 1, own_conv))
    grad_norm = lax.dynamic_slice(grad_norm, (me * depth,), (depth,))
    return (
        block_out,
        grad_in,
        grad_norm,
        grad_w_in,
        conv_full[:taps],
        conv_full[taps],
        own_small[:local_heads],
        own_small[local_heads : 2 * local_heads],
        own_small[2 * local_heads : 3 * local_heads],
        own_small[3 * local_heads :],
        grad_w_out,
    )


def solution(mesh):
    rows = ("replica", "fsdp")
    placed = (
        P(None, rows, None, None),
        P(None, rows, None),
        P(None, rows, None, None),
        P("fsdp"),
        P("fsdp", None),
        P(None, "fsdp"),
        P("fsdp"),
        P("fsdp"),
        P("fsdp"),
        P("fsdp"),
        P("fsdp"),
        P("fsdp", None),
    )
    return jax.shard_map(
        functools.partial(on_device, mesh.shape["replica"], mesh.shape["fsdp"]),
        mesh=mesh,
        in_specs=placed,
        out_specs=(
            P(None, rows, None, None),
            P(None, rows, None, None),
            P("fsdp"),
            P("fsdp", None),
            P(None, "fsdp"),
            P("fsdp"),
            P("fsdp"),
            P("fsdp"),
            P("fsdp"),
            P("fsdp"),
            P("fsdp", None),
        ),
        check_vma=False,
    )
```

```python
import functools

import jax
import jax.numpy as jnp
from jax import lax
from jax.experimental import pallas as pl
from jax.experimental.pallas import tpu as pltpu
from jax.sharding import PartitionSpec as P

EPS = 1e-05
HIGHEST = lax.Precision.HIGHEST
LANES = 128
F32 = jnp.float32
BF16 = jnp.bfloat16
LOG2E = 1.4426950408889634
VMEM_LIMIT = 60 << 20


def contract_rows(left, right, precision=None):
    return lax.dot_general(
        left, right, (((0,), (0,)), ((), ())), precision=precision, preferred_element_type=F32
    )


def contract_cols(left, right, precision=None):
    return lax.dot_general(
        left, right, (((1,), (1,)), ((), ())), precision=precision, preferred_element_type=F32
    )


def sigmoid(v):
    return 0.5 * jnp.tanh(0.5 * v) + 0.5


def convolve(conv_input, taps, bias, mask_refs):
    total = bias + taps[0] * conv_input
    shifted = []
    for offset in range(1, len(taps)):
        prior = pltpu.roll(conv_input, offset, 0) * mask_refs[offset - 1]
        shifted.append(prior)
        total = total + taps[offset] * prior
    return total, shifted


def prepare(dims, own_ref, proj_ref, seg_col_ref, seg_row_ref, mask_ref, head_ref, cw_ref,
            mask_wide, visible_bias, step_wide, cum_wide, cum_rows, state_act, affinity):
    tokens, inner, state2, heads, local_heads, taps = dims
    for offset in range(taps - 1):
        mask_wide[offset] = jnp.broadcast_to(mask_ref[:, offset : offset + 1], (tokens, LANES))
    rows = lax.broadcasted_iota(jnp.int32, (tokens, tokens), 0)
    cols = lax.broadcasted_iota(jnp.int32, (tokens, tokens), 1)
    visible = (rows >= cols) & (seg_col_ref[...] == seg_row_ref[...])
    visible_bias[...] = jnp.where(visible, 0.0, -1e30)
    common = 2 * inner
    raw = proj_ref[:, common + state2 : common + state2 + heads]
    raw = jnp.concatenate([raw, jnp.zeros((tokens, LANES - heads), F32)], 1)
    raw = pltpu.roll(raw, LANES - own_ref[0] * local_heads, 1)
    raw = raw + head_ref[0:1, :]
    step = jnp.maximum(raw, 0.0) + jnp.log1p(jnp.exp(-jnp.abs(raw)))
    log_decay = head_ref[1:2, :] * step
    lower = jnp.where(rows >= cols, 1.0, 0.0).astype(F32)
    cumulative = jnp.dot(lower, log_decay, precision=HIGHEST, preferred_element_type=F32)
    scaled_cum = cumulative * LOG2E
    flipped = scaled_cum.T
    lane = lax.broadcasted_iota(jnp.int32, (tokens, LANES), 1)
    for head in range(local_heads):
        cum_wide[head] = jnp.broadcast_to(scaled_cum[:, head : head + 1], (tokens, LANES))
        cum_rows[head] = flipped[head : head + 1, :]
    for pair in range(local_heads // 2):
        step_wide[pair] = jnp.where(
            lane < LANES // 2, step[:, 2 * pair : 2 * pair + 1], step[:, 2 * pair + 1 : 2 * pair + 2]
        )
    for part in range(state2 // LANES):
        at = inner + part * LANES
        conv, _ = convolve(
            proj_ref[:, common + part * LANES : common + (part + 1) * LANES],
            [cw_ref[j : j + 1, at : at + LANES] for j in range(taps)],
            cw_ref[taps : taps + 1, at : at + LANES],
            mask_wide,
        )
        state_act[part] = conv * sigmoid(conv)
    affinity[...] = contract_cols(state_act[1], state_act[0], HIGHEST)
    return raw, step, log_decay, rows, cols


def over_pairs(count, step, carry):
    group = 4 if count % 4 == 0 else 2

    def turn(index, carried):
        for inner in range(group):
            carried = step(index * group + inner, carried)
        return carried

    return lax.fori_loop(0, count // group, turn, carry)


def forward_kernel(dims, own_ref, proj_ref, seg_col_ref, seg_row_ref, mask_ref, head_ref, cw_ref, chan_ref,
                   gated_ref, square_ref, out_ref,
                   mask_wide, visible_bias, step_wide, cum_wide, cum_rows, state_act, affinity):
    tokens, inner, state2, heads, local_heads, taps = dims
    prepare(dims, own_ref, proj_ref, seg_col_ref, seg_row_ref, mask_ref, head_ref, cw_ref,
            mask_wide, visible_bias, step_wide, cum_wide, cum_rows, state_act, affinity)
    lane = lax.broadcasted_iota(jnp.int32, (tokens, LANES), 1)
    first = lane < LANES // 2
    blocks = tokens // LANES

    def pair_step(pair, squares):
        here = pl.ds(pl.multiple_of(pair * LANES, LANES), LANES)
        conv, _ = convolve(
            proj_ref[:, here], [cw_ref[j : j + 1, here] for j in range(taps)],
            cw_ref[taps : taps + 1, here], mask_wide,
        )
        values = conv * sigmoid(conv)
        weighted = values * step_wide[pair]
        out = chan_ref[0:1, here] * values
        parts = [out[b * LANES : (b + 1) * LANES] for b in range(blocks)]
        for which in range(2):
            head = 2 * pair + which
            mine = jnp.where(first == (which == 0), weighted, 0.0).astype(BF16)
            for tb in range(blocks):
                t_rows = slice(tb * LANES, (tb + 1) * LANES)
                pieces = []
                for sb in range(tb + 1):
                    s_cols = slice(sb * LANES, (sb + 1) * LANES)
                    distance = (cum_wide[head, t_rows, :] - cum_rows[head, :, s_cols]) + visible_bias[t_rows, s_cols]
                    pieces.append((affinity[t_rows, s_cols] * jnp.exp2(distance)).astype(BF16))
                weights = jnp.concatenate(pieces, 1) if tb > 0 else pieces[0]
                parts[tb] = parts[tb] + jnp.dot(
                    weights, mine[: (tb + 1) * LANES], preferred_element_type=F32
                )
        out = jnp.concatenate(parts, 0)
        out_ref[:, here] = out.astype(BF16)
        gate = proj_ref[:, pl.ds(pl.multiple_of(inner + pair * LANES, LANES), LANES)]
        gated = out * (gate * sigmoid(gate))
        gated_ref[:, here] = (gated * chan_ref[1:2, here]).astype(BF16)
        return squares + gated * gated

    squares = over_pairs(local_heads // 2, pair_step, jnp.zeros((tokens, LANES), F32))
    square_ref[...] = jnp.sum(squares, 1, keepdims=True)


def backward_kernel(dims, own_ref, proj_ref, seg_col_ref, seg_row_ref, mask_ref, head_ref, cw_ref, chan_ref,
                    stats_ref, gn_ref, out_ref,
                    gp_ref, grad_cw_ref, grad_chan_ref, grad_head_ref,
                    mask_wide, visible_bias, step_wide, cum_wide, cum_rows, state_act, affinity,
                    grad_affinity, row_sums, col_sums, wide_stats):
    tokens, inner, state2, heads, local_heads, taps = dims

    @pl.when(pl.program_id(0) == 0)
    def _():
        grad_cw_ref[...] = jnp.zeros_like(grad_cw_ref)
        grad_chan_ref[...] = jnp.zeros_like(grad_chan_ref)
        grad_head_ref[...] = jnp.zeros_like(grad_head_ref)

    raw, step, log_decay, rows, cols = prepare(
        dims, own_ref, proj_ref, seg_col_ref, seg_row_ref, mask_ref, head_ref, cw_ref,
        mask_wide, visible_bias, step_wide, cum_wide, cum_rows, state_act, affinity)
    grad_affinity[...] = jnp.zeros_like(grad_affinity)
    row_sums[...] = jnp.zeros_like(row_sums)
    col_sums[...] = jnp.zeros_like(col_sums)
    wide_stats[0] = jnp.broadcast_to(stats_ref[:, 0:1], (tokens, LANES))
    wide_stats[1] = jnp.broadcast_to(stats_ref[:, 1:2], (tokens, LANES))
    lane = lax.broadcasted_iota(jnp.int32, (tokens, LANES), 1)
    block_lane = lax.broadcasted_iota(jnp.int32, (LANES, LANES), 1)
    first = lane < LANES // 2
    blocks = tokens // LANES

    def conv_back(grad_conv, shifted, conv_input, here):
        grad_cw_ref[0:1, here] += jnp.sum(grad_conv * conv_input, 0, keepdims=True)
        grad_cw_ref[taps : taps + 1, here] += jnp.sum(grad_conv, 0, keepdims=True)
        back = cw_ref[0:1, here] * grad_conv
        for offset in range(1, taps):
            grad_cw_ref[offset : offset + 1, here] += jnp.sum(grad_conv * shifted[offset - 1], 0, keepdims=True)
            term = (cw_ref[offset : offset + 1, here] * grad_conv) * mask_wide[offset - 1]
            back = back + pltpu.roll(term, tokens - offset, 0)
        return back

    def pair_step(pair, carry):
        here = pl.ds(pl.multiple_of(pair * LANES, LANES), LANES)
        there = pl.ds(pl.multiple_of(inner + pair * LANES, LANES), LANES)
        conv_input = proj_ref[:, here]
        conv, shifted = convolve(
            conv_input, [cw_ref[j : j + 1, here] for j in range(taps)],
            cw_ref[taps : taps + 1, here], mask_wide,
        )
        conv_sig = sigmoid(conv)
        values = conv * conv_sig
        weighted = values * step_wide[pair]
        skip = chan_ref[0:1, here]
        halves = [jnp.where(first == (which == 0), weighted, 0.0).astype(BF16) for which in range(2)]
        out = out_ref[:, here].astype(F32)
        gate = proj_ref[:, there]
        gate_sig = sigmoid(gate)
        gate_silu = gate * gate_sig
        gated = out * gate_silu
        gn = gn_ref[:, here]
        gain = chan_ref[1:2, here]
        root = wide_stats[0]
        grad_chan_ref[1:2, here] += jnp.sum(gn * gated * root, 0, keepdims=True)
        grad_gated = root * (gn * gain) - gated * wide_stats[1]
        grad_out = grad_gated * gate_silu
        gp_ref[:, there] = (grad_gated * out * (gate_sig * (1.0 + gate * (1.0 - gate_sig)))).astype(BF16)
        grad_chan_ref[0:1, here] += jnp.sum(grad_out * values, 0, keepdims=True)
        back_parts = [jnp.zeros((LANES, LANES), F32) for _ in range(blocks)]
        for which in range(2):
            head = 2 * pair + which
            mine = jnp.where(first == (which == 0), grad_out, 0.0).astype(BF16)
            for tb in range(blocks):
                t_rows = slice(tb * LANES, (tb + 1) * LANES)
                sums = None
                for sb in range(tb + 1):
                    s_cols = slice(sb * LANES, (sb + 1) * LANES)
                    distance = (cum_wide[head, t_rows, :] - cum_rows[head, :, s_cols]) + visible_bias[t_rows, s_cols]
                    decay = jnp.exp2(distance)
                    weights = affinity[t_rows, s_cols] * decay
                    cross = contract_cols(mine[t_rows], halves[which][s_cols])
                    grad_affinity[t_rows, s_cols] += cross * decay
                    energy = cross * weights
                    col_sums[head, :, s_cols] += jnp.sum(energy, 0, keepdims=True)
                    sums = energy if sums is None else sums + energy
                    back_parts[sb] = back_parts[sb] + contract_rows(weights.astype(BF16), mine[t_rows])
                row_sums[t_rows, :] += jnp.where(
                    block_lane == head, jnp.sum(sums, 1, keepdims=True), 0.0
                )
        grad_values = jnp.concatenate(back_parts, 0) * step_wide[pair] + skip * grad_out
        grad_conv = grad_values * (conv_sig * (1.0 + conv * (1.0 - conv_sig)))
        gp_ref[:, here] = conv_back(grad_conv, shifted, conv_input, here).astype(BF16)
        return carry

    over_pairs(local_heads // 2, pair_step, 0)

    common = 2 * inner
    grad_states = [
        contract_rows(grad_affinity[...], state_act[1], HIGHEST),
        jnp.dot(grad_affinity[...], state_act[0], precision=HIGHEST, preferred_element_type=F32),
    ]
    for part in range(state2 // LANES):
        at = slice(inner + part * LANES, inner + (part + 1) * LANES)
        spot = slice(common + part * LANES, common + (part + 1) * LANES)
        conv_input = proj_ref[:, spot]
        conv, shifted = convolve(
            conv_input, [cw_ref[j : j + 1, at] for j in range(taps)], cw_ref[taps : taps + 1, at], mask_wide
        )
        conv_sig = sigmoid(conv)
        grad_conv = grad_states[part] * (conv_sig * (1.0 + conv * (1.0 - conv_sig)))
        gp_ref[:, spot] = conv_back(grad_conv, shifted, conv_input, at).astype(BF16)

    col_rows = [col_sums[head] for head in range(local_heads)]
    col_rows.append(jnp.zeros((LANES - local_heads, tokens), F32))
    col_energy = jnp.concatenate(col_rows, 0).T
    upper = jnp.where(cols >= rows, 1.0, 0.0).astype(F32)
    grad_decay = jnp.dot(upper, row_sums[...] - col_energy, precision=HIGHEST, preferred_element_type=F32)
    step_sig = sigmoid(raw)
    ratio = jnp.where(raw < -20.0, 1.0, step_sig / jnp.maximum(step, 1e-30))
    grad_raw = col_energy * ratio + (head_ref[1:2, :] * grad_decay) * step_sig
    grad_head_ref[0:1, :] += jnp.sum(grad_raw, 0, keepdims=True)
    grad_head_ref[1:2, :] += jnp.sum(grad_decay * log_decay, 0, keepdims=True)
    placed = pltpu.roll(grad_raw, own_ref[0] * local_heads, 1)
    gp_ref[:, common + state2 : common + state2 + heads] = placed[:, :heads].astype(BF16)


def mixer_specs(dims, width, start=0):
    tokens, inner, state2, heads, local_heads, taps = dims
    fixed = lambda shape: pl.BlockSpec(shape, lambda s: (0,) * len(shape))
    in_specs = [
        pl.BlockSpec(memory_space=pltpu.SMEM),
        pl.BlockSpec((tokens, width), lambda s: (s + start, 0)),
        pl.BlockSpec((None, tokens, 1), lambda s: (s + start, 0, 0)),
        pl.BlockSpec((None, 1, tokens), lambda s: (s + start, 0, 0)),
        pl.BlockSpec((None, tokens, 8), lambda s: (s + start, 0, 0)),
        fixed((8, LANES)),
        fixed((8, inner + state2)),
        fixed((8, inner)),
    ]
    scratch = [
        pltpu.VMEM((taps - 1, tokens, LANES), F32),
        pltpu.VMEM((tokens, tokens), F32),
        pltpu.VMEM((local_heads // 2, tokens, LANES), F32),
        pltpu.VMEM((local_heads, tokens, LANES), F32),
        pltpu.VMEM((local_heads, 1, tokens), F32),
        pltpu.VMEM((state2 // LANES, tokens, LANES), F32),
        pltpu.VMEM((tokens, tokens), F32),
    ]
    return in_specs, scratch


def mix_forward(dims, operands):
    tokens, inner, state2, heads, local_heads, taps = dims
    total, width = operands[1].shape
    in_specs, scratch = mixer_specs(dims, width)
    return pl.pallas_call(
        functools.partial(forward_kernel, dims),
        grid=(total // tokens,),
        in_specs=in_specs,
        out_specs=[
            pl.BlockSpec((tokens, inner), lambda s: (s, 0)),
            pl.BlockSpec((tokens, 1), lambda s: (s, 0)),
            pl.BlockSpec((tokens, inner), lambda s: (s, 0)),
        ],
        out_shape=[
            jax.ShapeDtypeStruct((total, inner), BF16),
            jax.ShapeDtypeStruct((total, 1), F32),
            jax.ShapeDtypeStruct((total, inner), BF16),
        ],
        scratch_shapes=scratch,
        compiler_params=pltpu.CompilerParams(vmem_limit_bytes=VMEM_LIMIT),
        cost_estimate=pl.CostEstimate(
            flops=total * local_heads * tokens * 4 * 64,
            bytes_accessed=total * width * 4,
            transcendentals=total * local_heads * tokens,
        ),
        name="mix_forward",
    )(*operands)


def mix_backward(dims, operands, stats, grad_normed, scan_out, start, count):
    tokens, inner, state2, heads, local_heads, taps = dims
    total, width = count * tokens, operands[1].shape[1]
    in_specs, scratch = mixer_specs(dims, width, start)
    fixed = lambda shape: pl.BlockSpec(shape, lambda s: (0,) * len(shape))
    return pl.pallas_call(
        functools.partial(backward_kernel, dims),
        grid=(count,),
        in_specs=in_specs + [
            pl.BlockSpec((tokens, 2), lambda s: (s + start, 0)),
            pl.BlockSpec((tokens, inner), lambda s: (s + start, 0)),
            pl.BlockSpec((tokens, inner), lambda s: (s + start, 0)),
        ],
        out_specs=[
            pl.BlockSpec((tokens, width), lambda s: (s, 0)),
            fixed((8, inner + state2)),
            fixed((8, inner)),
            fixed((8, LANES)),
        ],
        out_shape=[
            jax.ShapeDtypeStruct((total, width), BF16),
            jax.ShapeDtypeStruct((8, inner + state2), F32),
            jax.ShapeDtypeStruct((8, inner), F32),
            jax.ShapeDtypeStruct((8, LANES), F32),
        ],
        scratch_shapes=scratch + [
            pltpu.VMEM((tokens, tokens), F32),
            pltpu.VMEM((tokens, LANES), F32),
            pltpu.VMEM((local_heads, 1, tokens), F32),
            pltpu.VMEM((2, tokens, LANES), F32),
        ],
        compiler_params=pltpu.CompilerParams(vmem_limit_bytes=VMEM_LIMIT),
        cost_estimate=pl.CostEstimate(
            flops=total * local_heads * tokens * 12 * 64,
            bytes_accessed=total * width * 6,
            transcendentals=2 * total * local_heads * tokens,
        ),
        name="mix_backward",
    )(*operands, stats, grad_normed, scan_out)


def norm_kernel(x_ref, gain_ref, scaled_ref):
    wide = x_ref[...].astype(F32)
    root = lax.rsqrt(jnp.mean(wide * wide, 1, keepdims=True) + EPS)
    scaled_ref[...] = (wide * root * gain_ref[...]).astype(BF16)


def norm_rows(inputs, gain):
    rows, width = inputs.shape
    block = pl.BlockSpec((256, width), lambda s: (s, 0))
    return pl.pallas_call(
        norm_kernel,
        grid=(rows // 256,),
        in_specs=[block, pl.BlockSpec((1, width), lambda s: (0, 0))],
        out_specs=block,
        out_shape=jax.ShapeDtypeStruct(inputs.shape, BF16),
        compiler_params=pltpu.CompilerParams(vmem_limit_bytes=VMEM_LIMIT),
        cost_estimate=pl.CostEstimate(flops=4 * rows * width, bytes_accessed=4 * rows * width, transcendentals=rows),
        name="norm_rows",
    )(inputs, gain)


def swap(array, axis, size, bit):
    return lax.ppermute(array, axis, [(i, i ^ bit) for i in range(size)])


def axis_bits(size):
    bits = []
    bit = 1
    while bit < size:
        bits.append(bit)
        bit *= 2
    return bits


def gather_relative(array, axis, size):
    held = array[None]
    for bit in reversed(axis_bits(size)):
        held = jnp.concatenate([held, swap(held, axis, size, bit)], 0)
    return held


def scatter_relative(array, axis, size):
    total = array
    for bit in axis_bits(size):
        half = total.shape[0] // 2
        received = swap(total[half:].astype(BF16), axis, size, bit)
        total = total[:half].astype(F32) + received.astype(F32)
    return total[0]


def sum_tokens(array, axis, size):
    kinds, tokens = array.shape
    for bit in axis_bits(size):
        stride = tokens // (2 * bit)
        received = swap(array, axis, size, bit).reshape(kinds, bit, 2, stride)
        array = array + received[:, :, ::-1].reshape(kinds, tokens)
    return array


def halve_sum(array, order, replica, size):
    total = array
    for bit in order:
        blocks, rows, columns = total.shape
        mine = (replica // bit) % 2
        halves = total.reshape(blocks, 2, rows // 2, columns)
        kept = lax.dynamic_index_in_dim(halves, mine, 1, keepdims=False)
        sent = lax.dynamic_index_in_dim(halves, 1 - mine, 1, keepdims=False)
        received = swap(sent.astype(BF16), "replica", size, bit)
        total = kept + received.astype(F32)
    return total


def double_gather(array, order, replica, size):
    held = array
    for bit in reversed(order):
        received = swap(held, "replica", size, bit)
        upper = (replica // bit) % 2 == 1
        held = jnp.where(
            upper,
            jnp.concatenate([received, held], 1),
            jnp.concatenate([held, received], 1),
        )
    return held


def flip(index, bit):
    return index + bit * (1 - 2 * ((index // bit) % 2))


MESH = pl.DeviceIdType.MESH


def greet(peers):
    barrier = pltpu.get_barrier_semaphore()
    for peer in peers:
        pl.semaphore_signal(barrier, inc=1, device_id=peer, device_id_type=MESH)
    pl.semaphore_wait(barrier, len(peers))


def copy_peers(me):
    return [flip(me, 1), flip(me, 2), flip(flip(me, 1), 2)]


def gather_kernel(full_inner, inner, x_ref, seg_ref, small_ref, w_ref,
                  scaled_ref, seg_all_ref, small_all_ref, cols_ref,
                  x_all_ref, scaled, gain, cols_held, send_sems, recv_sems, local_sems, store_sems, norm_sems):
    me = lax.axis_index("fsdp")
    replica = lax.axis_index("replica")
    depth, common = w_ref.shape[1], w_ref.shape[0] - 2 * full_inner
    peers = [(replica, peer) for peer in copy_peers(me)]
    beside, above = (flip(replica, 1), me), (flip(replica, 2), me)
    greet(peers + [beside, above])
    number = [0]
    started = []

    def send(from_ref, to_ref, device):
        slot = number[0]
        number[0] += 1
        copy = pltpu.make_async_remote_copy(
            src_ref=from_ref, dst_ref=to_ref, send_sem=send_sems.at[slot], recv_sem=recv_sems.at[slot],
            device_id=device, device_id_type=MESH,
        )
        copy.start()
        started.append(copy)
        return copy

    parts = [(0, inner), (inner, inner), (2 * inner, common)]

    def targets(owner, first, count):
        lanes = pl.ds(pl.multiple_of(owner * depth, depth), depth)
        return [
            cols_ref.at[pl.ds(pl.multiple_of(base + first * (length // 4), 16), count * (length // 4)), lanes]
            for base, length in parts
        ]

    def sources(device, first, count):
        bases = [full_inner + device * inner, device * inner, 2 * full_inner]
        return [
            w_ref.at[pl.ds(pl.multiple_of(base + first * (length // 4), 16), count * (length // 4))]
            for base, (_, length) in zip(bases, parts)
        ]

    def send_parts(from_refs, to_refs, device):
        return [send(source, target, device) for source, target in zip(from_refs, to_refs)]

    spot = replica % 4
    smalls = [send(small_ref, small_all_ref.at[me], peer) for peer in peers]
    smalls += [send(seg_ref, seg_all_ref.at[slot], peer) for peer, slot in zip(peers, (2, 1, 3))]
    across = [send_parts(sources(peers[which][1], spot, 1), targets(me, spot, 1), peers[which]) for which in (1, 2)]
    x_y = send(x_ref, x_all_ref.at[1], peers[1])
    near = send_parts(sources(peers[0][1], 0, 4), targets(me, 0, 4), peers[0])
    x_near = send(x_ref, x_all_ref.at[2], peers[0])
    held = [cols_held.at[pl.ds(base, length)] for base, length in parts]
    own = list(zip(sources(me, 0, 4), held, targets(me, 0, 4)))
    loads = [pltpu.make_async_copy(source, held, local_sems.at[i]) for i, (source, held, _) in enumerate(own)]
    stores = [pltpu.make_async_copy(held, target, store_sems.at[i]) for i, (_, held, target) in enumerate(own)]
    x_own = pltpu.make_async_copy(x_ref, x_all_ref.at[0], local_sems.at[3])
    small_own = pltpu.make_async_copy(small_ref, small_all_ref.at[me], local_sems.at[4])
    stores.append(pltpu.make_async_copy(seg_ref, seg_all_ref.at[0], local_sems.at[5]))
    for copy in loads + [x_own, small_own, stores[-1]]:
        copy.start()
    for load, store in zip(loads, stores):
        load.wait()
        store.start()

    rows_at_once = 128
    block_rows, width = scaled.shape[1:]
    tiles_of_owner = depth // LANES

    def normalise(block):
        def step(piece, carry):
            rows = pl.ds(pl.multiple_of(piece * rows_at_once, rows_at_once), rows_at_once)
            wide = x_all_ref[block, rows, :].astype(F32)
            root = lax.rsqrt(jnp.mean(wide * wide, 1, keepdims=True) + EPS)
            scaled[block, rows, :] = (wide * root * gain[...]).astype(BF16)
            return carry

        lax.fori_loop(0, block_rows // rows_at_once, step, 0)
        store = pltpu.make_async_copy(
            scaled.at[block], scaled_ref.at[pl.ds(block * block_rows, block_rows)], norm_sems.at[block]
        )
        store.start()
        stores.append(store)

    small_own.wait()
    for copy in smalls:
        copy.wait_recv()
    for tile in range(width // LANES):
        gain[:, tile * LANES : (tile + 1) * LANES] = small_all_ref[
            tile // tiles_of_owner, tile % tiles_of_owner : tile % tiles_of_owner + 1, :
        ]
    x_own.wait()
    normalise(0)

    def relay(which, first, count, device):
        refs = targets(peers[which][1], first, count)
        return send_parts(refs, refs, device)

    for copy in across[0]:
        copy.wait_recv()
    first_beside = relay(1, spot, 1, beside)
    for copy in across[1]:
        copy.wait_recv()
    first_above = relay(2, spot, 1, above)
    for copy in first_beside:
        copy.wait_recv()
    last = relay(1, (spot // 2) * 2, 2, above)
    for copy in first_above:
        copy.wait_recv()
    last += relay(2, spot, 1, beside)
    last += relay(2, flip(spot, 2), 1, beside)
    x_near.wait_recv()
    normalise(2)
    x_y.wait_recv()
    x_last = send(x_all_ref.at[1], x_all_ref.at[3], peers[0])
    normalise(1)
    x_last.wait_recv()
    normalise(3)
    for copy in last + near:
        copy.wait_recv()
    for copy in stores:
        copy.wait()
    for copy in started:
        copy.wait_send()


GATHER_COPIES = 34


def gather_inputs(size, inner, x, segments, small, w_flipped):
    full, depth = w_flipped.shape
    full_inner = inner * size
    columns = 2 * inner + full - 2 * full_inner
    anywhere = pl.BlockSpec(memory_space=pltpu.HBM)
    return pl.pallas_call(
        functools.partial(gather_kernel, full_inner, inner),
        in_specs=[anywhere] * 4,
        out_specs=[anywhere] * 2 + [pl.BlockSpec(memory_space=pltpu.VMEM), anywhere],
        out_shape=[
            jax.ShapeDtypeStruct((size * x.shape[0], x.shape[1]), BF16),
            jax.ShapeDtypeStruct((size,) + segments.shape, jnp.int32),
            jax.ShapeDtypeStruct((size,) + small.shape, F32),
            jax.ShapeDtypeStruct((columns, size * depth), BF16),
        ],
        scratch_shapes=[
            pltpu.VMEM((size,) + x.shape, BF16),
            pltpu.VMEM((size,) + x.shape, BF16),
            pltpu.VMEM((1, x.shape[1]), F32),
            pltpu.VMEM((columns, depth), BF16),
            pltpu.SemaphoreType.DMA((GATHER_COPIES,)),
            pltpu.SemaphoreType.DMA((GATHER_COPIES,)),
            pltpu.SemaphoreType.DMA((6,)),
            pltpu.SemaphoreType.DMA((3,)),
            pltpu.SemaphoreType.DMA((4,)),
        ],
        compiler_params=pltpu.CompilerParams(
            collective_id=1, has_side_effects=True, vmem_limit_bytes=VMEM_LIMIT
        ),
        cost_estimate=pl.CostEstimate(flops=0, bytes_accessed=200 << 20, transcendentals=0),
        name="gather_inputs",
    )(x, segments, small, w_flipped)


PARTS = {
    "side": {"got": 2, "lift": 2, "sent": 4, "swapped": 4, "final": 4},
    "lift": {"got": 1, "sent": 2, "swapped": 2, "sent_side": 4, "got_side": 4, "final": 4},
}
SLOTS = 9
IN_ROWS = (64,) * 32
SHARED_AT = 4
COLUMN_BLOCK = 256
ROW_BLOCK = 256
LANE_TILE = 1024
PER_TURN = 3
AGAIN = 1
TOKEN_PIECES = 8


def reduce_chunks(inner, common):
    pieces = []
    start = 0
    for rows in IN_ROWS:
        pieces.append(("in", start, rows))
        start += rows
    pieces.insert(SHARED_AT, ("shared", 0, common))
    counts = {}
    placed = []
    for number, (kind, start, rows) in enumerate(pieces):
        order = "lift" if number % 3 == 2 else "side"
        key = (kind == "shared", rows, order)
        where = counts.get(key, 0)
        counts[key] = where + 1
        placed.append((kind, start, rows, order, where))
    return placed, counts


def reduce_kernel(plan, gp_first_ref, gp_last_ref, scaled_ref, cols_ref, tok_out_ref, small_ref,
                  sum_in_ref, sum_shared_ref, got_out_ref, own_grad_ref, got_grad_ref, small_sum_ref,
                  far_land_ref, across_ref, *scratch):
    chunks, counts, inner, depth, common, norm_row = plan
    groups = {}
    position = 0
    for key in counts:
        names = list(PARTS[key[2]])
        groups[key] = dict(zip(names, scratch[position : position + len(names)]))
        position += len(names)
    (shared_in, shared_sum, small_got, scaled, cols, grads, gp_cols, gp_flipped, gp_rows, tiles, far_tile, norm_sum,
     send_sems, recv_sems, local_sems, tok_send, tok_recv,
     small_send, small_recv, shared_send, shared_recv, far_send, far_recv, load_sems, store_sems) = scratch[position:]
    whole_loads = [
        pltpu.make_async_copy(scaled_ref, scaled, load_sems.at[0]),
        pltpu.make_async_copy(cols_ref, cols, load_sems.at[1]),
    ]
    for copy in whole_loads:
        copy.start()
    loaded = [False, False]

    def need(which):
        if not loaded[which]:
            whole_loads[which].wait()
            loaded[which] = True

    column_blocks = [(start, COLUMN_BLOCK) for start in range(0, 2 * inner, COLUMN_BLOCK)]
    column_blocks.insert(1, (2 * inner, common))
    width = scaled.shape[1]
    rows_of_block = tiles.shape[1]
    lane_tiles = width // LANE_TILE
    column_loads = []
    columns_done = []

    first_rows = gp_first_ref.shape[0]
    all_rows = first_rows + gp_last_ref.shape[0]

    def load_columns(number):
        if number < len(column_blocks):
            start, count = column_blocks[number]
            lanes = pl.ds(0, count)
            copies = [
                pltpu.make_async_copy(
                    gp_first_ref.at[:, pl.ds(start, count)], gp_cols.at[pl.ds(0, first_rows), lanes], load_sems.at[2]
                ),
                pltpu.make_async_copy(
                    gp_last_ref.at[:, pl.ds(start, count)],
                    gp_cols.at[pl.ds(first_rows, all_rows - first_rows), lanes], load_sems.at[5],
                ),
            ]
            for copy in copies:
                copy.start()
            column_loads.append(copies)

    def next_columns():
        number = len(columns_done)
        if number == len(column_blocks):
            return
        start, count = column_blocks[number]
        need(0)
        for copy in column_loads[number]:
            copy.wait()
        gp_flipped[pl.ds(0, count), :] = gp_cols[:, pl.ds(0, count)].T
        load_columns(number + 1)

        def lanes_step(tile, carry):
            lanes = pl.ds(pl.multiple_of(tile * LANE_TILE, LANE_TILE), LANE_TILE)
            grads[pl.ds(start, count), lanes] = jnp.dot(
                gp_flipped[pl.ds(0, count), :], scaled[:, lanes], preferred_element_type=F32
            ).astype(BF16)
            return carry

        lax.fori_loop(0, lane_tiles, lanes_step, 0)
        columns_done.append(start)

    def ensure_columns(start):
        while start not in columns_done:
            next_columns()

    load_columns(0)
    me = lax.axis_index("fsdp")
    replica = lax.axis_index("replica")
    up = replica // 2
    inside = (up == 1) | (up == 2)
    outside = (up == 0) | (up == 3)
    half = up // 2
    aside = replica % 2
    beside = (flip(replica, 1), me)
    partner = (flip(replica, 2), me)
    middle = (flip(flip(replica, 2), 4), me)
    peers = [(replica, peer) for peer in copy_peers(me)]
    greet(peers + [beside, partner, middle])

    def remote(from_ref, to_ref, device, sends, recvs):
        return pltpu.make_async_remote_copy(
            src_ref=from_ref, dst_ref=to_ref, send_sem=sends, recv_sem=recvs, device_id=device, device_id_type=MESH
        )

    def lanes_of(device):
        return pl.ds(pl.multiple_of(device * depth, depth), depth)

    def activations():
        rows = got_out_ref.shape[0] // TOKEN_PIECES
        copies = []
        for piece in range(TOKEN_PIECES):
            at = pl.ds(piece * rows, rows)
            copy = remote(tok_out_ref.at[1, at], got_out_ref.at[at], peers[1], tok_send.at[0, piece], tok_recv.at[0, piece])
            copy.start()
            copies.append(copy)
            yield
        for piece in range(TOKEN_PIECES):
            at = pl.ds(piece * rows, rows)
            copy = remote(across_ref.at[at], got_grad_ref.at[at], peers[1], tok_send.at[1, piece], tok_recv.at[1, piece])
            copy.start()
            copies.append(copy)
            yield
        for copy in copies:
            copy.wait()

    def row_products():
        half_blocks = all_rows // (2 * rows_of_block)
        quarter_blocks = half_blocks // 2
        later = list(range(quarter_blocks, half_blocks))
        sooner = list(range(quarter_blocks))
        order = [(True, i) for i in later] + [(False, i) for i in later]
        order += [(True, i) for i in sooner] + [(False, i) for i in sooner]
        norm_sum[...] = jnp.zeros_like(norm_sum)
        row_loads = []

        def load_rows(number):
            if number < len(order):
                far, block = order[number]
                at = (half_blocks + block if far else block) * rows_of_block
                if at < first_rows:
                    source = gp_first_ref.at[pl.ds(at, rows_of_block)]
                else:
                    source = gp_last_ref.at[pl.ds(at - first_rows, rows_of_block)]
                copy = pltpu.make_async_copy(source, gp_rows, load_sems.at[3])
                copy.start()
                row_loads.append((copy, at))

        load_rows(0)
        need(0)
        need(1)
        arrivals = {}
        busy = [None, None]
        for number, (far, block) in enumerate(order):
            slot = number % 2
            if busy[slot] is not None:
                busy[slot]()
            if not far:
                arrivals[block].wait_recv()
                load = pltpu.make_async_copy(far_land_ref.at[block], far_tile, load_sems.at[4])
                load.start()
                load.wait()
            copy, at = row_loads[number]
            copy.wait()

            def lanes_step(tile, carry):
                lanes = pl.ds(pl.multiple_of(tile * LANE_TILE, LANE_TILE), LANE_TILE)
                part = jnp.dot(gp_rows[...], cols[:, lanes], preferred_element_type=F32)
                norm_sum[:, lanes] += jnp.sum(
                    part * scaled[pl.ds(at, rows_of_block), lanes].astype(F32), 0, keepdims=True
                )
                if not far:
                    part = part + far_tile[:, lanes].astype(F32)
                tiles[slot, :, lanes] = part.astype(BF16)
                return carry

            lax.fori_loop(0, lane_tiles, lanes_step, 0)
            load_rows(number + 1)
            if far:
                sent = remote(tiles.at[slot], far_land_ref.at[block], peers[0], far_send.at[block], far_recv.at[block])
                sent.start()
                arrivals[block] = sent
                busy[slot] = sent.wait_send
            else:
                target = own_grad_ref if block < quarter_blocks else across_ref
                place = pl.ds((block % quarter_blocks) * rows_of_block, rows_of_block)
                store = pltpu.make_async_copy(tiles.at[slot], target.at[place], store_sems.at[block])
                store.start()
                busy[slot] = store.wait
            yield
        for wait in busy:
            wait()
        for tile in range(width // LANES):
            small_sum_ref[norm_row + tile : norm_row + tile + 1, :] = norm_sum[:, tile * LANES : (tile + 1) * LANES]

    def smalls():
        small_sum_ref[...] = small_ref[...]
        yield from row_products()
        for level, peer in enumerate([peers[0], peers[1], beside, partner, middle]):
            copy = remote(small_sum_ref, small_got.at[level], peer, small_send.at[level], small_recv.at[level])
            copy.start()
            yield
            copy.wait()
            small_sum_ref[...] += small_got[level]

    def run(number, kind, start, rows, order, where):
        held = {name: ref.at[where] for name, ref in groups[kind == "shared", rows, order].items()}
        if kind == "in":
            group = 0 if start >= inner else 4
            local_start = start % inner
            ensure_columns(start // COLUMN_BLOCK * COLUMN_BLOCK)
            base_ref, base_start = grads, start
            place = lambda at, count: sum_in_ref.at[pl.ds(group, 4), pl.ds(pl.multiple_of(local_start + at, 16), count)]
        else:
            ensure_columns(2 * inner)
            base_ref, base_start = shared_sum, 0
            place = lambda at, count: sum_shared_ref.at[pl.ds(at, count)]
            copies = []
            for offset in range(3):
                copy = remote(
                    grads.at[pl.ds(2 * inner, rows), lanes_of(peers[offset][1])],
                    shared_in.at[offset], peers[offset], shared_send.at[offset], shared_recv.at[offset],
                )
                copy.start()
                copies.append(copy)
            yield
            total = grads[pl.ds(2 * inner, rows), lanes_of(me)].astype(F32)
            for offset in range(3):
                copies[offset].wait_recv()
                total = total + shared_in[offset].astype(F32)
            shared_sum[...] = total.astype(BF16)

        def source(at, count):
            return base_ref.at[pl.ds(pl.multiple_of(base_start + at, 16), count)]

        def link(from_ref, to_ref, device, slot):
            return remote(from_ref, to_ref, device, send_sems.at[number, slot], recv_sems.at[number, slot])

        def added(names_at, at, count):
            total = source(at, count)[...].astype(F32)
            for name, base in names_at:
                local = pl.multiple_of(at - base, count)
                total = total + held[name][pl.ds(local, count), :].astype(F32)
            return total

        two, four = rows // 2, rows // 4
        if order == "side":
            mine, other = pl.multiple_of(aside * two, two), pl.multiple_of((1 - aside) * two, two)
            low, high = pl.multiple_of(mine + half * four, four), pl.multiple_of(mine + (1 - half) * four, four)
            side = link(source(other, two), held["got"], beside, 0)
            side.start()
            yield
            side.wait_recv()
            lift = link(held["lift"], held["lift"], partner, 1)

            @pl.when(outside)
            def _():
                held["lift"][...] = added([("got", mine)], mine, two).astype(BF16)
                lift.start()

            yield
            bases = [("got", mine), ("lift", mine)]
            across = link(held["sent"], held["swapped"], middle, 2)

            @pl.when(inside)
            def _():
                lift.wait_recv()
                held["sent"][...] = added(bases, high, four).astype(BF16)
                across.start()

            yield
            bases = bases + [("swapped", low)]
        else:
            mine, other = pl.multiple_of(half * two, two), pl.multiple_of((1 - half) * two, two)
            low, high = pl.multiple_of(mine + aside * four, four), pl.multiple_of(mine + (1 - aside) * four, four)
            lift = link(source(0, rows), held["got"], partner, 1)

            @pl.when(outside)
            def _():
                lift.start()

            yield
            bases = [("got", 0)]
            across = link(held["sent"], held["swapped"], middle, 2)

            @pl.when(inside)
            def _():
                lift.wait_recv()
                held["sent"][...] = added(bases, other, two).astype(BF16)
                across.start()

            yield
            bases = bases + [("swapped", mine)]
            side = link(held["sent_side"], held["got_side"], beside, 0)

            @pl.when(inside)
            def _():
                across.wait_recv()
                held["sent_side"][...] = added(bases, high, four).astype(BF16)
                side.start()

            yield
            bases = bases + [("got_side", low)]

        final = held["final"]
        trade = []
        if kind == "in":
            target = sum_in_ref.at[group + me, pl.ds(pl.multiple_of(local_start + low, 16), four)]
            trade = [
                link(final.at[:, lanes_of(peers[offset][1])], target, peers[offset], 3 + offset) for offset in range(3)
            ]
            own = pltpu.make_async_copy(final.at[:, lanes_of(me)], target, local_sems.at[number])
        else:
            own = pltpu.make_async_copy(final, place(low, four), local_sems.at[number])

        if order == "side":
            back = [
                link(place(low, four), place(low, four), middle, 6),
                link(place(mine, two), place(mine, two), partner, 7),
                link(place(mine, two), place(mine, two), beside, 8),
            ]
        else:
            back = [
                link(place(low, four), place(low, four), beside, 6),
                link(place(mine, two), place(mine, two), middle, 7),
                link(place(0, rows), place(0, rows), partner, 8),
            ]

        @pl.when(inside)
        def _():
            (across if order == "side" else side).wait_recv()
            final[...] = added(bases, low, four).astype(BF16)
            for copy in trade:
                copy.start()
            own.start()

        yield AGAIN

        @pl.when(inside)
        def _():
            own.wait()
            for copy in trade:
                copy.wait_recv()
            back[0].start()

        yield

        @pl.when(inside)
        def _():
            back[0].wait_recv()
            back[1].start()
            if order == "side":
                back[2].start()

        yield
        if order == "side":

            @pl.when(outside)
            def _():
                back[1].wait_recv()
                back[2].start()

            yield
            back[2].wait_recv()
            side.wait_send()
            back[2].wait_send()

            @pl.when(outside)
            def _():
                lift.wait_send()

            @pl.when(inside)
            def _():
                across.wait_send()
                for copy in trade + back[:2]:
                    copy.wait_send()

        else:

            @pl.when(inside)
            def _():
                back[1].wait_recv()
                back[2].start()

            yield

            @pl.when(outside)
            def _():
                back[2].wait_recv()
                lift.wait_send()

            @pl.when(inside)
            def _():
                across.wait_send()
                side.wait_send()
                for copy in trade + back:
                    copy.wait_send()

        if kind == "shared":
            for copy in copies:
                copy.wait_send()

    waiting = [run(number, *chunk) for number, chunk in enumerate(chunks)]
    active, extra = [], [smalls(), activations()]

    def advance(running):
        still, again = [], []
        for steps in running:
            try:
                if next(steps) == AGAIN:
                    again.append(steps)
                still.append(steps)
            except StopIteration:
                pass
        for steps in again:
            next(steps)
        return still

    while waiting or active:
        active = advance(active + waiting[:PER_TURN])
        waiting = waiting[PER_TURN:]
        extra = advance(extra)
        next_columns()
    while extra:
        extra = advance(extra)


def reduce_gradients(size, depth, inner, common, norm_row, gp_first, gp_last, scaled, cols, tok_out, small):
    total, width = scaled.shape
    own_rows = tok_out.shape[1]
    chunks, counts = reduce_chunks(inner, common)
    scratch = []
    for (shared, rows, order), count in counts.items():
        for fraction in PARTS[order].values():
            scratch.append(pltpu.VMEM((count, rows // fraction, depth if shared else width), BF16))
    sems = pltpu.SemaphoreType.DMA
    half_blocks = total // 2 // ROW_BLOCK
    scratch += [
        pltpu.VMEM((3, common, depth), BF16),
        pltpu.VMEM((common, depth), BF16),
        pltpu.VMEM((5,) + small.shape, F32),
        pltpu.VMEM(scaled.shape, BF16),
        pltpu.VMEM(cols.shape, BF16),
        pltpu.VMEM(cols.shape, BF16),
        pltpu.VMEM((total, max(common, COLUMN_BLOCK)), BF16),
        pltpu.VMEM((max(common, COLUMN_BLOCK), total), BF16),
        pltpu.VMEM((ROW_BLOCK, gp_first.shape[1]), BF16),
        pltpu.VMEM((2, ROW_BLOCK, width), BF16),
        pltpu.VMEM((ROW_BLOCK, width), BF16),
        pltpu.VMEM((1, width), F32),
        sems((len(chunks), SLOTS)), sems((len(chunks), SLOTS)), sems((len(chunks),)),
        sems((2, TOKEN_PIECES)), sems((2, TOKEN_PIECES)), sems((5,)), sems((5,)), sems((3,)), sems((3,)),
        sems((half_blocks,)), sems((half_blocks,)), sems((6,)), sems((half_blocks,)),
    ]
    anywhere = pl.BlockSpec(memory_space=pltpu.HBM)
    local = pl.BlockSpec(memory_space=pltpu.VMEM)
    own = jax.ShapeDtypeStruct((own_rows, width), BF16)
    return pl.pallas_call(
        functools.partial(reduce_kernel, (chunks, counts, inner, depth, common, norm_row)),
        in_specs=[anywhere] * 5 + [local],
        out_specs=[anywhere] * 5 + [local] + [anywhere] * 2,
        out_shape=[
            jax.ShapeDtypeStruct((2 * size, inner, depth), BF16),
            jax.ShapeDtypeStruct((common, depth), BF16),
            own, own, own,
            jax.ShapeDtypeStruct(small.shape, F32),
            jax.ShapeDtypeStruct((half_blocks, ROW_BLOCK, width), BF16),
            own,
        ],
        scratch_shapes=scratch,
        compiler_params=pltpu.CompilerParams(
            collective_id=0, has_side_effects=True, vmem_limit_bytes=VMEM_LIMIT
        ),
        cost_estimate=pl.CostEstimate(
            flops=total * width, bytes_accessed=1 << 20, transcendentals=0
        ),
        name="reduce_gradients",
    )(gp_first, gp_last, scaled, cols, tok_out, small)


def small_pieces(size, copies, depth, inner, columns, me, replica, scaled_low, gp, normed_low, cot_all):
    replica_bits = axis_bits(copies)
    orders = [replica_bits, replica_bits[1:] + replica_bits[:1]]
    pieces = []
    part_rows = inner // 2
    for part in range(2):
        grad = contract_rows(normed_low[:, part * part_rows : (part + 1) * part_rows], cot_all)
        order = orders[part % 2]
        mine = halve_sum(grad[None], order, replica, copies)
        pieces.append(double_gather(mine.astype(BF16), order, replica, copies)[0])
    grad_w_out = jnp.concatenate(pieces, 0).astype(F32)


    def columns_sum(start, stop, order, shared):
        grad = contract_rows(scaled_low, gp[:, start:stop])
        mine = halve_sum(grad.reshape(size, depth, stop - start), order, replica, copies)
        own = lax.dynamic_index_in_dim(mine, me, 0, keepdims=False)
        got = [own]
        for offset in range(1, size):
            there = lax.dynamic_index_in_dim(mine, me ^ offset, 0, keepdims=False)
            got.append(swap(there.astype(BF16), "fsdp", size, offset))
        if shared:
            held = sum(block.astype(F32) for block in got)[None].astype(BF16)
        else:
            held = jnp.stack([block.astype(BF16) for block in got])
        return double_gather(held, order, replica, copies)

    halves = inner // 2
    value_parts = [columns_sum(c * halves, (c + 1) * halves, orders[c % 2], False) for c in range(2)]
    gate_parts = [
        columns_sum(inner + c * halves, inner + (c + 1) * halves, orders[c % 2], False) for c in range(2)
    ]
    shared_part = columns_sum(2 * inner, columns, orders[0], True)[0]

    def in_place(parts):
        placed = []
        for device in range(size):
            for part in parts:
                placed.append(lax.dynamic_index_in_dim(part, me ^ device, 0, keepdims=False))
        return placed

    grad_w_in = jnp.concatenate(in_place(gate_parts) + in_place(value_parts) + [shared_part], 1).astype(F32)
    return grad_w_in, grad_w_out


def recut(size, full_inner, inner, me, w_in):
    depth, full = w_in.shape

    def columns_of(device):
        return jnp.concatenate(
            [
                lax.dynamic_slice(w_in, (0, full_inner + device * inner), (depth, inner)),
                lax.dynamic_slice(w_in, (0, device * inner), (depth, inner)),
                w_in[:, 2 * full_inner :],
            ],
            1,
        )

    w_cols = jnp.zeros((size * depth, 2 * inner + full - 2 * full_inner), BF16)
    w_cols = lax.dynamic_update_slice(w_cols, columns_of(me), (me * depth, 0))
    for offset in range(1, size):
        received = swap(columns_of(me ^ offset), "fsdp", size, offset)
        w_cols = lax.dynamic_update_slice(w_cols, received, ((me ^ offset) * depth, 0))
    return w_cols


def on_device(copies, size, hidden_in, segment_ids, cotangent, norm_gain, w_in, conv_weight, conv_bias,
              dt_bias, a_log, skip_gain, gate_gain, w_out):
    micro_count, seq_count, tokens, width = hidden_in.shape
    own_rows = micro_count * seq_count * tokens
    total = size * own_rows
    inner = gate_gain.shape[0]
    local_heads = dt_bias.shape[0]
    heads = local_heads * size
    channel = inner // local_heads
    full_inner = inner * size
    taps, own_conv = conv_weight.shape
    conv_width = own_conv * size
    state2 = conv_width - full_inner
    depth = w_in.shape[0]
    common = state2 + heads
    columns = 2 * inner + common
    dims = (tokens, inner, state2, heads, local_heads, taps)
    me = lax.axis_index("fsdp")
    replica = lax.axis_index("replica")

    own_x = hidden_in.reshape(own_rows, width)
    own_cot = cotangent.reshape(own_rows, width)
    small = jnp.concatenate([norm_gain, conv_weight.reshape(-1), conv_bias])
    segments = segment_ids.reshape(micro_count * seq_count, tokens)
    fused = copies == 8 and size == 4 and sum(IN_ROWS) == 2 * inner
    if fused:
        padded = jnp.pad(small.astype(F32), (0, -small.shape[0] % (8 * LANES))).reshape(-1, LANES)
        scaled_low, seg_all, small, w_cols = gather_inputs(
            size, inner, own_x, segments.reshape(-1, LANES), padded, w_in.T
        )
        small = small.reshape(size, -1)
        own_cot_later, _ = lax.optimization_barrier((own_cot, seg_all))
        cot_across = swap(own_cot_later, "fsdp", size, 2)
        cot_beside = swap(own_cot_later, "fsdp", size, 1)
    else:
        small = lax.all_gather(small, "fsdp", axis=0, tiled=False).astype(F32)
        x_all = gather_relative(own_x, "fsdp", size).reshape(total, width)
        seg_all = gather_relative(segments, "fsdp", size)
        w_cols = recut(size, full_inner, inner, me, w_in).T
        cot_all = gather_relative(own_cot, "fsdp", size).reshape(total, width)
    seg_all = seg_all.reshape(total // tokens, tokens)
    full_norm = small[:, :depth].reshape(1, width)
    full_cw = small[:, depth : depth + taps * own_conv].reshape(size, taps, own_conv)
    full_cw = full_cw.transpose(1, 0, 2).reshape(taps, conv_width)
    full_cb = small[:, depth + taps * own_conv : depth + (taps + 1) * own_conv].reshape(1, conv_width)

    def normalise(inputs):
        wide = inputs.astype(F32)
        return lax.rsqrt(jnp.mean(wide * wide, -1, keepdims=True) + EPS)

    if not fused:
        scaled_low = norm_rows(x_all, full_norm)
    projected = contract_cols(scaled_low, w_cols)

    conv_all = jnp.concatenate([full_cw, full_cb, jnp.zeros((7 - taps, conv_width), F32)], 0)
    conv_own = jnp.concatenate(
        [lax.dynamic_slice(conv_all, (0, me * inner), (8, inner)), conv_all[:, full_inner:]], 1
    )
    pad_heads = lambda row: jnp.pad(row.astype(F32), (0, LANES - local_heads))
    head_rows = jnp.stack([pad_heads(dt_bias), pad_heads(-jnp.exp(a_log.astype(F32)))])
    head_rows = jnp.pad(head_rows, ((0, 6), (0, 0)))
    chan_rows = jnp.stack([jnp.repeat(skip_gain.astype(F32), channel), gate_gain.astype(F32)])
    chan_rows = jnp.pad(chan_rows, ((0, 6), (0, 0)))
    same = []
    for offset in range(1, taps):
        equal = (seg_all[:, offset:] == seg_all[:, :-offset]).astype(F32)
        same.append(jnp.pad(equal, ((0, 0), (offset, 0))))
    same = jnp.pad(jnp.stack(same, 2), ((0, 0), (0, 0), (0, 9 - taps)))
    operands = (
        me.astype(jnp.int32).reshape(1), projected, seg_all[:, :, None], seg_all[:, None, :], same,
        head_rows, conv_own, chan_rows,
    )
    gated, squares, scan_out = mix_forward(dims, operands)
    if fused:
        cot_across, squares = lax.optimization_barrier((cot_across, squares))
        cot_all = jnp.concatenate([own_cot, cot_across, cot_beside, swap(cot_across, "fsdp", size, 1)], 0)
    twice = lambda row: jnp.stack([row, row])
    root = lax.rsqrt(sum_tokens(twice(squares[:, 0]), "fsdp", size)[0] / full_inner + EPS)
    normed_low = (gated.astype(F32) * root[:, None]).astype(BF16)
    w_later = w_out
    if fused:
        near = total // 2
        far_out = jnp.dot(gated[near:], w_out, preferred_element_type=F32).astype(BF16)
        normed_low, far_out = lax.optimization_barrier((normed_low, far_out))
        far_out = swap(far_out, "fsdp", size, 1)
        grad_out = contract_rows(normed_low, cot_all).astype(BF16)
        w_later, grad_out = lax.optimization_barrier((w_out, grad_out))
        own_out = lax.psum_scatter(grad_out, "replica", scatter_dimension=0, tiled=True)
    grad_normed = contract_cols(cot_all, w_later)
    cross = jnp.sum(gated.astype(F32) * grad_normed, 1)
    pull = root * root * root * sum_tokens(twice(cross), "fsdp", size)[0] / full_inner

    sequences = total // tokens
    stats = jnp.stack([root, pull], 1)
    if fused:
        early = sequences * 3 // 4
        gp_first, *small_first = mix_backward(dims, operands, stats, grad_normed, scan_out, 0, early)
        tok_out = jnp.dot(gated[:near], w_out, preferred_element_type=F32) + far_out.astype(F32)
        tok_out = tok_out.astype(BF16).reshape(2, own_rows, width)
        head_rows, own_out, small_first[2], tok_out = lax.optimization_barrier(
            (head_rows, own_out, small_first[2], tok_out)
        )
        grad_w_out = lax.all_gather(own_out, "replica", axis=0, tiled=True).astype(F32)
        operands = operands[:5] + (head_rows,) + operands[6:]
        gp_last, *small_last = mix_backward(
            dims, operands, stats, grad_normed, scan_out, early, sequences - early
        )
        grad_conv, grad_chan, grad_head = [first + last for first, last in zip(small_first, small_last)]
    else:
        gp, grad_conv, grad_chan, grad_head = mix_backward(
            dims, operands, stats, grad_normed, scan_out, 0, sequences
        )
    own_wide = own_x.astype(F32)
    own_root = normalise(own_x)

    conv_full = jnp.zeros((8, conv_width), F32)
    conv_full = lax.dynamic_update_slice(conv_full, grad_conv[:, inner:], (0, full_inner))
    conv_full = lax.dynamic_update_slice(conv_full, grad_conv[:, :inner], (0, me * inner))
    conv_full = conv_full[: taps + 1].reshape(-1)
    skip_grad = grad_chan[0].reshape(local_heads, channel).sum(1)
    own_small = jnp.concatenate(
        [grad_head[0, :local_heads], grad_head[1, :local_heads], skip_grad, grad_chan[1]]
    )

    if fused:
        spread = lax.dynamic_update_slice(jnp.zeros((size, own_small.shape[0]), F32), own_small[None], (me, 0))
        norm_row = -(-conv_full.shape[0] // LANES)
        conv_padded = jnp.pad(conv_full, (0, norm_row * LANES - conv_full.shape[0]))
        vector = jnp.concatenate([conv_padded, jnp.zeros((width,), F32), spread.reshape(-1)])
        vector = jnp.pad(vector, (0, -vector.shape[0] % (8 * LANES))).reshape(-1, LANES)
        sum_in, sum_shared, got_out, own_grad, got_grad, vector, _, _ = reduce_gradients(
            size, depth, inner, common, norm_row, gp_first, gp_last, scaled_low, w_cols, tok_out, vector
        )
        grad_w_in = jnp.concatenate([sum_in.reshape(2 * full_inner, depth), sum_shared], 0).astype(F32).T
        out_sum = tok_out[0].astype(F32) + got_out.astype(F32)
        grad_scaled = own_grad.astype(F32) + got_grad.astype(F32)
        vector = vector.reshape(-1)
        conv_full = vector[: conv_full.shape[0]]
        start = norm_row * LANES
        grad_norm = vector[start : start + width] / full_norm[0]
        start = start + width
        own_small = lax.dynamic_slice(vector, (start + me * own_small.shape[0],), own_small.shape)
    else:
        out_part = jnp.dot(gated, w_out, preferred_element_type=F32).astype(BF16)
        out_sum = scatter_relative(out_part.reshape(size, own_rows, width), "fsdp", size)
        grad_w_in, grad_w_out = small_pieces(
            size, copies, depth, inner, columns, me, replica, scaled_low, gp, normed_low, cot_all
        )
        scaled_part = jnp.dot(gp, w_cols, preferred_element_type=F32).astype(BF16)
        grad_scaled = scatter_relative(scaled_part.reshape(size, own_rows, width), "fsdp", size)
        grad_norm = jnp.sum(grad_scaled * own_wide * own_root, 0)
        conv_full, grad_norm = lax.psum((conv_full, grad_norm), ("replica", "fsdp"))
        own_small = lax.psum(own_small, "replica")

    block_out = (own_wide + root[:own_rows, None] * out_sum).astype(BF16).reshape(hidden_in.shape)
    gained = grad_scaled * full_norm
    inner_mean = jnp.mean(gained * own_wide, -1, keepdims=True)
    grad_in = own_cot.astype(F32) + own_root * gained - own_wide * (own_root * own_root * own_root * inner_mean)
    grad_in = grad_in.reshape(hidden_in.shape)
    conv_full = lax.dynamic_slice(conv_full.reshape(taps + 1, conv_width), (0, me * own_conv), (taps + 1, own_conv))
    grad_norm = lax.dynamic_slice(grad_norm, (me * depth,), (depth,))
    return (
        block_out,
        grad_in,
        grad_norm,
        grad_w_in,
        conv_full[:taps],
        conv_full[taps],
        own_small[:local_heads],
        own_small[local_heads : 2 * local_heads],
        own_small[2 * local_heads : 3 * local_heads],
        own_small[3 * local_heads :],
        grad_w_out,
    )


def solution(mesh):
    rows = ("replica", "fsdp")
    placed = (
        P(None, rows, None, None),
        P(None, rows, None),
        P(None, rows, None, None),
        P("fsdp"),
        P("fsdp", None),
        P(None, "fsdp"),
        P("fsdp"),
        P("fsdp"),
        P("fsdp"),
        P("fsdp"),
        P("fsdp"),
        P("fsdp", None),
    )
    return jax.shard_map(
        functools.partial(on_device, mesh.shape["replica"], mesh.shape["fsdp"]),
        mesh=mesh,
        in_specs=placed,
        out_specs=(
            P(None, rows, None, None),
            P(None, rows, None, None),
            P("fsdp"),
            P("fsdp", None),
            P(None, "fsdp"),
            P("fsdp"),
            P("fsdp"),
            P("fsdp"),
            P("fsdp"),
            P("fsdp"),
            P("fsdp", None),
        ),
        check_vma=False,
    )
```

```python
import functools

import jax
import jax.numpy as jnp
from jax import lax
from jax.experimental import pallas as pl
from jax.experimental.pallas import tpu as pltpu
from jax.sharding import PartitionSpec as P

EPS = 1e-05
HIGHEST = lax.Precision.HIGHEST
LANES = 128
F32 = jnp.float32
BF16 = jnp.bfloat16
LOG2E = 1.4426950408889634
VMEM_LIMIT = 60 << 20


def contract_rows(left, right, precision=None):
    return lax.dot_general(
        left, right, (((0,), (0,)), ((), ())), precision=precision, preferred_element_type=F32
    )


def contract_cols(left, right, precision=None):
    return lax.dot_general(
        left, right, (((1,), (1,)), ((), ())), precision=precision, preferred_element_type=F32
    )


def sigmoid(v):
    return 0.5 * jnp.tanh(0.5 * v) + 0.5


def convolve(conv_input, taps, bias, mask_refs):
    total = bias + taps[0] * conv_input
    shifted = []
    for offset in range(1, len(taps)):
        prior = pltpu.roll(conv_input, offset, 0) * mask_refs[offset - 1]
        shifted.append(prior)
        total = total + taps[offset] * prior
    return total, shifted


def prepare(dims, own_ref, proj_ref, seg_row_ref, mask_ref, head_ref, cw_ref,
            mask_wide, visible_bias, step_wide, cum_wide, cum_rows, state_act, affinity):
    tokens, inner, state2, heads, local_heads, taps = dims
    for offset in range(taps - 1):
        mask_wide[offset] = jnp.broadcast_to(mask_ref[:, offset : offset + 1], (tokens, LANES))
    rows = lax.broadcasted_iota(jnp.int32, (tokens, tokens), 0)
    cols = lax.broadcasted_iota(jnp.int32, (tokens, tokens), 1)
    visible = (rows >= cols) & (mask_ref[:, taps - 1 : taps] == seg_row_ref[...])
    visible_bias[...] = jnp.where(visible, 0.0, -1e30)
    common = 2 * inner
    raw = proj_ref[:, common + state2 : common + state2 + heads]
    raw = jnp.concatenate([raw, jnp.zeros((tokens, LANES - heads), F32)], 1)
    raw = pltpu.roll(raw, LANES - own_ref[0] * local_heads, 1)
    raw = raw + head_ref[0:1, :]
    step = jnp.maximum(raw, 0.0) + jnp.log1p(jnp.exp(-jnp.abs(raw)))
    log_decay = head_ref[1:2, :] * step
    lower = jnp.where(rows >= cols, 1.0, 0.0).astype(F32)
    cumulative = jnp.dot(lower, log_decay, precision=HIGHEST, preferred_element_type=F32)
    scaled_cum = cumulative * LOG2E
    flipped = scaled_cum.T
    lane = lax.broadcasted_iota(jnp.int32, (tokens, LANES), 1)
    for head in range(local_heads):
        cum_wide[head] = jnp.broadcast_to(scaled_cum[:, head : head + 1], (tokens, LANES))
        cum_rows[head] = flipped[head : head + 1, :]
    for pair in range(local_heads // 2):
        step_wide[pair] = jnp.where(
            lane < LANES // 2, step[:, 2 * pair : 2 * pair + 1], step[:, 2 * pair + 1 : 2 * pair + 2]
        )
    for part in range(state2 // LANES):
        at = inner + part * LANES
        conv, _ = convolve(
            proj_ref[:, common + part * LANES : common + (part + 1) * LANES],
            [cw_ref[j : j + 1, at : at + LANES] for j in range(taps)],
            cw_ref[taps : taps + 1, at : at + LANES],
            mask_wide,
        )
        state_act[part] = conv * sigmoid(conv)
    affinity[...] = contract_cols(state_act[1], state_act[0], HIGHEST)
    return raw, step, log_decay, rows, cols


def over_pairs(count, step, carry):
    group = 4 if count % 4 == 0 else 2

    def turn(index, carried):
        for inner in range(group):
            carried = step(index * group + inner, carried)
        return carried

    return lax.fori_loop(0, count // group, turn, carry)


def forward_kernel(dims, own_ref, proj_ref, seg_row_ref, mask_ref, head_ref, cw_ref, chan_ref,
                   gated_ref, square_ref, out_ref,
                   mask_wide, visible_bias, step_wide, cum_wide, cum_rows, state_act, affinity):
    tokens, inner, state2, heads, local_heads, taps = dims
    prepare(dims, own_ref, proj_ref, seg_row_ref, mask_ref, head_ref, cw_ref,
            mask_wide, visible_bias, step_wide, cum_wide, cum_rows, state_act, affinity)
    lane = lax.broadcasted_iota(jnp.int32, (tokens, LANES), 1)
    first = lane < LANES // 2
    blocks = tokens // LANES

    def pair_step(pair, squares):
        here = pl.ds(pl.multiple_of(pair * LANES, LANES), LANES)
        conv, _ = convolve(
            proj_ref[:, here], [cw_ref[j : j + 1, here] for j in range(taps)],
            cw_ref[taps : taps + 1, here], mask_wide,
        )
        values = conv * sigmoid(conv)
        weighted = values * step_wide[pair]
        out = chan_ref[0:1, here] * values
        parts = [out[b * LANES : (b + 1) * LANES] for b in range(blocks)]
        for which in range(2):
            head = 2 * pair + which
            mine = jnp.where(first == (which == 0), weighted, 0.0).astype(BF16)
            for tb in range(blocks):
                t_rows = slice(tb * LANES, (tb + 1) * LANES)
                pieces = []
                for sb in range(tb + 1):
                    s_cols = slice(sb * LANES, (sb + 1) * LANES)
                    distance = (cum_wide[head, t_rows, :] - cum_rows[head, :, s_cols]) + visible_bias[t_rows, s_cols]
                    pieces.append((affinity[t_rows, s_cols] * jnp.exp2(distance)).astype(BF16))
                weights = jnp.concatenate(pieces, 1) if tb > 0 else pieces[0]
                parts[tb] = parts[tb] + jnp.dot(
                    weights, mine[: (tb + 1) * LANES], preferred_element_type=F32
                )
        out = jnp.concatenate(parts, 0)
        out_ref[:, here] = out.astype(BF16)
        gate = proj_ref[:, pl.ds(pl.multiple_of(inner + pair * LANES, LANES), LANES)]
        gated = out * (gate * sigmoid(gate))
        gated_ref[:, here] = (gated * chan_ref[1:2, here]).astype(BF16)
        return squares + gated * gated

    squares = over_pairs(local_heads // 2, pair_step, jnp.zeros((tokens, LANES), F32))
    square_ref[...] = jnp.sum(squares, 1, keepdims=True)


def backward_kernel(dims, own_ref, proj_ref, seg_row_ref, mask_ref, head_ref, cw_ref, chan_ref,
                    stats_ref, gn_ref, out_ref,
                    gp_ref, grad_cw_ref, grad_chan_ref, grad_head_ref,
                    mask_wide, visible_bias, step_wide, cum_wide, cum_rows, state_act, affinity,
                    grad_affinity, row_sums, col_sums, wide_stats):
    tokens, inner, state2, heads, local_heads, taps = dims

    @pl.when(pl.program_id(0) == 0)
    def _():
        grad_cw_ref[...] = jnp.zeros_like(grad_cw_ref)
        grad_chan_ref[...] = jnp.zeros_like(grad_chan_ref)
        grad_head_ref[...] = jnp.zeros_like(grad_head_ref)

    raw, step, log_decay, rows, cols = prepare(
        dims, own_ref, proj_ref, seg_row_ref, mask_ref, head_ref, cw_ref,
        mask_wide, visible_bias, step_wide, cum_wide, cum_rows, state_act, affinity)
    grad_affinity[...] = jnp.zeros_like(grad_affinity)
    row_sums[...] = jnp.zeros_like(row_sums)
    col_sums[...] = jnp.zeros_like(col_sums)
    wide_stats[0] = jnp.broadcast_to(stats_ref[:, 0:1], (tokens, LANES))
    wide_stats[1] = jnp.broadcast_to(stats_ref[:, 1:2], (tokens, LANES))
    lane = lax.broadcasted_iota(jnp.int32, (tokens, LANES), 1)
    block_lane = lax.broadcasted_iota(jnp.int32, (LANES, LANES), 1)
    first = lane < LANES // 2
    blocks = tokens // LANES

    def conv_back(grad_conv, shifted, conv_input, here):
        grad_cw_ref[0:1, here] += jnp.sum(grad_conv * conv_input, 0, keepdims=True)
        grad_cw_ref[taps : taps + 1, here] += jnp.sum(grad_conv, 0, keepdims=True)
        back = cw_ref[0:1, here] * grad_conv
        for offset in range(1, taps):
            grad_cw_ref[offset : offset + 1, here] += jnp.sum(grad_conv * shifted[offset - 1], 0, keepdims=True)
            term = (cw_ref[offset : offset + 1, here] * grad_conv) * mask_wide[offset - 1]
            back = back + pltpu.roll(term, tokens - offset, 0)
        return back

    def pair_step(pair, carry):
        here = pl.ds(pl.multiple_of(pair * LANES, LANES), LANES)
        there = pl.ds(pl.multiple_of(inner + pair * LANES, LANES), LANES)
        conv_input = proj_ref[:, here]
        conv, shifted = convolve(
            conv_input, [cw_ref[j : j + 1, here] for j in range(taps)],
            cw_ref[taps : taps + 1, here], mask_wide,
        )
        conv_sig = sigmoid(conv)
        values = conv * conv_sig
        weighted = values * step_wide[pair]
        skip = chan_ref[0:1, here]
        halves = [jnp.where(first == (which == 0), weighted, 0.0).astype(BF16) for which in range(2)]
        out = out_ref[:, here].astype(F32)
        gate = proj_ref[:, there]
        gate_sig = sigmoid(gate)
        gate_silu = gate * gate_sig
        gated = out * gate_silu
        gn = gn_ref[:, here]
        gain = chan_ref[1:2, here]
        root = wide_stats[0]
        grad_chan_ref[1:2, here] += jnp.sum(gn * gated * root, 0, keepdims=True)
        grad_gated = root * (gn * gain) - gated * wide_stats[1]
        grad_out = grad_gated * gate_silu
        gp_ref[:, there] = (grad_gated * out * (gate_sig * (1.0 + gate * (1.0 - gate_sig)))).astype(BF16)
        grad_chan_ref[0:1, here] += jnp.sum(grad_out * values, 0, keepdims=True)
        back_parts = [jnp.zeros((LANES, LANES), F32) for _ in range(blocks)]
        for which in range(2):
            head = 2 * pair + which
            mine = jnp.where(first == (which == 0), grad_out, 0.0).astype(BF16)
            for tb in range(blocks):
                t_rows = slice(tb * LANES, (tb + 1) * LANES)
                sums = None
                for sb in range(tb + 1):
                    s_cols = slice(sb * LANES, (sb + 1) * LANES)
                    distance = (cum_wide[head, t_rows, :] - cum_rows[head, :, s_cols]) + visible_bias[t_rows, s_cols]
                    decay = jnp.exp2(distance)
                    weights = affinity[t_rows, s_cols] * decay
                    cross = contract_cols(mine[t_rows], halves[which][s_cols])
                    grad_affinity[t_rows, s_cols] += cross * decay
                    energy = cross * weights
                    col_sums[head, :, s_cols] += jnp.sum(energy, 0, keepdims=True)
                    sums = energy if sums is None else sums + energy
                    back_parts[sb] = back_parts[sb] + contract_rows(weights.astype(BF16), mine[t_rows])
                row_sums[t_rows, :] += jnp.where(
                    block_lane == head, jnp.sum(sums, 1, keepdims=True), 0.0
                )
        grad_values = jnp.concatenate(back_parts, 0) * step_wide[pair] + skip * grad_out
        grad_conv = grad_values * (conv_sig * (1.0 + conv * (1.0 - conv_sig)))
        gp_ref[:, here] = conv_back(grad_conv, shifted, conv_input, here).astype(BF16)
        return carry

    over_pairs(local_heads // 2, pair_step, 0)

    common = 2 * inner
    grad_states = [
        contract_rows(grad_affinity[...], state_act[1], HIGHEST),
        jnp.dot(grad_affinity[...], state_act[0], precision=HIGHEST, preferred_element_type=F32),
    ]
    for part in range(state2 // LANES):
        at = slice(inner + part * LANES, inner + (part + 1) * LANES)
        spot = slice(common + part * LANES, common + (part + 1) * LANES)
        conv_input = proj_ref[:, spot]
        conv, shifted = convolve(
            conv_input, [cw_ref[j : j + 1, at] for j in range(taps)], cw_ref[taps : taps + 1, at], mask_wide
        )
        conv_sig = sigmoid(conv)
        grad_conv = grad_states[part] * (conv_sig * (1.0 + conv * (1.0 - conv_sig)))
        gp_ref[:, spot] = conv_back(grad_conv, shifted, conv_input, at).astype(BF16)

    col_rows = [col_sums[head] for head in range(local_heads)]
    col_rows.append(jnp.zeros((LANES - local_heads, tokens), F32))
    col_energy = jnp.concatenate(col_rows, 0).T
    upper = jnp.where(cols >= rows, 1.0, 0.0).astype(F32)
    grad_decay = jnp.dot(upper, row_sums[...] - col_energy, precision=HIGHEST, preferred_element_type=F32)
    step_sig = sigmoid(raw)
    ratio = jnp.where(raw < -20.0, 1.0, step_sig / jnp.maximum(step, 1e-30))
    grad_raw = col_energy * ratio + (head_ref[1:2, :] * grad_decay) * step_sig
    grad_head_ref[0:1, :] += jnp.sum(grad_raw, 0, keepdims=True)
    grad_head_ref[1:2, :] += jnp.sum(grad_decay * log_decay, 0, keepdims=True)
    placed = pltpu.roll(grad_raw, own_ref[0] * local_heads, 1)
    gp_ref[:, common + state2 : common + state2 + heads] = placed[:, :heads].astype(BF16)


def mixer_specs(dims, width, start=0):
    tokens, inner, state2, heads, local_heads, taps = dims
    fixed = lambda shape: pl.BlockSpec(shape, lambda s: (0,) * len(shape))
    in_specs = [
        pl.BlockSpec(memory_space=pltpu.SMEM),
        pl.BlockSpec((tokens, width), lambda s: (s + start, 0)),
        pl.BlockSpec((None, 1, tokens), lambda s: (s + start, 0, 0)),
        pl.BlockSpec((None, tokens, 8), lambda s: (s + start, 0, 0)),
        fixed((8, LANES)),
        fixed((8, inner + state2)),
        fixed((8, inner)),
    ]
    scratch = [
        pltpu.VMEM((taps - 1, tokens, LANES), F32),
        pltpu.VMEM((tokens, tokens), F32),
        pltpu.VMEM((local_heads // 2, tokens, LANES), F32),
        pltpu.VMEM((local_heads, tokens, LANES), F32),
        pltpu.VMEM((local_heads, 1, tokens), F32),
        pltpu.VMEM((state2 // LANES, tokens, LANES), F32),
        pltpu.VMEM((tokens, tokens), F32),
    ]
    return in_specs, scratch


def mix_forward(dims, operands):
    tokens, inner, state2, heads, local_heads, taps = dims
    total, width = operands[1].shape
    in_specs, scratch = mixer_specs(dims, width)
    return pl.pallas_call(
        functools.partial(forward_kernel, dims),
        grid=(total // tokens,),
        in_specs=in_specs,
        out_specs=[
            pl.BlockSpec((tokens, inner), lambda s: (s, 0)),
            pl.BlockSpec((tokens, 1), lambda s: (s, 0)),
            pl.BlockSpec((tokens, inner), lambda s: (s, 0)),
        ],
        out_shape=[
            jax.ShapeDtypeStruct((total, inner), BF16),
            jax.ShapeDtypeStruct((total, 1), F32),
            jax.ShapeDtypeStruct((total, inner), BF16),
        ],
        scratch_shapes=scratch,
        compiler_params=pltpu.CompilerParams(vmem_limit_bytes=VMEM_LIMIT),
        cost_estimate=pl.CostEstimate(
            flops=total * local_heads * tokens * 4 * 64,
            bytes_accessed=total * width * 4,
            transcendentals=total * local_heads * tokens,
        ),
        name="mix_forward",
    )(*operands)


def mix_backward(dims, operands, stats, grad_normed, scan_out, start, count):
    tokens, inner, state2, heads, local_heads, taps = dims
    total, width = count * tokens, operands[1].shape[1]
    in_specs, scratch = mixer_specs(dims, width, start)
    fixed = lambda shape: pl.BlockSpec(shape, lambda s: (0,) * len(shape))
    return pl.pallas_call(
        functools.partial(backward_kernel, dims),
        grid=(count,),
        in_specs=in_specs + [
            pl.BlockSpec((tokens, 2), lambda s: (s + start, 0)),
            pl.BlockSpec((tokens, inner), lambda s: (s + start, 0)),
            pl.BlockSpec((tokens, inner), lambda s: (s + start, 0)),
        ],
        out_specs=[
            pl.BlockSpec((tokens, width), lambda s: (s, 0)),
            fixed((8, inner + state2)),
            fixed((8, inner)),
            fixed((8, LANES)),
        ],
        out_shape=[
            jax.ShapeDtypeStruct((total, width), BF16),
            jax.ShapeDtypeStruct((8, inner + state2), F32),
            jax.ShapeDtypeStruct((8, inner), F32),
            jax.ShapeDtypeStruct((8, LANES), F32),
        ],
        scratch_shapes=scratch + [
            pltpu.VMEM((tokens, tokens), F32),
            pltpu.VMEM((tokens, LANES), F32),
            pltpu.VMEM((local_heads, 1, tokens), F32),
            pltpu.VMEM((2, tokens, LANES), F32),
        ],
        compiler_params=pltpu.CompilerParams(vmem_limit_bytes=VMEM_LIMIT),
        cost_estimate=pl.CostEstimate(
            flops=total * local_heads * tokens * 12 * 64,
            bytes_accessed=total * width * 6,
            transcendentals=2 * total * local_heads * tokens,
        ),
        name="mix_backward",
    )(*operands, stats, grad_normed, scan_out)


def norm_kernel(x_ref, gain_ref, scaled_ref):
    wide = x_ref[...].astype(F32)
    root = lax.rsqrt(jnp.mean(wide * wide, 1, keepdims=True) + EPS)
    scaled_ref[...] = (wide * root * gain_ref[...]).astype(BF16)


def norm_rows(inputs, gain):
    rows, width = inputs.shape
    block = pl.BlockSpec((256, width), lambda s: (s, 0))
    return pl.pallas_call(
        norm_kernel,
        grid=(rows // 256,),
        in_specs=[block, pl.BlockSpec((1, width), lambda s: (0, 0))],
        out_specs=block,
        out_shape=jax.ShapeDtypeStruct(inputs.shape, BF16),
        compiler_params=pltpu.CompilerParams(vmem_limit_bytes=VMEM_LIMIT),
        cost_estimate=pl.CostEstimate(flops=4 * rows * width, bytes_accessed=4 * rows * width, transcendentals=rows),
        name="norm_rows",
    )(inputs, gain)


def swap(array, axis, size, bit):
    return lax.ppermute(array, axis, [(i, i ^ bit) for i in range(size)])


def axis_bits(size):
    bits = []
    bit = 1
    while bit < size:
        bits.append(bit)
        bit *= 2
    return bits


def gather_relative(array, axis, size):
    held = array[None]
    for bit in reversed(axis_bits(size)):
        held = jnp.concatenate([held, swap(held, axis, size, bit)], 0)
    return held


def scatter_relative(array, axis, size):
    total = array
    for bit in axis_bits(size):
        half = total.shape[0] // 2
        received = swap(total[half:].astype(BF16), axis, size, bit)
        total = total[:half].astype(F32) + received.astype(F32)
    return total[0]


def sum_tokens(array, axis, size):
    kinds, tokens = array.shape
    for bit in axis_bits(size):
        stride = tokens // (2 * bit)
        received = swap(array, axis, size, bit).reshape(kinds, bit, 2, stride)
        array = array + received[:, :, ::-1].reshape(kinds, tokens)
    return array


def halve_sum(array, order, replica, size):
    total = array
    for bit in order:
        blocks, rows, columns = total.shape
        mine = (replica // bit) % 2
        halves = total.reshape(blocks, 2, rows // 2, columns)
        kept = lax.dynamic_index_in_dim(halves, mine, 1, keepdims=False)
        sent = lax.dynamic_index_in_dim(halves, 1 - mine, 1, keepdims=False)
        received = swap(sent.astype(BF16), "replica", size, bit)
        total = kept + received.astype(F32)
    return total


def double_gather(array, order, replica, size):
    held = array
    for bit in reversed(order):
        received = swap(held, "replica", size, bit)
        upper = (replica // bit) % 2 == 1
        held = jnp.where(
            upper,
            jnp.concatenate([received, held], 1),
            jnp.concatenate([held, received], 1),
        )
    return held


def flip(index, bit):
    return index + bit * (1 - 2 * ((index // bit) % 2))


MESH = pl.DeviceIdType.MESH


def greet(peers):
    barrier = pltpu.get_barrier_semaphore()
    for peer in peers:
        pl.semaphore_signal(barrier, inc=1, device_id=peer, device_id_type=MESH)
    pl.semaphore_wait(barrier, len(peers))


def copy_peers(me):
    return [flip(me, 1), flip(me, 2), flip(flip(me, 1), 2)]


def gather_kernel(full_inner, inner, x_ref, seg_ref, small_ref, w_ref,
                  scaled_ref, seg_all_ref, small_all_ref, cols_ref,
                  x_all_ref, scaled, gain, cols_held, send_sems, recv_sems, local_sems, store_sems, norm_sems):
    me = lax.axis_index("fsdp")
    replica = lax.axis_index("replica")
    depth, common = w_ref.shape[1], w_ref.shape[0] - 2 * full_inner
    peers = [(replica, peer) for peer in copy_peers(me)]
    beside, above = (flip(replica, 1), me), (flip(replica, 2), me)
    greet(peers + [beside, above])
    number = [0]
    started = []

    def send(from_ref, to_ref, device):
        slot = number[0]
        number[0] += 1
        copy = pltpu.make_async_remote_copy(
            src_ref=from_ref, dst_ref=to_ref, send_sem=send_sems.at[slot], recv_sem=recv_sems.at[slot],
            device_id=device, device_id_type=MESH,
        )
        copy.start()
        started.append(copy)
        return copy

    parts = [(0, inner), (inner, inner), (2 * inner, common)]

    def targets(owner, first, count):
        lanes = pl.ds(pl.multiple_of(owner * depth, depth), depth)
        return [
            cols_ref.at[pl.ds(pl.multiple_of(base + first * (length // 4), 16), count * (length // 4)), lanes]
            for base, length in parts
        ]

    def sources(device, first, count):
        bases = [full_inner + device * inner, device * inner, 2 * full_inner]
        return [
            w_ref.at[pl.ds(pl.multiple_of(base + first * (length // 4), 16), count * (length // 4))]
            for base, (_, length) in zip(bases, parts)
        ]

    def send_parts(from_refs, to_refs, device):
        return [send(source, target, device) for source, target in zip(from_refs, to_refs)]

    spot = replica % 4
    smalls = [send(small_ref, small_all_ref.at[me], peer) for peer in peers]
    smalls += [send(seg_ref, seg_all_ref.at[slot], peer) for peer, slot in zip(peers, (2, 1, 3))]
    across = [send_parts(sources(peers[which][1], spot, 1), targets(me, spot, 1), peers[which]) for which in (1, 2)]
    x_y = send(x_ref, x_all_ref.at[1], peers[1])
    near = send_parts(sources(peers[0][1], 0, 4), targets(me, 0, 4), peers[0])
    x_near = send(x_ref, x_all_ref.at[2], peers[0])
    held = [cols_held.at[pl.ds(base, length)] for base, length in parts]
    own = list(zip(sources(me, 0, 4), held, targets(me, 0, 4)))
    loads = [pltpu.make_async_copy(source, held, local_sems.at[i]) for i, (source, held, _) in enumerate(own)]
    stores = [pltpu.make_async_copy(held, target, store_sems.at[i]) for i, (_, held, target) in enumerate(own)]
    x_own = pltpu.make_async_copy(x_ref, x_all_ref.at[0], local_sems.at[3])
    small_own = pltpu.make_async_copy(small_ref, small_all_ref.at[me], local_sems.at[4])
    stores.append(pltpu.make_async_copy(seg_ref, seg_all_ref.at[0], local_sems.at[5]))
    for copy in loads + [x_own, small_own, stores[-1]]:
        copy.start()
    for load, store in zip(loads, stores):
        load.wait()
        store.start()

    rows_at_once = 128
    block_rows, width = scaled.shape[1:]
    tiles_of_owner = depth // LANES

    def normalise(block):
        def step(piece, carry):
            rows = pl.ds(pl.multiple_of(piece * rows_at_once, rows_at_once), rows_at_once)
            wide = x_all_ref[block, rows, :].astype(F32)
            root = lax.rsqrt(jnp.mean(wide * wide, 1, keepdims=True) + EPS)
            scaled[block, rows, :] = (wide * root * gain[...]).astype(BF16)
            return carry

        lax.fori_loop(0, block_rows // rows_at_once, step, 0)
        store = pltpu.make_async_copy(
            scaled.at[block], scaled_ref.at[pl.ds(block * block_rows, block_rows)], norm_sems.at[block]
        )
        store.start()
        stores.append(store)

    small_own.wait()
    for copy in smalls:
        copy.wait_recv()
    for tile in range(width // LANES):
        gain[:, tile * LANES : (tile + 1) * LANES] = small_all_ref[
            tile // tiles_of_owner, tile % tiles_of_owner : tile % tiles_of_owner + 1, :
        ]
    x_own.wait()
    normalise(0)

    def relay(which, first, count, device):
        refs = targets(peers[which][1], first, count)
        return send_parts(refs, refs, device)

    for copy in across[0]:
        copy.wait_recv()
    first_beside = relay(1, spot, 1, beside)
    for copy in across[1]:
        copy.wait_recv()
    first_above = relay(2, spot, 1, above)
    for copy in first_beside:
        copy.wait_recv()
    last = relay(1, (spot // 2) * 2, 2, above)
    for copy in first_above:
        copy.wait_recv()
    last += relay(2, spot, 1, beside)
    last += relay(2, flip(spot, 2), 1, beside)
    x_near.wait_recv()
    normalise(2)
    x_y.wait_recv()
    x_last = send(x_all_ref.at[1], x_all_ref.at[3], peers[0])
    normalise(1)
    x_last.wait_recv()
    normalise(3)
    for copy in last + near:
        copy.wait_recv()
    for copy in stores:
        copy.wait()
    for copy in started:
        copy.wait_send()


GATHER_COPIES = 34


def gather_inputs(size, inner, x, segments, small, w_flipped):
    full, depth = w_flipped.shape
    full_inner = inner * size
    columns = 2 * inner + full - 2 * full_inner
    anywhere = pl.BlockSpec(memory_space=pltpu.HBM)
    return pl.pallas_call(
        functools.partial(gather_kernel, full_inner, inner),
        in_specs=[anywhere] * 4,
        out_specs=[anywhere] * 2 + [pl.BlockSpec(memory_space=pltpu.VMEM), anywhere],
        out_shape=[
            jax.ShapeDtypeStruct((size * x.shape[0], x.shape[1]), BF16),
            jax.ShapeDtypeStruct((size,) + segments.shape, jnp.int32),
            jax.ShapeDtypeStruct((size,) + small.shape, F32),
            jax.ShapeDtypeStruct((columns, size * depth), BF16),
        ],
        scratch_shapes=[
            pltpu.VMEM((size,) + x.shape, BF16),
            pltpu.VMEM((size,) + x.shape, BF16),
            pltpu.VMEM((1, x.shape[1]), F32),
            pltpu.VMEM((columns, depth), BF16),
            pltpu.SemaphoreType.DMA((GATHER_COPIES,)),
            pltpu.SemaphoreType.DMA((GATHER_COPIES,)),
            pltpu.SemaphoreType.DMA((6,)),
            pltpu.SemaphoreType.DMA((3,)),
            pltpu.SemaphoreType.DMA((4,)),
        ],
        compiler_params=pltpu.CompilerParams(
            collective_id=1, has_side_effects=True, vmem_limit_bytes=VMEM_LIMIT
        ),
        cost_estimate=pl.CostEstimate(flops=0, bytes_accessed=200 << 20, transcendentals=0),
        name="gather_inputs",
    )(x, segments, small, w_flipped)


PARTS = {
    "side": {"got": 2, "lift": 2, "sent": 4, "swapped": 4, "final": 4},
    "lift": {"got": 1, "sent": 2, "swapped": 2, "sent_side": 4, "got_side": 4, "final": 4},
}
SLOTS = 9
IN_ROWS = (64,) * 32
SHARED_AT = 4
COLUMN_BLOCK = 256
ROW_BLOCK = 256
LANE_TILE = 1024
PER_TURN = 3
AGAIN = 1
TOKEN_PIECES = 8


def reduce_chunks(inner, common):
    pieces = []
    start = 0
    for rows in IN_ROWS:
        pieces.append(("in", start, rows))
        start += rows
    pieces.insert(SHARED_AT, ("shared", 0, common))
    counts = {}
    placed = []
    for number, (kind, start, rows) in enumerate(pieces):
        order = "lift" if number % 3 == 2 else "side"
        key = (kind == "shared", rows, order)
        where = counts.get(key, 0)
        counts[key] = where + 1
        placed.append((kind, start, rows, order, where))
    return placed, counts


def reduce_kernel(plan, gp_first_ref, gp_last_ref, scaled_ref, cols_ref, tok_out_ref, small_ref,
                  sum_in_ref, sum_shared_ref, got_out_ref, own_grad_ref, got_grad_ref, small_sum_ref,
                  far_land_ref, across_ref, *scratch):
    chunks, counts, inner, depth, common, norm_row = plan
    groups = {}
    position = 0
    for key in counts:
        names = list(PARTS[key[2]])
        groups[key] = dict(zip(names, scratch[position : position + len(names)]))
        position += len(names)
    (shared_in, shared_sum, small_got, scaled, cols, grads, gp_cols, gp_flipped, gp_rows, tiles, far_tile, norm_sum,
     send_sems, recv_sems, local_sems, tok_send, tok_recv,
     small_send, small_recv, shared_send, shared_recv, far_send, far_recv, load_sems, store_sems) = scratch[position:]
    whole_loads = [
        pltpu.make_async_copy(scaled_ref, scaled, load_sems.at[0]),
        pltpu.make_async_copy(cols_ref, cols, load_sems.at[1]),
    ]
    for copy in whole_loads:
        copy.start()
    loaded = [False, False]

    def need(which):
        if not loaded[which]:
            whole_loads[which].wait()
            loaded[which] = True

    column_blocks = [(start, COLUMN_BLOCK) for start in range(0, 2 * inner, COLUMN_BLOCK)]
    column_blocks.insert(1, (2 * inner, common))
    width = scaled.shape[1]
    rows_of_block = tiles.shape[1]
    lane_tiles = width // LANE_TILE
    column_loads = []
    columns_done = []

    first_rows = gp_first_ref.shape[0]
    all_rows = first_rows + gp_last_ref.shape[0]

    def load_columns(number):
        if number < len(column_blocks):
            start, count = column_blocks[number]
            lanes = pl.ds(0, count)
            copies = [
                pltpu.make_async_copy(
                    gp_first_ref.at[:, pl.ds(start, count)], gp_cols.at[pl.ds(0, first_rows), lanes], load_sems.at[2]
                ),
                pltpu.make_async_copy(
                    gp_last_ref.at[:, pl.ds(start, count)],
                    gp_cols.at[pl.ds(first_rows, all_rows - first_rows), lanes], load_sems.at[5],
                ),
            ]
            for copy in copies:
                copy.start()
            column_loads.append(copies)

    def next_columns():
        number = len(columns_done)
        if number == len(column_blocks):
            return
        start, count = column_blocks[number]
        need(0)
        for copy in column_loads[number]:
            copy.wait()
        gp_flipped[pl.ds(0, count), :] = gp_cols[:, pl.ds(0, count)].T
        load_columns(number + 1)

        def lanes_step(tile, carry):
            lanes = pl.ds(pl.multiple_of(tile * LANE_TILE, LANE_TILE), LANE_TILE)
            grads[pl.ds(start, count), lanes] = jnp.dot(
                gp_flipped[pl.ds(0, count), :], scaled[:, lanes], preferred_element_type=F32
            ).astype(BF16)
            return carry

        lax.fori_loop(0, lane_tiles, lanes_step, 0)
        columns_done.append(start)

    def ensure_columns(start):
        while start not in columns_done:
            next_columns()

    load_columns(0)
    me = lax.axis_index("fsdp")
    replica = lax.axis_index("replica")
    up = replica // 2
    inside = (up == 1) | (up == 2)
    outside = (up == 0) | (up == 3)
    half = up // 2
    aside = replica % 2
    beside = (flip(replica, 1), me)
    partner = (flip(replica, 2), me)
    middle = (flip(flip(replica, 2), 4), me)
    peers = [(replica, peer) for peer in copy_peers(me)]
    greet(peers + [beside, partner, middle])

    def remote(from_ref, to_ref, device, sends, recvs):
        return pltpu.make_async_remote_copy(
            src_ref=from_ref, dst_ref=to_ref, send_sem=sends, recv_sem=recvs, device_id=device, device_id_type=MESH
        )

    def lanes_of(device):
        return pl.ds(pl.multiple_of(device * depth, depth), depth)

    def activations():
        rows = got_out_ref.shape[0] // TOKEN_PIECES
        copies = []
        for piece in range(TOKEN_PIECES):
            at = pl.ds(piece * rows, rows)
            copy = remote(tok_out_ref.at[1, at], got_out_ref.at[at], peers[1], tok_send.at[0, piece], tok_recv.at[0, piece])
            copy.start()
            copies.append(copy)
            yield
        for piece in range(TOKEN_PIECES):
            at = pl.ds(piece * rows, rows)
            copy = remote(across_ref.at[at], got_grad_ref.at[at], peers[1], tok_send.at[1, piece], tok_recv.at[1, piece])
            copy.start()
            copies.append(copy)
            yield
        for copy in copies:
            copy.wait()

    def row_products():
        half_blocks = all_rows // (2 * rows_of_block)
        quarter_blocks = half_blocks // 2
        later = list(range(quarter_blocks, half_blocks))
        sooner = list(range(quarter_blocks))
        order = [(True, i) for i in later] + [(False, i) for i in later]
        order += [(True, i) for i in sooner] + [(False, i) for i in sooner]
        norm_sum[...] = jnp.zeros_like(norm_sum)
        row_loads = []

        def load_rows(number):
            if number < len(order):
                far, block = order[number]
                at = (half_blocks + block if far else block) * rows_of_block
                if at < first_rows:
                    source = gp_first_ref.at[pl.ds(at, rows_of_block)]
                else:
                    source = gp_last_ref.at[pl.ds(at - first_rows, rows_of_block)]
                copy = pltpu.make_async_copy(source, gp_rows, load_sems.at[3])
                copy.start()
                row_loads.append((copy, at))

        load_rows(0)
        need(0)
        need(1)
        arrivals = {}
        busy = [None, None]
        for number, (far, block) in enumerate(order):
            slot = number % 2
            if busy[slot] is not None:
                busy[slot]()
            if not far:
                arrivals[block].wait_recv()
                load = pltpu.make_async_copy(far_land_ref.at[block], far_tile, load_sems.at[4])
                load.start()
                load.wait()
            copy, at = row_loads[number]
            copy.wait()

            def lanes_step(tile, carry):
                lanes = pl.ds(pl.multiple_of(tile * LANE_TILE, LANE_TILE), LANE_TILE)
                part = jnp.dot(gp_rows[...], cols[:, lanes], preferred_element_type=F32)
                norm_sum[:, lanes] += jnp.sum(
                    part * scaled[pl.ds(at, rows_of_block), lanes].astype(F32), 0, keepdims=True
                )
                if not far:
                    part = part + far_tile[:, lanes].astype(F32)
                tiles[slot, :, lanes] = part.astype(BF16)
                return carry

            lax.fori_loop(0, lane_tiles, lanes_step, 0)
            load_rows(number + 1)
            if far:
                sent = remote(tiles.at[slot], far_land_ref.at[block], peers[0], far_send.at[block], far_recv.at[block])
                sent.start()
                arrivals[block] = sent
                busy[slot] = sent.wait_send
            else:
                target = own_grad_ref if block < quarter_blocks else across_ref
                place = pl.ds((block % quarter_blocks) * rows_of_block, rows_of_block)
                store = pltpu.make_async_copy(tiles.at[slot], target.at[place], store_sems.at[block])
                store.start()
                busy[slot] = store.wait
            yield
        for wait in busy:
            wait()
        for tile in range(width // LANES):
            small_sum_ref[norm_row + tile : norm_row + tile + 1, :] = norm_sum[:, tile * LANES : (tile + 1) * LANES]

    def smalls():
        small_sum_ref[...] = small_ref[...]
        yield from row_products()
        for level, peer in enumerate([peers[0], peers[1], beside, partner, middle]):
            copy = remote(small_sum_ref, small_got.at[level], peer, small_send.at[level], small_recv.at[level])
            copy.start()
            yield
            copy.wait()
            small_sum_ref[...] += small_got[level]

    def run(number, kind, start, rows, order, where):
        held = {name: ref.at[where] for name, ref in groups[kind == "shared", rows, order].items()}
        if kind == "in":
            group = 0 if start >= inner else 4
            local_start = start % inner
            ensure_columns(start // COLUMN_BLOCK * COLUMN_BLOCK)
            base_ref, base_start = grads, start
            place = lambda at, count: sum_in_ref.at[pl.ds(group, 4), pl.ds(pl.multiple_of(local_start + at, 16), count)]
        else:
            ensure_columns(2 * inner)
            base_ref, base_start = shared_sum, 0
            place = lambda at, count: sum_shared_ref.at[pl.ds(at, count)]
            copies = []
            for offset in range(3):
                copy = remote(
                    grads.at[pl.ds(2 * inner, rows), lanes_of(peers[offset][1])],
                    shared_in.at[offset], peers[offset], shared_send.at[offset], shared_recv.at[offset],
                )
                copy.start()
                copies.append(copy)
            yield
            total = grads[pl.ds(2 * inner, rows), lanes_of(me)].astype(F32)
            for offset in range(3):
                copies[offset].wait_recv()
                total = total + shared_in[offset].astype(F32)
            shared_sum[...] = total.astype(BF16)

        def source(at, count):
            return base_ref.at[pl.ds(pl.multiple_of(base_start + at, 16), count)]

        def link(from_ref, to_ref, device, slot):
            return remote(from_ref, to_ref, device, send_sems.at[number, slot], recv_sems.at[number, slot])

        def added(names_at, at, count):
            total = source(at, count)[...].astype(F32)
            for name, base in names_at:
                local = pl.multiple_of(at - base, count)
                total = total + held[name][pl.ds(local, count), :].astype(F32)
            return total

        two, four = rows // 2, rows // 4
        if order == "side":
            mine, other = pl.multiple_of(aside * two, two), pl.multiple_of((1 - aside) * two, two)
            low, high = pl.multiple_of(mine + half * four, four), pl.multiple_of(mine + (1 - half) * four, four)
            side = link(source(other, two), held["got"], beside, 0)
            side.start()
            yield
            side.wait_recv()
            lift = link(held["lift"], held["lift"], partner, 1)

            @pl.when(outside)
            def _():
                held["lift"][...] = added([("got", mine)], mine, two).astype(BF16)
                lift.start()

            yield
            bases = [("got", mine), ("lift", mine)]
            across = link(held["sent"], held["swapped"], middle, 2)

            @pl.when(inside)
            def _():
                lift.wait_recv()
                held["sent"][...] = added(bases, high, four).astype(BF16)
                across.start()

            yield
            bases = bases + [("swapped", low)]
        else:
            mine, other = pl.multiple_of(half * two, two), pl.multiple_of((1 - half) * two, two)
            low, high = pl.multiple_of(mine + aside * four, four), pl.multiple_of(mine + (1 - aside) * four, four)
            lift = link(source(0, rows), held["got"], partner, 1)

            @pl.when(outside)
            def _():
                lift.start()

            yield
            bases = [("got", 0)]
            across = link(held["sent"], held["swapped"], middle, 2)

            @pl.when(inside)
            def _():
                lift.wait_recv()
                held["sent"][...] = added(bases, other, two).astype(BF16)
                across.start()

            yield
            bases = bases + [("swapped", mine)]
            side = link(held["sent_side"], held["got_side"], beside, 0)

            @pl.when(inside)
            def _():
                across.wait_recv()
                held["sent_side"][...] = added(bases, high, four).astype(BF16)
                side.start()

            yield
            bases = bases + [("got_side", low)]

        final = held["final"]
        trade = []
        if kind == "in":
            target = sum_in_ref.at[group + me, pl.ds(pl.multiple_of(local_start + low, 16), four)]
            trade = [
                link(final.at[:, lanes_of(peers[offset][1])], target, peers[offset], 3 + offset) for offset in range(3)
            ]
            own = pltpu.make_async_copy(final.at[:, lanes_of(me)], target, local_sems.at[number])
        else:
            own = pltpu.make_async_copy(final, place(low, four), local_sems.at[number])

        if order == "side":
            back = [
                link(place(low, four), place(low, four), middle, 6),
                link(place(mine, two), place(mine, two), partner, 7),
                link(place(mine, two), place(mine, two), beside, 8),
            ]
        else:
            back = [
                link(place(low, four), place(low, four), beside, 6),
                link(place(mine, two), place(mine, two), middle, 7),
                link(place(0, rows), place(0, rows), partner, 8),
            ]

        @pl.when(inside)
        def _():
            (across if order == "side" else side).wait_recv()
            final[...] = added(bases, low, four).astype(BF16)
            for copy in trade:
                copy.start()
            own.start()

        yield AGAIN

        @pl.when(inside)
        def _():
            own.wait()
            for copy in trade:
                copy.wait_recv()
            back[0].start()

        yield

        @pl.when(inside)
        def _():
            back[0].wait_recv()
            back[1].start()
            if order == "side":
                back[2].start()

        yield
        if order == "side":

            @pl.when(outside)
            def _():
                back[1].wait_recv()
                back[2].start()

            yield
            back[2].wait_recv()
            side.wait_send()
            back[2].wait_send()

            @pl.when(outside)
            def _():
                lift.wait_send()

            @pl.when(inside)
            def _():
                across.wait_send()
                for copy in trade + back[:2]:
                    copy.wait_send()

        else:

            @pl.when(inside)
            def _():
                back[1].wait_recv()
                back[2].start()

            yield

            @pl.when(outside)
            def _():
                back[2].wait_recv()
                lift.wait_send()

            @pl.when(inside)
            def _():
                across.wait_send()
                side.wait_send()
                for copy in trade + back:
                    copy.wait_send()

        if kind == "shared":
            for copy in copies:
                copy.wait_send()

    waiting = [run(number, *chunk) for number, chunk in enumerate(chunks)]
    active, extra = [], [smalls(), activations()]

    def advance(running):
        still, again = [], []
        for steps in running:
            try:
                if next(steps) == AGAIN:
                    again.append(steps)
                still.append(steps)
            except StopIteration:
                pass
        for steps in again:
            next(steps)
        return still

    while waiting or active:
        active = advance(active + waiting[:PER_TURN])
        waiting = waiting[PER_TURN:]
        extra = advance(extra)
        next_columns()
    while extra:
        extra = advance(extra)


def reduce_gradients(size, depth, inner, common, norm_row, gp_first, gp_last, scaled, cols, tok_out, small):
    total, width = scaled.shape
    own_rows = tok_out.shape[1]
    chunks, counts = reduce_chunks(inner, common)
    scratch = []
    for (shared, rows, order), count in counts.items():
        for fraction in PARTS[order].values():
            scratch.append(pltpu.VMEM((count, rows // fraction, depth if shared else width), BF16))
    sems = pltpu.SemaphoreType.DMA
    half_blocks = total // 2 // ROW_BLOCK
    scratch += [
        pltpu.VMEM((3, common, depth), BF16),
        pltpu.VMEM((common, depth), BF16),
        pltpu.VMEM((5,) + small.shape, F32),
        pltpu.VMEM(scaled.shape, BF16),
        pltpu.VMEM(cols.shape, BF16),
        pltpu.VMEM(cols.shape, BF16),
        pltpu.VMEM((total, max(common, COLUMN_BLOCK)), BF16),
        pltpu.VMEM((max(common, COLUMN_BLOCK), total), BF16),
        pltpu.VMEM((ROW_BLOCK, gp_first.shape[1]), BF16),
        pltpu.VMEM((2, ROW_BLOCK, width), BF16),
        pltpu.VMEM((ROW_BLOCK, width), BF16),
        pltpu.VMEM((1, width), F32),
        sems((len(chunks), SLOTS)), sems((len(chunks), SLOTS)), sems((len(chunks),)),
        sems((2, TOKEN_PIECES)), sems((2, TOKEN_PIECES)), sems((5,)), sems((5,)), sems((3,)), sems((3,)),
        sems((half_blocks,)), sems((half_blocks,)), sems((6,)), sems((half_blocks,)),
    ]
    anywhere = pl.BlockSpec(memory_space=pltpu.HBM)
    local = pl.BlockSpec(memory_space=pltpu.VMEM)
    own = jax.ShapeDtypeStruct((own_rows, width), BF16)
    return pl.pallas_call(
        functools.partial(reduce_kernel, (chunks, counts, inner, depth, common, norm_row)),
        in_specs=[anywhere] * 5 + [local],
        out_specs=[anywhere] * 5 + [local] + [anywhere] * 2,
        out_shape=[
            jax.ShapeDtypeStruct((2 * size, inner, depth), BF16),
            jax.ShapeDtypeStruct((common, depth), BF16),
            own, own, own,
            jax.ShapeDtypeStruct(small.shape, F32),
            jax.ShapeDtypeStruct((half_blocks, ROW_BLOCK, width), BF16),
            own,
        ],
        scratch_shapes=scratch,
        compiler_params=pltpu.CompilerParams(
            collective_id=0, has_side_effects=True, vmem_limit_bytes=VMEM_LIMIT
        ),
        cost_estimate=pl.CostEstimate(
            flops=total * width, bytes_accessed=1 << 20, transcendentals=0
        ),
        name="reduce_gradients",
    )(gp_first, gp_last, scaled, cols, tok_out, small)


def small_pieces(size, copies, depth, inner, columns, me, replica, scaled_low, gp, normed_low, cot_all):
    replica_bits = axis_bits(copies)
    orders = [replica_bits, replica_bits[1:] + replica_bits[:1]]
    pieces = []
    part_rows = inner // 2
    for part in range(2):
        grad = contract_rows(normed_low[:, part * part_rows : (part + 1) * part_rows], cot_all)
        order = orders[part % 2]
        mine = halve_sum(grad[None], order, replica, copies)
        pieces.append(double_gather(mine.astype(BF16), order, replica, copies)[0])
    grad_w_out = jnp.concatenate(pieces, 0).astype(F32)


    def columns_sum(start, stop, order, shared):
        grad = contract_rows(scaled_low, gp[:, start:stop])
        mine = halve_sum(grad.reshape(size, depth, stop - start), order, replica, copies)
        own = lax.dynamic_index_in_dim(mine, me, 0, keepdims=False)
        got = [own]
        for offset in range(1, size):
            there = lax.dynamic_index_in_dim(mine, me ^ offset, 0, keepdims=False)
            got.append(swap(there.astype(BF16), "fsdp", size, offset))
        if shared:
            held = sum(block.astype(F32) for block in got)[None].astype(BF16)
        else:
            held = jnp.stack([block.astype(BF16) for block in got])
        return double_gather(held, order, replica, copies)

    halves = inner // 2
    value_parts = [columns_sum(c * halves, (c + 1) * halves, orders[c % 2], False) for c in range(2)]
    gate_parts = [
        columns_sum(inner + c * halves, inner + (c + 1) * halves, orders[c % 2], False) for c in range(2)
    ]
    shared_part = columns_sum(2 * inner, columns, orders[0], True)[0]

    def in_place(parts):
        placed = []
        for device in range(size):
            for part in parts:
                placed.append(lax.dynamic_index_in_dim(part, me ^ device, 0, keepdims=False))
        return placed

    grad_w_in = jnp.concatenate(in_place(gate_parts) + in_place(value_parts) + [shared_part], 1).astype(F32)
    return grad_w_in, grad_w_out


def recut(size, full_inner, inner, me, w_in):
    depth, full = w_in.shape

    def columns_of(device):
        return jnp.concatenate(
            [
                lax.dynamic_slice(w_in, (0, full_inner + device * inner), (depth, inner)),
                lax.dynamic_slice(w_in, (0, device * inner), (depth, inner)),
                w_in[:, 2 * full_inner :],
            ],
            1,
        )

    w_cols = jnp.zeros((size * depth, 2 * inner + full - 2 * full_inner), BF16)
    w_cols = lax.dynamic_update_slice(w_cols, columns_of(me), (me * depth, 0))
    for offset in range(1, size):
        received = swap(columns_of(me ^ offset), "fsdp", size, offset)
        w_cols = lax.dynamic_update_slice(w_cols, received, ((me ^ offset) * depth, 0))
    return w_cols


def on_device(copies, size, hidden_in, segment_ids, cotangent, norm_gain, w_in, conv_weight, conv_bias,
              dt_bias, a_log, skip_gain, gate_gain, w_out):
    micro_count, seq_count, tokens, width = hidden_in.shape
    own_rows = micro_count * seq_count * tokens
    total = size * own_rows
    inner = gate_gain.shape[0]
    local_heads = dt_bias.shape[0]
    heads = local_heads * size
    channel = inner // local_heads
    full_inner = inner * size
    taps, own_conv = conv_weight.shape
    conv_width = own_conv * size
    state2 = conv_width - full_inner
    depth = w_in.shape[0]
    common = state2 + heads
    columns = 2 * inner + common
    dims = (tokens, inner, state2, heads, local_heads, taps)
    me = lax.axis_index("fsdp")
    replica = lax.axis_index("replica")

    own_x = hidden_in.reshape(own_rows, width)
    own_cot = cotangent.reshape(own_rows, width)
    small = jnp.concatenate([norm_gain, conv_weight.reshape(-1), conv_bias])
    segments = segment_ids.reshape(micro_count * seq_count, tokens)
    fused = copies == 8 and size == 4 and sum(IN_ROWS) == 2 * inner
    if fused:
        padded = jnp.pad(small.astype(F32), (0, -small.shape[0] % (8 * LANES))).reshape(-1, LANES)
        scaled_low, seg_all, small, w_cols = gather_inputs(
            size, inner, own_x, segments.reshape(-1, LANES), padded, w_in.T
        )
        small = small.reshape(size, -1)
        own_cot_later, _ = lax.optimization_barrier((own_cot, seg_all))
        cot_across = swap(own_cot_later, "fsdp", size, 2)
        cot_beside = swap(own_cot_later, "fsdp", size, 1)
    else:
        small = lax.all_gather(small, "fsdp", axis=0, tiled=False).astype(F32)
        x_all = gather_relative(own_x, "fsdp", size).reshape(total, width)
        seg_all = gather_relative(segments, "fsdp", size)
        w_cols = recut(size, full_inner, inner, me, w_in).T
        cot_all = gather_relative(own_cot, "fsdp", size).reshape(total, width)
    seg_all = seg_all.reshape(total // tokens, tokens)
    full_norm = small[:, :depth].reshape(1, width)
    full_cw = small[:, depth : depth + taps * own_conv].reshape(size, taps, own_conv)
    full_cw = full_cw.transpose(1, 0, 2).reshape(taps, conv_width)
    full_cb = small[:, depth + taps * own_conv : depth + (taps + 1) * own_conv].reshape(1, conv_width)

    def normalise(inputs):
        wide = inputs.astype(F32)
        return lax.rsqrt(jnp.mean(wide * wide, -1, keepdims=True) + EPS)

    if not fused:
        scaled_low = norm_rows(x_all, full_norm)
    projected = contract_cols(scaled_low, w_cols)

    conv_all = jnp.concatenate([full_cw, full_cb, jnp.zeros((7 - taps, conv_width), F32)], 0)
    conv_own = jnp.concatenate(
        [lax.dynamic_slice(conv_all, (0, me * inner), (8, inner)), conv_all[:, full_inner:]], 1
    )
    pad_heads = lambda row: jnp.pad(row.astype(F32), (0, LANES - local_heads))
    head_rows = jnp.stack([pad_heads(dt_bias), pad_heads(-jnp.exp(a_log.astype(F32)))])
    head_rows = jnp.pad(head_rows, ((0, 6), (0, 0)))
    chan_rows = jnp.stack([jnp.repeat(skip_gain.astype(F32), channel), gate_gain.astype(F32)])
    chan_rows = jnp.pad(chan_rows, ((0, 6), (0, 0)))
    same = []
    for offset in range(1, taps):
        equal = (seg_all[:, offset:] == seg_all[:, :-offset]).astype(F32)
        same.append(jnp.pad(equal, ((0, 0), (offset, 0))))
    seg_wide = seg_all.astype(F32)
    same.append(seg_wide)
    same = jnp.pad(jnp.stack(same, 2), ((0, 0), (0, 0), (0, 8 - taps)))
    operands = (
        me.astype(jnp.int32).reshape(1), projected, seg_wide[:, None, :], same,
        head_rows, conv_own, chan_rows,
    )
    gated, squares, scan_out = mix_forward(dims, operands)
    if fused:
        cot_across, squares = lax.optimization_barrier((cot_across, squares))
        cot_all = jnp.concatenate([own_cot, cot_across, cot_beside, swap(cot_across, "fsdp", size, 1)], 0)
    twice = lambda row: jnp.stack([row, row])
    root = lax.rsqrt(sum_tokens(twice(squares[:, 0]), "fsdp", size)[0] / full_inner + EPS)
    normed_low = (gated.astype(F32) * root[:, None]).astype(BF16)
    w_later = w_out
    if fused:
        near = total // 2
        far_out = jnp.dot(gated[near:], w_out, preferred_element_type=F32).astype(BF16)
        normed_low, far_out = lax.optimization_barrier((normed_low, far_out))
        far_out = swap(far_out, "fsdp", size, 1)
        grad_out = contract_rows(normed_low, cot_all).astype(BF16)
        w_later, grad_out = lax.optimization_barrier((w_out, grad_out))
        own_out = lax.psum_scatter(grad_out, "replica", scatter_dimension=0, tiled=True)
    grad_normed = contract_cols(cot_all, w_later)
    cross = jnp.sum(gated.astype(F32) * grad_normed, 1)
    pull = root * root * root * sum_tokens(twice(cross), "fsdp", size)[0] / full_inner

    sequences = total // tokens
    stats = jnp.stack([root, pull], 1)
    if fused:
        early = sequences * 3 // 4
        gp_first, *small_first = mix_backward(dims, operands, stats, grad_normed, scan_out, 0, early)
        tok_out = jnp.dot(gated[:near], w_out, preferred_element_type=F32) + far_out.astype(F32)
        tok_out = tok_out.astype(BF16).reshape(2, own_rows, width)
        head_rows, own_out, small_first[2], tok_out = lax.optimization_barrier(
            (head_rows, own_out, small_first[2], tok_out)
        )
        grad_w_out = lax.all_gather(own_out, "replica", axis=0, tiled=True).astype(F32)
        operands = operands[:4] + (head_rows,) + operands[5:]
        gp_last, *small_last = mix_backward(
            dims, operands, stats, grad_normed, scan_out, early, sequences - early
        )
        grad_conv, grad_chan, grad_head = [first + last for first, last in zip(small_first, small_last)]
    else:
        gp, grad_conv, grad_chan, grad_head = mix_backward(
            dims, operands, stats, grad_normed, scan_out, 0, sequences
        )
    own_wide = own_x.astype(F32)
    own_root = normalise(own_x)

    conv_full = jnp.zeros((8, conv_width), F32)
    conv_full = lax.dynamic_update_slice(conv_full, grad_conv[:, inner:], (0, full_inner))
    conv_full = lax.dynamic_update_slice(conv_full, grad_conv[:, :inner], (0, me * inner))
    conv_full = conv_full[: taps + 1].reshape(-1)
    skip_grad = grad_chan[0].reshape(local_heads, channel).sum(1)
    own_small = jnp.concatenate(
        [grad_head[0, :local_heads], grad_head[1, :local_heads], skip_grad, grad_chan[1]]
    )

    if fused:
        spread = lax.dynamic_update_slice(jnp.zeros((size, own_small.shape[0]), F32), own_small[None], (me, 0))
        norm_row = -(-conv_full.shape[0] // LANES)
        conv_padded = jnp.pad(conv_full, (0, norm_row * LANES - conv_full.shape[0]))
        vector = jnp.concatenate([conv_padded, jnp.zeros((width,), F32), spread.reshape(-1)])
        vector = jnp.pad(vector, (0, -vector.shape[0] % (8 * LANES))).reshape(-1, LANES)
        sum_in, sum_shared, got_out, own_grad, got_grad, vector, _, _ = reduce_gradients(
            size, depth, inner, common, norm_row, gp_first, gp_last, scaled_low, w_cols, tok_out, vector
        )
        grad_w_in = jnp.concatenate([sum_in.reshape(2 * full_inner, depth), sum_shared], 0).astype(F32).T
        out_sum = tok_out[0].astype(F32) + got_out.astype(F32)
        grad_scaled = own_grad.astype(F32) + got_grad.astype(F32)
        vector = vector.reshape(-1)
        conv_full = vector[: conv_full.shape[0]]
        start = norm_row * LANES
        grad_norm = vector[start : start + width] / full_norm[0]
        start = start + width
        own_small = lax.dynamic_slice(vector, (start + me * own_small.shape[0],), own_small.shape)
    else:
        out_part = jnp.dot(gated, w_out, preferred_element_type=F32).astype(BF16)
        out_sum = scatter_relative(out_part.reshape(size, own_rows, width), "fsdp", size)
        grad_w_in, grad_w_out = small_pieces(
            size, copies, depth, inner, columns, me, replica, scaled_low, gp, normed_low, cot_all
        )
        scaled_part = jnp.dot(gp, w_cols, preferred_element_type=F32).astype(BF16)
        grad_scaled = scatter_relative(scaled_part.reshape(size, own_rows, width), "fsdp", size)
        grad_norm = jnp.sum(grad_scaled * own_wide * own_root, 0)
        conv_full, grad_norm = lax.psum((conv_full, grad_norm), ("replica", "fsdp"))
        own_small = lax.psum(own_small, "replica")

    block_out = (own_wide + root[:own_rows, None] * out_sum).astype(BF16).reshape(hidden_in.shape)
    gained = grad_scaled * full_norm
    inner_mean = jnp.mean(gained * own_wide, -1, keepdims=True)
    grad_in = own_cot.astype(F32) + own_root * gained - own_wide * (own_root * own_root * own_root * inner_mean)
    grad_in = grad_in.reshape(hidden_in.shape)
    conv_full = lax.dynamic_slice(conv_full.reshape(taps + 1, conv_width), (0, me * own_conv), (taps + 1, own_conv))
    grad_norm = lax.dynamic_slice(grad_norm, (me * depth,), (depth,))
    return (
        block_out,
        grad_in,
        grad_norm,
        grad_w_in,
        conv_full[:taps],
        conv_full[taps],
        own_small[:local_heads],
        own_small[local_heads : 2 * local_heads],
        own_small[2 * local_heads : 3 * local_heads],
        own_small[3 * local_heads :],
        grad_w_out,
    )


def solution(mesh):
    rows = ("replica", "fsdp")
    placed = (
        P(None, rows, None, None),
        P(None, rows, None),
        P(None, rows, None, None),
        P("fsdp"),
        P("fsdp", None),
        P(None, "fsdp"),
        P("fsdp"),
        P("fsdp"),
        P("fsdp"),
        P("fsdp"),
        P("fsdp"),
        P("fsdp", None),
    )
    return jax.shard_map(
        functools.partial(on_device, mesh.shape["replica"], mesh.shape["fsdp"]),
        mesh=mesh,
        in_specs=placed,
        out_specs=(
            P(None, rows, None, None),
            P(None, rows, None, None),
            P("fsdp"),
            P("fsdp", None),
            P(None, "fsdp"),
            P("fsdp"),
            P("fsdp"),
            P("fsdp"),
            P("fsdp"),
            P("fsdp"),
            P("fsdp", None),
        ),
        check_vma=False,
    )
```

```python
import functools

import jax
import jax.numpy as jnp
from jax import lax
from jax.experimental import pallas as pl
from jax.experimental.pallas import tpu as pltpu
from jax.sharding import PartitionSpec as P

EPS = 1e-05
HIGHEST = lax.Precision.HIGHEST
LANES = 128
F32 = jnp.float32
BF16 = jnp.bfloat16
LOG2E = 1.4426950408889634
VMEM_LIMIT = 60 << 20


def contract_rows(left, right, precision=None):
    return lax.dot_general(
        left, right, (((0,), (0,)), ((), ())), precision=precision, preferred_element_type=F32
    )


def contract_cols(left, right, precision=None):
    return lax.dot_general(
        left, right, (((1,), (1,)), ((), ())), precision=precision, preferred_element_type=F32
    )


def sigmoid(v):
    return 0.5 * jnp.tanh(0.5 * v) + 0.5


def convolve(conv_input, taps, bias, mask_refs):
    total = bias + taps[0] * conv_input
    shifted = []
    for offset in range(1, len(taps)):
        prior = pltpu.roll(conv_input, offset, 0) * mask_refs[offset - 1]
        shifted.append(prior)
        total = total + taps[offset] * prior
    return total, shifted


def prepare(dims, own_ref, proj_ref, seg_row_ref, mask_ref, head_ref, cw_ref,
            mask_wide, visible_bias, step_wide, cum_wide, cum_rows, state_act, affinity):
    tokens, inner, state2, heads, local_heads, taps = dims
    for offset in range(taps - 1):
        mask_wide[offset] = jnp.broadcast_to(mask_ref[:, offset : offset + 1], (tokens, LANES))
    rows = lax.broadcasted_iota(jnp.int32, (tokens, tokens), 0)
    cols = lax.broadcasted_iota(jnp.int32, (tokens, tokens), 1)
    visible = (rows >= cols) & (mask_ref[:, taps - 1 : taps] == seg_row_ref[...])
    visible_bias[...] = jnp.where(visible, 0.0, -1e30)
    common = 2 * inner
    raw = proj_ref[:, common + state2 : common + state2 + heads]
    raw = jnp.concatenate([raw, jnp.zeros((tokens, LANES - heads), F32)], 1)
    raw = pltpu.roll(raw, LANES - own_ref[0] * local_heads, 1)
    raw = raw + head_ref[0:1, :]
    step = jnp.maximum(raw, 0.0) + jnp.log1p(jnp.exp(-jnp.abs(raw)))
    log_decay = head_ref[1:2, :] * step
    lower = jnp.where(rows >= cols, 1.0, 0.0).astype(F32)
    cumulative = jnp.dot(lower, log_decay, precision=HIGHEST, preferred_element_type=F32)
    scaled_cum = cumulative * LOG2E
    flipped = scaled_cum.T
    lane = lax.broadcasted_iota(jnp.int32, (tokens, LANES), 1)
    for head in range(local_heads):
        cum_wide[head] = jnp.broadcast_to(scaled_cum[:, head : head + 1], (tokens, LANES))
        cum_rows[head] = flipped[head : head + 1, :]
    for pair in range(local_heads // 2):
        step_wide[pair] = jnp.where(
            lane < LANES // 2, step[:, 2 * pair : 2 * pair + 1], step[:, 2 * pair + 1 : 2 * pair + 2]
        )
    for part in range(state2 // LANES):
        at = inner + part * LANES
        conv, _ = convolve(
            proj_ref[:, common + part * LANES : common + (part + 1) * LANES],
            [cw_ref[j : j + 1, at : at + LANES] for j in range(taps)],
            cw_ref[taps : taps + 1, at : at + LANES],
            mask_wide,
        )
        state_act[part] = conv * sigmoid(conv)
    affinity[...] = contract_cols(state_act[1], state_act[0], HIGHEST)
    return raw, step, log_decay, rows, cols


def over_pairs(count, step, carry):
    group = 4 if count % 4 == 0 else 2

    def turn(index, carried):
        for inner in range(group):
            carried = step(index * group + inner, carried)
        return carried

    return lax.fori_loop(0, count // group, turn, carry)


def forward_kernel(dims, own_ref, proj_ref, seg_row_ref, mask_ref, head_ref, cw_ref, chan_ref,
                   gated_ref, square_ref, out_ref,
                   mask_wide, visible_bias, step_wide, cum_wide, cum_rows, state_act, affinity):
    tokens, inner, state2, heads, local_heads, taps = dims
    prepare(dims, own_ref, proj_ref, seg_row_ref, mask_ref, head_ref, cw_ref,
            mask_wide, visible_bias, step_wide, cum_wide, cum_rows, state_act, affinity)
    lane = lax.broadcasted_iota(jnp.int32, (tokens, LANES), 1)
    first = lane < LANES // 2
    blocks = tokens // LANES

    def pair_step(pair, squares):
        here = pl.ds(pl.multiple_of(pair * LANES, LANES), LANES)
        conv, _ = convolve(
            proj_ref[:, here], [cw_ref[j : j + 1, here] for j in range(taps)],
            cw_ref[taps : taps + 1, here], mask_wide,
        )
        values = conv * sigmoid(conv)
        weighted = values * step_wide[pair]
        out = chan_ref[0:1, here] * values
        parts = [out[b * LANES : (b + 1) * LANES] for b in range(blocks)]
        for which in range(2):
            head = 2 * pair + which
            mine = jnp.where(first == (which == 0), weighted, 0.0).astype(BF16)
            for tb in range(blocks):
                t_rows = slice(tb * LANES, (tb + 1) * LANES)
                pieces = []
                for sb in range(tb + 1):
                    s_cols = slice(sb * LANES, (sb + 1) * LANES)
                    distance = (cum_wide[head, t_rows, :] - cum_rows[head, :, s_cols]) + visible_bias[t_rows, s_cols]
                    pieces.append((affinity[t_rows, s_cols] * jnp.exp2(distance)).astype(BF16))
                weights = jnp.concatenate(pieces, 1) if tb > 0 else pieces[0]
                parts[tb] = parts[tb] + jnp.dot(
                    weights, mine[: (tb + 1) * LANES], preferred_element_type=F32
                )
        out = jnp.concatenate(parts, 0)
        out_ref[:, here] = out.astype(BF16)
        gate = proj_ref[:, pl.ds(pl.multiple_of(inner + pair * LANES, LANES), LANES)]
        gated = out * (gate * sigmoid(gate))
        gated_ref[:, here] = (gated * chan_ref[1:2, here]).astype(BF16)
        return squares + gated * gated

    squares = over_pairs(local_heads // 2, pair_step, jnp.zeros((tokens, LANES), F32))
    square_ref[...] = jnp.sum(squares, 1, keepdims=True)


def backward_kernel(dims, own_ref, proj_ref, seg_row_ref, mask_ref, head_ref, cw_ref, chan_ref,
                    stats_ref, gn_ref, out_ref,
                    gp_ref, grad_cw_ref, grad_chan_ref, grad_head_ref,
                    mask_wide, visible_bias, step_wide, cum_wide, cum_rows, state_act, affinity,
                    grad_affinity, row_sums, col_sums, wide_stats):
    tokens, inner, state2, heads, local_heads, taps = dims

    @pl.when(pl.program_id(0) == 0)
    def _():
        grad_cw_ref[...] = jnp.zeros_like(grad_cw_ref)
        grad_chan_ref[...] = jnp.zeros_like(grad_chan_ref)
        grad_head_ref[...] = jnp.zeros_like(grad_head_ref)

    raw, step, log_decay, rows, cols = prepare(
        dims, own_ref, proj_ref, seg_row_ref, mask_ref, head_ref, cw_ref,
        mask_wide, visible_bias, step_wide, cum_wide, cum_rows, state_act, affinity)
    grad_affinity[...] = jnp.zeros_like(grad_affinity)
    row_sums[...] = jnp.zeros_like(row_sums)
    col_sums[...] = jnp.zeros_like(col_sums)
    wide_stats[0] = jnp.broadcast_to(stats_ref[:, 0:1], (tokens, LANES))
    wide_stats[1] = jnp.broadcast_to(stats_ref[:, 1:2], (tokens, LANES))
    lane = lax.broadcasted_iota(jnp.int32, (tokens, LANES), 1)
    block_lane = lax.broadcasted_iota(jnp.int32, (LANES, LANES), 1)
    first = lane < LANES // 2
    blocks = tokens // LANES

    def conv_back(grad_conv, shifted, conv_input, here):
        grad_cw_ref[0:1, here] += jnp.sum(grad_conv * conv_input, 0, keepdims=True)
        grad_cw_ref[taps : taps + 1, here] += jnp.sum(grad_conv, 0, keepdims=True)
        back = cw_ref[0:1, here] * grad_conv
        for offset in range(1, taps):
            grad_cw_ref[offset : offset + 1, here] += jnp.sum(grad_conv * shifted[offset - 1], 0, keepdims=True)
            term = (cw_ref[offset : offset + 1, here] * grad_conv) * mask_wide[offset - 1]
            back = back + pltpu.roll(term, tokens - offset, 0)
        return back

    def pair_step(pair, carry):
        here = pl.ds(pl.multiple_of(pair * LANES, LANES), LANES)
        there = pl.ds(pl.multiple_of(inner + pair * LANES, LANES), LANES)
        conv_input = proj_ref[:, here]
        conv, shifted = convolve(
            conv_input, [cw_ref[j : j + 1, here] for j in range(taps)],
            cw_ref[taps : taps + 1, here], mask_wide,
        )
        conv_sig = sigmoid(conv)
        values = conv * conv_sig
        weighted = values * step_wide[pair]
        skip = chan_ref[0:1, here]
        halves = [jnp.where(first == (which == 0), weighted, 0.0).astype(BF16) for which in range(2)]
        out = out_ref[:, here].astype(F32)
        gate = proj_ref[:, there]
        gate_sig = sigmoid(gate)
        gate_silu = gate * gate_sig
        gated = out * gate_silu
        gn = gn_ref[:, here]
        gain = chan_ref[1:2, here]
        root = wide_stats[0]
        grad_chan_ref[1:2, here] += jnp.sum(gn * gated * root, 0, keepdims=True)
        grad_gated = root * (gn * gain) - gated * wide_stats[1]
        grad_out = grad_gated * gate_silu
        gp_ref[:, there] = (grad_gated * out * (gate_sig * (1.0 + gate * (1.0 - gate_sig)))).astype(BF16)
        grad_chan_ref[0:1, here] += jnp.sum(grad_out * values, 0, keepdims=True)
        back_parts = [jnp.zeros((LANES, LANES), F32) for _ in range(blocks)]
        for which in range(2):
            head = 2 * pair + which
            mine = jnp.where(first == (which == 0), grad_out, 0.0).astype(BF16)
            for tb in range(blocks):
                t_rows = slice(tb * LANES, (tb + 1) * LANES)
                sums = None
                for sb in range(tb + 1):
                    s_cols = slice(sb * LANES, (sb + 1) * LANES)
                    distance = (cum_wide[head, t_rows, :] - cum_rows[head, :, s_cols]) + visible_bias[t_rows, s_cols]
                    decay = jnp.exp2(distance)
                    weights = affinity[t_rows, s_cols] * decay
                    cross = contract_cols(mine[t_rows], halves[which][s_cols])
                    grad_affinity[t_rows, s_cols] += cross * decay
                    energy = cross * weights
                    col_sums[head, :, s_cols] += jnp.sum(energy, 0, keepdims=True)
                    sums = energy if sums is None else sums + energy
                    back_parts[sb] = back_parts[sb] + contract_rows(weights.astype(BF16), mine[t_rows])
                row_sums[t_rows, :] += jnp.where(
                    block_lane == head, jnp.sum(sums, 1, keepdims=True), 0.0
                )
        grad_values = jnp.concatenate(back_parts, 0) * step_wide[pair] + skip * grad_out
        grad_conv = grad_values * (conv_sig * (1.0 + conv * (1.0 - conv_sig)))
        gp_ref[:, here] = conv_back(grad_conv, shifted, conv_input, here).astype(BF16)
        return carry

    over_pairs(local_heads // 2, pair_step, 0)

    common = 2 * inner
    grad_states = [
        contract_rows(grad_affinity[...], state_act[1], HIGHEST),
        jnp.dot(grad_affinity[...], state_act[0], precision=HIGHEST, preferred_element_type=F32),
    ]
    for part in range(state2 // LANES):
        at = slice(inner + part * LANES, inner + (part + 1) * LANES)
        spot = slice(common + part * LANES, common + (part + 1) * LANES)
        conv_input = proj_ref[:, spot]
        conv, shifted = convolve(
            conv_input, [cw_ref[j : j + 1, at] for j in range(taps)], cw_ref[taps : taps + 1, at], mask_wide
        )
        conv_sig = sigmoid(conv)
        grad_conv = grad_states[part] * (conv_sig * (1.0 + conv * (1.0 - conv_sig)))
        gp_ref[:, spot] = conv_back(grad_conv, shifted, conv_input, at).astype(BF16)

    col_rows = [col_sums[head] for head in range(local_heads)]
    col_rows.append(jnp.zeros((LANES - local_heads, tokens), F32))
    col_energy = jnp.concatenate(col_rows, 0).T
    upper = jnp.where(cols >= rows, 1.0, 0.0).astype(F32)
    grad_decay = jnp.dot(upper, row_sums[...] - col_energy, precision=HIGHEST, preferred_element_type=F32)
    step_sig = sigmoid(raw)
    ratio = jnp.where(raw < -20.0, 1.0, step_sig / jnp.maximum(step, 1e-30))
    grad_raw = col_energy * ratio + (head_ref[1:2, :] * grad_decay) * step_sig
    grad_head_ref[0:1, :] += jnp.sum(grad_raw, 0, keepdims=True)
    grad_head_ref[1:2, :] += jnp.sum(grad_decay * log_decay, 0, keepdims=True)
    placed = pltpu.roll(grad_raw, own_ref[0] * local_heads, 1)
    gp_ref[:, common + state2 : common + state2 + heads] = placed[:, :heads].astype(BF16)


def mixer_specs(dims, width, start=0):
    tokens, inner, state2, heads, local_heads, taps = dims
    fixed = lambda shape: pl.BlockSpec(shape, lambda s: (0,) * len(shape))
    in_specs = [
        pl.BlockSpec(memory_space=pltpu.SMEM),
        pl.BlockSpec((tokens, width), lambda s: (s + start, 0)),
        pl.BlockSpec((None, 1, tokens), lambda s: (s + start, 0, 0)),
        pl.BlockSpec((None, tokens, 8), lambda s: (s + start, 0, 0)),
        fixed((8, LANES)),
        fixed((8, inner + state2)),
        fixed((8, inner)),
    ]
    scratch = [
        pltpu.VMEM((taps - 1, tokens, LANES), F32),
        pltpu.VMEM((tokens, tokens), F32),
        pltpu.VMEM((local_heads // 2, tokens, LANES), F32),
        pltpu.VMEM((local_heads, tokens, LANES), F32),
        pltpu.VMEM((local_heads, 1, tokens), F32),
        pltpu.VMEM((state2 // LANES, tokens, LANES), F32),
        pltpu.VMEM((tokens, tokens), F32),
    ]
    return in_specs, scratch


def mix_forward(dims, operands):
    tokens, inner, state2, heads, local_heads, taps = dims
    total, width = operands[1].shape
    in_specs, scratch = mixer_specs(dims, width)
    return pl.pallas_call(
        functools.partial(forward_kernel, dims),
        grid=(total // tokens,),
        in_specs=in_specs,
        out_specs=[
            pl.BlockSpec((tokens, inner), lambda s: (s, 0)),
            pl.BlockSpec((tokens, 1), lambda s: (s, 0)),
            pl.BlockSpec((tokens, inner), lambda s: (s, 0)),
        ],
        out_shape=[
            jax.ShapeDtypeStruct((total, inner), BF16),
            jax.ShapeDtypeStruct((total, 1), F32),
            jax.ShapeDtypeStruct((total, inner), BF16),
        ],
        scratch_shapes=scratch,
        compiler_params=pltpu.CompilerParams(vmem_limit_bytes=VMEM_LIMIT),
        cost_estimate=pl.CostEstimate(
            flops=total * local_heads * tokens * 4 * 64,
            bytes_accessed=total * width * 4,
            transcendentals=total * local_heads * tokens,
        ),
        name="mix_forward",
    )(*operands)


def mix_backward(dims, operands, stats, grad_normed, scan_out, start, count):
    tokens, inner, state2, heads, local_heads, taps = dims
    total, width = count * tokens, operands[1].shape[1]
    in_specs, scratch = mixer_specs(dims, width, start)
    fixed = lambda shape: pl.BlockSpec(shape, lambda s: (0,) * len(shape))
    return pl.pallas_call(
        functools.partial(backward_kernel, dims),
        grid=(count,),
        in_specs=in_specs + [
            pl.BlockSpec((tokens, 2), lambda s: (s + start, 0)),
            pl.BlockSpec((tokens, inner), lambda s: (s + start, 0)),
            pl.BlockSpec((tokens, inner), lambda s: (s + start, 0)),
        ],
        out_specs=[
            pl.BlockSpec((tokens, width), lambda s: (s, 0)),
            fixed((8, inner + state2)),
            fixed((8, inner)),
            fixed((8, LANES)),
        ],
        out_shape=[
            jax.ShapeDtypeStruct((total, width), BF16),
            jax.ShapeDtypeStruct((8, inner + state2), F32),
            jax.ShapeDtypeStruct((8, inner), F32),
            jax.ShapeDtypeStruct((8, LANES), F32),
        ],
        scratch_shapes=scratch + [
            pltpu.VMEM((tokens, tokens), F32),
            pltpu.VMEM((tokens, LANES), F32),
            pltpu.VMEM((local_heads, 1, tokens), F32),
            pltpu.VMEM((2, tokens, LANES), F32),
        ],
        compiler_params=pltpu.CompilerParams(vmem_limit_bytes=VMEM_LIMIT),
        cost_estimate=pl.CostEstimate(
            flops=total * local_heads * tokens * 12 * 64,
            bytes_accessed=total * width * 6,
            transcendentals=2 * total * local_heads * tokens,
        ),
        name="mix_backward",
    )(*operands, stats, grad_normed, scan_out)


def norm_kernel(x_ref, gain_ref, scaled_ref):
    wide = x_ref[...].astype(F32)
    root = lax.rsqrt(jnp.mean(wide * wide, 1, keepdims=True) + EPS)
    scaled_ref[...] = (wide * root * gain_ref[...]).astype(BF16)


def norm_rows(inputs, gain):
    rows, width = inputs.shape
    block = pl.BlockSpec((256, width), lambda s: (s, 0))
    return pl.pallas_call(
        norm_kernel,
        grid=(rows // 256,),
        in_specs=[block, pl.BlockSpec((1, width), lambda s: (0, 0))],
        out_specs=block,
        out_shape=jax.ShapeDtypeStruct(inputs.shape, BF16),
        compiler_params=pltpu.CompilerParams(vmem_limit_bytes=VMEM_LIMIT),
        cost_estimate=pl.CostEstimate(flops=4 * rows * width, bytes_accessed=4 * rows * width, transcendentals=rows),
        name="norm_rows",
    )(inputs, gain)


def swap(array, axis, size, bit):
    return lax.ppermute(array, axis, [(i, i ^ bit) for i in range(size)])


def axis_bits(size):
    bits = []
    bit = 1
    while bit < size:
        bits.append(bit)
        bit *= 2
    return bits


def gather_relative(array, axis, size):
    held = array[None]
    for bit in reversed(axis_bits(size)):
        held = jnp.concatenate([held, swap(held, axis, size, bit)], 0)
    return held


def scatter_relative(array, axis, size):
    total = array
    for bit in axis_bits(size):
        half = total.shape[0] // 2
        received = swap(total[half:].astype(BF16), axis, size, bit)
        total = total[:half].astype(F32) + received.astype(F32)
    return total[0]


def sum_tokens(array, axis, size):
    kinds, tokens = array.shape
    for bit in axis_bits(size):
        stride = tokens // (2 * bit)
        received = swap(array, axis, size, bit).reshape(kinds, bit, 2, stride)
        array = array + received[:, :, ::-1].reshape(kinds, tokens)
    return array


def halve_sum(array, order, replica, size):
    total = array
    for bit in order:
        blocks, rows, columns = total.shape
        mine = (replica // bit) % 2
        halves = total.reshape(blocks, 2, rows // 2, columns)
        kept = lax.dynamic_index_in_dim(halves, mine, 1, keepdims=False)
        sent = lax.dynamic_index_in_dim(halves, 1 - mine, 1, keepdims=False)
        received = swap(sent.astype(BF16), "replica", size, bit)
        total = kept + received.astype(F32)
    return total


def double_gather(array, order, replica, size):
    held = array
    for bit in reversed(order):
        received = swap(held, "replica", size, bit)
        upper = (replica // bit) % 2 == 1
        held = jnp.where(
            upper,
            jnp.concatenate([received, held], 1),
            jnp.concatenate([held, received], 1),
        )
    return held


def flip(index, bit):
    return index + bit * (1 - 2 * ((index // bit) % 2))


MESH = pl.DeviceIdType.MESH


def greet(peers):
    barrier = pltpu.get_barrier_semaphore()
    for peer in peers:
        pl.semaphore_signal(barrier, inc=1, device_id=peer, device_id_type=MESH)
    pl.semaphore_wait(barrier, len(peers))


def copy_peers(me):
    return [flip(me, 1), flip(me, 2), flip(flip(me, 1), 2)]


def gather_kernel(full_inner, inner, x_ref, seg_ref, small_ref, w_ref,
                  scaled_ref, seg_all_ref, small_all_ref, cols_ref,
                  x_all_ref, scaled, gain, cols_held, send_sems, recv_sems, local_sems, store_sems, norm_sems):
    me = lax.axis_index("fsdp")
    replica = lax.axis_index("replica")
    depth, common = w_ref.shape[1], w_ref.shape[0] - 2 * full_inner
    peers = [(replica, peer) for peer in copy_peers(me)]
    beside, above = (flip(replica, 1), me), (flip(replica, 2), me)
    greet(peers + [beside, above])
    number = [0]
    started = []

    def send(from_ref, to_ref, device):
        slot = number[0]
        number[0] += 1
        copy = pltpu.make_async_remote_copy(
            src_ref=from_ref, dst_ref=to_ref, send_sem=send_sems.at[slot], recv_sem=recv_sems.at[slot],
            device_id=device, device_id_type=MESH,
        )
        copy.start()
        started.append(copy)
        return copy

    parts = [(0, inner), (inner, inner), (2 * inner, common)]

    def targets(owner, first, count):
        lanes = pl.ds(pl.multiple_of(owner * depth, depth), depth)
        return [
            cols_ref.at[pl.ds(pl.multiple_of(base + first * (length // 4), 16), count * (length // 4)), lanes]
            for base, length in parts
        ]

    def sources(device, first, count):
        bases = [full_inner + device * inner, device * inner, 2 * full_inner]
        return [
            w_ref.at[pl.ds(pl.multiple_of(base + first * (length // 4), 16), count * (length // 4))]
            for base, (_, length) in zip(bases, parts)
        ]

    def send_parts(from_refs, to_refs, device):
        return [send(source, target, device) for source, target in zip(from_refs, to_refs)]

    spot = replica % 4
    smalls = [send(small_ref, small_all_ref.at[me], peer) for peer in peers]
    smalls += [send(seg_ref, seg_all_ref.at[slot], peer) for peer, slot in zip(peers, (2, 1, 3))]
    across = [send_parts(sources(peers[which][1], spot, 1), targets(me, spot, 1), peers[which]) for which in (1, 2)]
    x_y = send(x_ref, x_all_ref.at[1], peers[1])
    near = send_parts(sources(peers[0][1], 0, 4), targets(me, 0, 4), peers[0])
    x_near = send(x_ref, x_all_ref.at[2], peers[0])
    held = [cols_held.at[pl.ds(base, length)] for base, length in parts]
    own = list(zip(sources(me, 0, 4), held, targets(me, 0, 4)))
    loads = [pltpu.make_async_copy(source, held, local_sems.at[i]) for i, (source, held, _) in enumerate(own)]
    stores = [pltpu.make_async_copy(held, target, store_sems.at[i]) for i, (_, held, target) in enumerate(own)]
    x_own = pltpu.make_async_copy(x_ref, x_all_ref.at[0], local_sems.at[3])
    small_own = pltpu.make_async_copy(small_ref, small_all_ref.at[me], local_sems.at[4])
    stores.append(pltpu.make_async_copy(seg_ref, seg_all_ref.at[0], local_sems.at[5]))
    for copy in loads + [x_own, small_own, stores[-1]]:
        copy.start()
    for load, store in zip(loads, stores):
        load.wait()
        store.start()

    rows_at_once = 128
    block_rows, width = scaled.shape[1:]
    tiles_of_owner = depth // LANES

    def normalise(block):
        def step(piece, carry):
            rows = pl.ds(pl.multiple_of(piece * rows_at_once, rows_at_once), rows_at_once)
            wide = x_all_ref[block, rows, :].astype(F32)
            root = lax.rsqrt(jnp.mean(wide * wide, 1, keepdims=True) + EPS)
            scaled[block, rows, :] = (wide * root * gain[...]).astype(BF16)
            return carry

        lax.fori_loop(0, block_rows // rows_at_once, step, 0)
        store = pltpu.make_async_copy(
            scaled.at[block], scaled_ref.at[pl.ds(block * block_rows, block_rows)], norm_sems.at[block]
        )
        store.start()
        stores.append(store)

    small_own.wait()
    for copy in smalls:
        copy.wait_recv()
    for tile in range(width // LANES):
        gain[:, tile * LANES : (tile + 1) * LANES] = small_all_ref[
            tile // tiles_of_owner, tile % tiles_of_owner : tile % tiles_of_owner + 1, :
        ]
    x_own.wait()
    normalise(0)

    def relay(which, first, count, device):
        refs = targets(peers[which][1], first, count)
        return send_parts(refs, refs, device)

    for copy in across[0]:
        copy.wait_recv()
    first_beside = relay(1, spot, 1, beside)
    for copy in across[1]:
        copy.wait_recv()
    first_above = relay(2, spot, 1, above)
    for copy in first_beside:
        copy.wait_recv()
    last = relay(1, (spot // 2) * 2, 2, above)
    for copy in first_above:
        copy.wait_recv()
    last += relay(2, spot, 1, beside)
    last += relay(2, flip(spot, 2), 1, beside)
    x_near.wait_recv()
    normalise(2)
    x_y.wait_recv()
    x_last = send(x_all_ref.at[1], x_all_ref.at[3], peers[0])
    normalise(1)
    x_last.wait_recv()
    normalise(3)
    for copy in last + near:
        copy.wait_recv()
    for copy in stores:
        copy.wait()
    for copy in started:
        copy.wait_send()


GATHER_COPIES = 34


def gather_inputs(size, inner, x, segments, small, w_flipped):
    full, depth = w_flipped.shape
    full_inner = inner * size
    columns = 2 * inner + full - 2 * full_inner
    anywhere = pl.BlockSpec(memory_space=pltpu.HBM)
    return pl.pallas_call(
        functools.partial(gather_kernel, full_inner, inner),
        in_specs=[anywhere] * 4,
        out_specs=[anywhere] * 2 + [pl.BlockSpec(memory_space=pltpu.VMEM), anywhere],
        out_shape=[
            jax.ShapeDtypeStruct((size * x.shape[0], x.shape[1]), BF16),
            jax.ShapeDtypeStruct((size,) + segments.shape, jnp.int32),
            jax.ShapeDtypeStruct((size,) + small.shape, F32),
            jax.ShapeDtypeStruct((columns, size * depth), BF16),
        ],
        scratch_shapes=[
            pltpu.VMEM((size,) + x.shape, BF16),
            pltpu.VMEM((size,) + x.shape, BF16),
            pltpu.VMEM((1, x.shape[1]), F32),
            pltpu.VMEM((columns, depth), BF16),
            pltpu.SemaphoreType.DMA((GATHER_COPIES,)),
            pltpu.SemaphoreType.DMA((GATHER_COPIES,)),
            pltpu.SemaphoreType.DMA((6,)),
            pltpu.SemaphoreType.DMA((3,)),
            pltpu.SemaphoreType.DMA((4,)),
        ],
        compiler_params=pltpu.CompilerParams(
            collective_id=1, has_side_effects=True, vmem_limit_bytes=VMEM_LIMIT
        ),
        cost_estimate=pl.CostEstimate(flops=0, bytes_accessed=200 << 20, transcendentals=0),
        name="gather_inputs",
    )(x, segments, small, w_flipped)


PARTS = {
    "side": {"got": 2, "lift": 2, "sent": 4, "swapped": 4, "final": 4},
    "lift": {"got": 1, "sent": 2, "swapped": 2, "sent_side": 4, "got_side": 4, "final": 4},
}
SLOTS = 9
IN_ROWS = (64,) * 32
SHARED_AT = 4
COLUMN_BLOCK = 256
ROW_BLOCK = 256
LANE_TILE = 2048
PER_TURN = 3
AGAIN = 1
TOKEN_PIECES = 8


def reduce_chunks(inner, common):
    pieces = []
    start = 0
    for rows in IN_ROWS:
        pieces.append(("in", start, rows))
        start += rows
    pieces.insert(SHARED_AT, ("shared", 0, common))
    counts = {}
    placed = []
    for number, (kind, start, rows) in enumerate(pieces):
        order = "lift" if number % 3 == 2 else "side"
        key = (kind == "shared", rows, order)
        where = counts.get(key, 0)
        counts[key] = where + 1
        placed.append((kind, start, rows, order, where))
    return placed, counts


def reduce_kernel(plan, gp_first_ref, gp_last_ref, scaled_ref, cols_ref, tok_out_ref, small_ref,
                  sum_in_ref, sum_shared_ref, got_out_ref, own_grad_ref, got_grad_ref, small_sum_ref,
                  far_land_ref, across_ref, *scratch):
    chunks, counts, inner, depth, common, norm_row = plan
    groups = {}
    position = 0
    for key in counts:
        names = list(PARTS[key[2]])
        groups[key] = dict(zip(names, scratch[position : position + len(names)]))
        position += len(names)
    (shared_in, shared_sum, small_got, scaled, cols, grads, gp_cols, gp_flipped, gp_rows, tiles, far_tile, norm_sum,
     send_sems, recv_sems, local_sems, tok_send, tok_recv,
     small_send, small_recv, shared_send, shared_recv, far_send, far_recv, load_sems, store_sems) = scratch[position:]
    whole_loads = [
        pltpu.make_async_copy(scaled_ref, scaled, load_sems.at[0]),
        pltpu.make_async_copy(cols_ref, cols, load_sems.at[1]),
    ]
    for copy in whole_loads:
        copy.start()
    loaded = [False, False]

    def need(which):
        if not loaded[which]:
            whole_loads[which].wait()
            loaded[which] = True

    column_blocks = [(start, COLUMN_BLOCK) for start in range(0, 2 * inner, COLUMN_BLOCK)]
    column_blocks.insert(1, (2 * inner, common))
    width = scaled.shape[1]
    rows_of_block = tiles.shape[1]
    lane_tiles = width // LANE_TILE
    column_loads = []
    columns_done = []

    first_rows = gp_first_ref.shape[0]
    all_rows = first_rows + gp_last_ref.shape[0]

    def load_columns(number):
        if number < len(column_blocks):
            start, count = column_blocks[number]
            lanes = pl.ds(0, count)
            copies = [
                pltpu.make_async_copy(
                    gp_first_ref.at[:, pl.ds(start, count)], gp_cols.at[pl.ds(0, first_rows), lanes], load_sems.at[2]
                ),
                pltpu.make_async_copy(
                    gp_last_ref.at[:, pl.ds(start, count)],
                    gp_cols.at[pl.ds(first_rows, all_rows - first_rows), lanes], load_sems.at[5],
                ),
            ]
            for copy in copies:
                copy.start()
            column_loads.append(copies)

    def next_columns():
        number = len(columns_done)
        if number == len(column_blocks):
            return
        start, count = column_blocks[number]
        need(0)
        for copy in column_loads[number]:
            copy.wait()
        gp_flipped[pl.ds(0, count), :] = gp_cols[:, pl.ds(0, count)].T
        load_columns(number + 1)

        def lanes_step(tile, carry):
            lanes = pl.ds(pl.multiple_of(tile * LANE_TILE, LANE_TILE), LANE_TILE)
            grads[pl.ds(start, count), lanes] = jnp.dot(
                gp_flipped[pl.ds(0, count), :], scaled[:, lanes], preferred_element_type=F32
            ).astype(BF16)
            return carry

        lax.fori_loop(0, lane_tiles, lanes_step, 0)
        columns_done.append(start)

    def ensure_columns(start):
        while start not in columns_done:
            next_columns()

    load_columns(0)
    me = lax.axis_index("fsdp")
    replica = lax.axis_index("replica")
    up = replica // 2
    inside = (up == 1) | (up == 2)
    outside = (up == 0) | (up == 3)
    half = up // 2
    aside = replica % 2
    beside = (flip(replica, 1), me)
    partner = (flip(replica, 2), me)
    middle = (flip(flip(replica, 2), 4), me)
    peers = [(replica, peer) for peer in copy_peers(me)]
    greet(peers + [beside, partner, middle])

    def remote(from_ref, to_ref, device, sends, recvs):
        return pltpu.make_async_remote_copy(
            src_ref=from_ref, dst_ref=to_ref, send_sem=sends, recv_sem=recvs, device_id=device, device_id_type=MESH
        )

    def lanes_of(device):
        return pl.ds(pl.multiple_of(device * depth, depth), depth)

    def activations():
        rows = got_out_ref.shape[0] // TOKEN_PIECES
        copies = []
        for piece in range(TOKEN_PIECES):
            at = pl.ds(piece * rows, rows)
            copy = remote(tok_out_ref.at[1, at], got_out_ref.at[at], peers[1], tok_send.at[0, piece], tok_recv.at[0, piece])
            copy.start()
            copies.append(copy)
            yield
        for piece in range(TOKEN_PIECES):
            at = pl.ds(piece * rows, rows)
            copy = remote(across_ref.at[at], got_grad_ref.at[at], peers[1], tok_send.at[1, piece], tok_recv.at[1, piece])
            copy.start()
            copies.append(copy)
            yield
        for copy in copies:
            copy.wait()

    def row_products():
        half_blocks = all_rows // (2 * rows_of_block)
        quarter_blocks = half_blocks // 2
        later = list(range(quarter_blocks, half_blocks))
        sooner = list(range(quarter_blocks))
        order = [(True, i) for i in later] + [(False, i) for i in later]
        order += [(True, i) for i in sooner] + [(False, i) for i in sooner]
        norm_sum[...] = jnp.zeros_like(norm_sum)
        row_loads = []

        def load_rows(number):
            if number < len(order):
                far, block = order[number]
                at = (half_blocks + block if far else block) * rows_of_block
                if at < first_rows:
                    source = gp_first_ref.at[pl.ds(at, rows_of_block)]
                else:
                    source = gp_last_ref.at[pl.ds(at - first_rows, rows_of_block)]
                copy = pltpu.make_async_copy(source, gp_rows, load_sems.at[3])
                copy.start()
                row_loads.append((copy, at))

        load_rows(0)
        need(0)
        need(1)
        arrivals = {}
        busy = [None, None]
        for number, (far, block) in enumerate(order):
            slot = number % 2
            if busy[slot] is not None:
                busy[slot]()
            if not far:
                arrivals[block].wait_recv()
                load = pltpu.make_async_copy(far_land_ref.at[block], far_tile, load_sems.at[4])
                load.start()
                load.wait()
            copy, at = row_loads[number]
            copy.wait()

            def lanes_step(tile, carry):
                lanes = pl.ds(pl.multiple_of(tile * LANE_TILE, LANE_TILE), LANE_TILE)
                part = jnp.dot(gp_rows[...], cols[:, lanes], preferred_element_type=F32)
                norm_sum[:, lanes] += jnp.sum(
                    part * scaled[pl.ds(at, rows_of_block), lanes].astype(F32), 0, keepdims=True
                )
                if not far:
                    part = part + far_tile[:, lanes].astype(F32)
                tiles[slot, :, lanes] = part.astype(BF16)
                return carry

            lax.fori_loop(0, lane_tiles, lanes_step, 0)
            load_rows(number + 1)
            if far:
                sent = remote(tiles.at[slot], far_land_ref.at[block], peers[0], far_send.at[block], far_recv.at[block])
                sent.start()
                arrivals[block] = sent
                busy[slot] = sent.wait_send
            else:
                target = own_grad_ref if block < quarter_blocks else across_ref
                place = pl.ds((block % quarter_blocks) * rows_of_block, rows_of_block)
                store = pltpu.make_async_copy(tiles.at[slot], target.at[place], store_sems.at[block])
                store.start()
                busy[slot] = store.wait
            yield
        for wait in busy:
            wait()
        for tile in range(width // LANES):
            small_sum_ref[norm_row + tile : norm_row + tile + 1, :] = norm_sum[:, tile * LANES : (tile + 1) * LANES]

    def smalls():
        small_sum_ref[...] = small_ref[...]
        yield from row_products()
        for level, peer in enumerate([peers[0], peers[1], beside, partner, middle]):
            copy = remote(small_sum_ref, small_got.at[level], peer, small_send.at[level], small_recv.at[level])
            copy.start()
            yield
            copy.wait()
            small_sum_ref[...] += small_got[level]

    def run(number, kind, start, rows, order, where):
        held = {name: ref.at[where] for name, ref in groups[kind == "shared", rows, order].items()}
        if kind == "in":
            group = 0 if start >= inner else 4
            local_start = start % inner
            ensure_columns(start // COLUMN_BLOCK * COLUMN_BLOCK)
            base_ref, base_start = grads, start
            place = lambda at, count: sum_in_ref.at[pl.ds(group, 4), pl.ds(pl.multiple_of(local_start + at, 16), count)]
        else:
            ensure_columns(2 * inner)
            base_ref, base_start = shared_sum, 0
            place = lambda at, count: sum_shared_ref.at[pl.ds(at, count)]
            copies = []
            for offset in range(3):
                copy = remote(
                    grads.at[pl.ds(2 * inner, rows), lanes_of(peers[offset][1])],
                    shared_in.at[offset], peers[offset], shared_send.at[offset], shared_recv.at[offset],
                )
                copy.start()
                copies.append(copy)
            yield
            total = grads[pl.ds(2 * inner, rows), lanes_of(me)].astype(F32)
            for offset in range(3):
                copies[offset].wait_recv()
                total = total + shared_in[offset].astype(F32)
            shared_sum[...] = total.astype(BF16)

        def source(at, count):
            return base_ref.at[pl.ds(pl.multiple_of(base_start + at, 16), count)]

        def link(from_ref, to_ref, device, slot):
            return remote(from_ref, to_ref, device, send_sems.at[number, slot], recv_sems.at[number, slot])

        def added(names_at, at, count):
            total = source(at, count)[...].astype(F32)
            for name, base in names_at:
                local = pl.multiple_of(at - base, count)
                total = total + held[name][pl.ds(local, count), :].astype(F32)
            return total

        two, four = rows // 2, rows // 4
        if order == "side":
            mine, other = pl.multiple_of(aside * two, two), pl.multiple_of((1 - aside) * two, two)
            low, high = pl.multiple_of(mine + half * four, four), pl.multiple_of(mine + (1 - half) * four, four)
            side = link(source(other, two), held["got"], beside, 0)
            side.start()
            yield
            side.wait_recv()
            lift = link(held["lift"], held["lift"], partner, 1)

            @pl.when(outside)
            def _():
                held["lift"][...] = added([("got", mine)], mine, two).astype(BF16)
                lift.start()

            yield
            bases = [("got", mine), ("lift", mine)]
            across = link(held["sent"], held["swapped"], middle, 2)

            @pl.when(inside)
            def _():
                lift.wait_recv()
                held["sent"][...] = added(bases, high, four).astype(BF16)
                across.start()

            yield
            bases = bases + [("swapped", low)]
        else:
            mine, other = pl.multiple_of(half * two, two), pl.multiple_of((1 - half) * two, two)
            low, high = pl.multiple_of(mine + aside * four, four), pl.multiple_of(mine + (1 - aside) * four, four)
            lift = link(source(0, rows), held["got"], partner, 1)

            @pl.when(outside)
            def _():
                lift.start()

            yield
            bases = [("got", 0)]
            across = link(held["sent"], held["swapped"], middle, 2)

            @pl.when(inside)
            def _():
                lift.wait_recv()
                held["sent"][...] = added(bases, other, two).astype(BF16)
                across.start()

            yield
            bases = bases + [("swapped", mine)]
            side = link(held["sent_side"], held["got_side"], beside, 0)

            @pl.when(inside)
            def _():
                across.wait_recv()
                held["sent_side"][...] = added(bases, high, four).astype(BF16)
                side.start()

            yield
            bases = bases + [("got_side", low)]

        final = held["final"]
        trade = []
        if kind == "in":
            target = sum_in_ref.at[group + me, pl.ds(pl.multiple_of(local_start + low, 16), four)]
            trade = [
                link(final.at[:, lanes_of(peers[offset][1])], target, peers[offset], 3 + offset) for offset in range(3)
            ]
            own = pltpu.make_async_copy(final.at[:, lanes_of(me)], target, local_sems.at[number])
        else:
            own = pltpu.make_async_copy(final, place(low, four), local_sems.at[number])

        if order == "side":
            back = [
                link(place(low, four), place(low, four), middle, 6),
                link(place(mine, two), place(mine, two), partner, 7),
                link(place(mine, two), place(mine, two), beside, 8),
            ]
        else:
            back = [
                link(place(low, four), place(low, four), beside, 6),
                link(place(mine, two), place(mine, two), middle, 7),
                link(place(0, rows), place(0, rows), partner, 8),
            ]

        @pl.when(inside)
        def _():
            (across if order == "side" else side).wait_recv()
            final[...] = added(bases, low, four).astype(BF16)
            for copy in trade:
                copy.start()
            own.start()

        yield AGAIN

        @pl.when(inside)
        def _():
            own.wait()
            for copy in trade:
                copy.wait_recv()
            back[0].start()

        yield

        @pl.when(inside)
        def _():
            back[0].wait_recv()
            back[1].start()
            if order == "side":
                back[2].start()

        yield
        if order == "side":

            @pl.when(outside)
            def _():
                back[1].wait_recv()
                back[2].start()

            yield
            back[2].wait_recv()
            side.wait_send()
            back[2].wait_send()

            @pl.when(outside)
            def _():
                lift.wait_send()

            @pl.when(inside)
            def _():
                across.wait_send()
                for copy in trade + back[:2]:
                    copy.wait_send()

        else:

            @pl.when(inside)
            def _():
                back[1].wait_recv()
                back[2].start()

            yield

            @pl.when(outside)
            def _():
                back[2].wait_recv()
                lift.wait_send()

            @pl.when(inside)
            def _():
                across.wait_send()
                side.wait_send()
                for copy in trade + back:
                    copy.wait_send()

        if kind == "shared":
            for copy in copies:
                copy.wait_send()

    waiting = [run(number, *chunk) for number, chunk in enumerate(chunks)]
    active, extra = [], [smalls(), activations()]

    def advance(running):
        still, again = [], []
        for steps in running:
            try:
                if next(steps) == AGAIN:
                    again.append(steps)
                still.append(steps)
            except StopIteration:
                pass
        for steps in again:
            next(steps)
        return still

    while waiting or active:
        active = advance(active + waiting[:PER_TURN])
        waiting = waiting[PER_TURN:]
        extra = advance(extra)
        next_columns()
    while extra:
        extra = advance(extra)


def reduce_gradients(size, depth, inner, common, norm_row, gp_first, gp_last, scaled, cols, tok_out, small):
    total, width = scaled.shape
    own_rows = tok_out.shape[1]
    chunks, counts = reduce_chunks(inner, common)
    scratch = []
    for (shared, rows, order), count in counts.items():
        for fraction in PARTS[order].values():
            scratch.append(pltpu.VMEM((count, rows // fraction, depth if shared else width), BF16))
    sems = pltpu.SemaphoreType.DMA
    half_blocks = total // 2 // ROW_BLOCK
    scratch += [
        pltpu.VMEM((3, common, depth), BF16),
        pltpu.VMEM((common, depth), BF16),
        pltpu.VMEM((5,) + small.shape, F32),
        pltpu.VMEM(scaled.shape, BF16),
        pltpu.VMEM(cols.shape, BF16),
        pltpu.VMEM(cols.shape, BF16),
        pltpu.VMEM((total, max(common, COLUMN_BLOCK)), BF16),
        pltpu.VMEM((max(common, COLUMN_BLOCK), total), BF16),
        pltpu.VMEM((ROW_BLOCK, gp_first.shape[1]), BF16),
        pltpu.VMEM((2, ROW_BLOCK, width), BF16),
        pltpu.VMEM((ROW_BLOCK, width), BF16),
        pltpu.VMEM((1, width), F32),
        sems((len(chunks), SLOTS)), sems((len(chunks), SLOTS)), sems((len(chunks),)),
        sems((2, TOKEN_PIECES)), sems((2, TOKEN_PIECES)), sems((5,)), sems((5,)), sems((3,)), sems((3,)),
        sems((half_blocks,)), sems((half_blocks,)), sems((6,)), sems((half_blocks,)),
    ]
    anywhere = pl.BlockSpec(memory_space=pltpu.HBM)
    local = pl.BlockSpec(memory_space=pltpu.VMEM)
    own = jax.ShapeDtypeStruct((own_rows, width), BF16)
    return pl.pallas_call(
        functools.partial(reduce_kernel, (chunks, counts, inner, depth, common, norm_row)),
        in_specs=[anywhere] * 5 + [local],
        out_specs=[anywhere] * 5 + [local] + [anywhere] * 2,
        out_shape=[
            jax.ShapeDtypeStruct((2 * size, inner, depth), BF16),
            jax.ShapeDtypeStruct((common, depth), BF16),
            own, own, own,
            jax.ShapeDtypeStruct(small.shape, F32),
            jax.ShapeDtypeStruct((half_blocks, ROW_BLOCK, width), BF16),
            own,
        ],
        scratch_shapes=scratch,
        compiler_params=pltpu.CompilerParams(
            collective_id=0, has_side_effects=True, vmem_limit_bytes=VMEM_LIMIT
        ),
        cost_estimate=pl.CostEstimate(
            flops=total * width, bytes_accessed=1 << 20, transcendentals=0
        ),
        name="reduce_gradients",
    )(gp_first, gp_last, scaled, cols, tok_out, small)


def small_pieces(size, copies, depth, inner, columns, me, replica, scaled_low, gp, normed_low, cot_all):
    replica_bits = axis_bits(copies)
    orders = [replica_bits, replica_bits[1:] + replica_bits[:1]]
    pieces = []
    part_rows = inner // 2
    for part in range(2):
        grad = contract_rows(normed_low[:, part * part_rows : (part + 1) * part_rows], cot_all)
        order = orders[part % 2]
        mine = halve_sum(grad[None], order, replica, copies)
        pieces.append(double_gather(mine.astype(BF16), order, replica, copies)[0])
    grad_w_out = jnp.concatenate(pieces, 0).astype(F32)


    def columns_sum(start, stop, order, shared):
        grad = contract_rows(scaled_low, gp[:, start:stop])
        mine = halve_sum(grad.reshape(size, depth, stop - start), order, replica, copies)
        own = lax.dynamic_index_in_dim(mine, me, 0, keepdims=False)
        got = [own]
        for offset in range(1, size):
            there = lax.dynamic_index_in_dim(mine, me ^ offset, 0, keepdims=False)
            got.append(swap(there.astype(BF16), "fsdp", size, offset))
        if shared:
            held = sum(block.astype(F32) for block in got)[None].astype(BF16)
        else:
            held = jnp.stack([block.astype(BF16) for block in got])
        return double_gather(held, order, replica, copies)

    halves = inner // 2
    value_parts = [columns_sum(c * halves, (c + 1) * halves, orders[c % 2], False) for c in range(2)]
    gate_parts = [
        columns_sum(inner + c * halves, inner + (c + 1) * halves, orders[c % 2], False) for c in range(2)
    ]
    shared_part = columns_sum(2 * inner, columns, orders[0], True)[0]

    def in_place(parts):
        placed = []
        for device in range(size):
            for part in parts:
                placed.append(lax.dynamic_index_in_dim(part, me ^ device, 0, keepdims=False))
        return placed

    grad_w_in = jnp.concatenate(in_place(gate_parts) + in_place(value_parts) + [shared_part], 1).astype(F32)
    return grad_w_in, grad_w_out


def recut(size, full_inner, inner, me, w_in):
    depth, full = w_in.shape

    def columns_of(device):
        return jnp.concatenate(
            [
                lax.dynamic_slice(w_in, (0, full_inner + device * inner), (depth, inner)),
                lax.dynamic_slice(w_in, (0, device * inner), (depth, inner)),
                w_in[:, 2 * full_inner :],
            ],
            1,
        )

    w_cols = jnp.zeros((size * depth, 2 * inner + full - 2 * full_inner), BF16)
    w_cols = lax.dynamic_update_slice(w_cols, columns_of(me), (me * depth, 0))
    for offset in range(1, size):
        received = swap(columns_of(me ^ offset), "fsdp", size, offset)
        w_cols = lax.dynamic_update_slice(w_cols, received, ((me ^ offset) * depth, 0))
    return w_cols


def on_device(copies, size, hidden_in, segment_ids, cotangent, norm_gain, w_in, conv_weight, conv_bias,
              dt_bias, a_log, skip_gain, gate_gain, w_out):
    micro_count, seq_count, tokens, width = hidden_in.shape
    own_rows = micro_count * seq_count * tokens
    total = size * own_rows
    inner = gate_gain.shape[0]
    local_heads = dt_bias.shape[0]
    heads = local_heads * size
    channel = inner // local_heads
    full_inner = inner * size
    taps, own_conv = conv_weight.shape
    conv_width = own_conv * size
    state2 = conv_width - full_inner
    depth = w_in.shape[0]
    common = state2 + heads
    columns = 2 * inner + common
    dims = (tokens, inner, state2, heads, local_heads, taps)
    me = lax.axis_index("fsdp")
    replica = lax.axis_index("replica")

    own_x = hidden_in.reshape(own_rows, width)
    own_cot = cotangent.reshape(own_rows, width)
    small = jnp.concatenate([norm_gain, conv_weight.reshape(-1), conv_bias])
    segments = segment_ids.reshape(micro_count * seq_count, tokens)
    fused = copies == 8 and size == 4 and sum(IN_ROWS) == 2 * inner
    if fused:
        padded = jnp.pad(small.astype(F32), (0, -small.shape[0] % (8 * LANES))).reshape(-1, LANES)
        scaled_low, seg_all, small, w_cols = gather_inputs(
            size, inner, own_x, segments.reshape(-1, LANES), padded, w_in.T
        )
        small = small.reshape(size, -1)
        own_cot_later, _ = lax.optimization_barrier((own_cot, seg_all))
        cot_across = swap(own_cot_later, "fsdp", size, 2)
        cot_beside = swap(own_cot_later, "fsdp", size, 1)
    else:
        small = lax.all_gather(small, "fsdp", axis=0, tiled=False).astype(F32)
        x_all = gather_relative(own_x, "fsdp", size).reshape(total, width)
        seg_all = gather_relative(segments, "fsdp", size)
        w_cols = recut(size, full_inner, inner, me, w_in).T
        cot_all = gather_relative(own_cot, "fsdp", size).reshape(total, width)
    seg_all = seg_all.reshape(total // tokens, tokens)
    full_norm = small[:, :depth].reshape(1, width)
    full_cw = small[:, depth : depth + taps * own_conv].reshape(size, taps, own_conv)
    full_cw = full_cw.transpose(1, 0, 2).reshape(taps, conv_width)
    full_cb = small[:, depth + taps * own_conv : depth + (taps + 1) * own_conv].reshape(1, conv_width)

    def normalise(inputs):
        wide = inputs.astype(F32)
        return lax.rsqrt(jnp.mean(wide * wide, -1, keepdims=True) + EPS)

    if not fused:
        scaled_low = norm_rows(x_all, full_norm)
    projected = contract_cols(scaled_low, w_cols)

    conv_all = jnp.concatenate([full_cw, full_cb, jnp.zeros((7 - taps, conv_width), F32)], 0)
    conv_own = jnp.concatenate(
        [lax.dynamic_slice(conv_all, (0, me * inner), (8, inner)), conv_all[:, full_inner:]], 1
    )
    pad_heads = lambda row: jnp.pad(row.astype(F32), (0, LANES - local_heads))
    head_rows = jnp.stack([pad_heads(dt_bias), pad_heads(-jnp.exp(a_log.astype(F32)))])
    head_rows = jnp.pad(head_rows, ((0, 6), (0, 0)))
    chan_rows = jnp.stack([jnp.repeat(skip_gain.astype(F32), channel), gate_gain.astype(F32)])
    chan_rows = jnp.pad(chan_rows, ((0, 6), (0, 0)))
    same = []
    for offset in range(1, taps):
        equal = (seg_all[:, offset:] == seg_all[:, :-offset]).astype(F32)
        same.append(jnp.pad(equal, ((0, 0), (offset, 0))))
    seg_wide = seg_all.astype(F32)
    same.append(seg_wide)
    same = jnp.pad(jnp.stack(same, 2), ((0, 0), (0, 0), (0, 8 - taps)))
    operands = (
        me.astype(jnp.int32).reshape(1), projected, seg_wide[:, None, :], same,
        head_rows, conv_own, chan_rows,
    )
    gated, squares, scan_out = mix_forward(dims, operands)
    if fused:
        cot_across, squares = lax.optimization_barrier((cot_across, squares))
        cot_all = jnp.concatenate([own_cot, cot_across, cot_beside, swap(cot_across, "fsdp", size, 1)], 0)
    twice = lambda row: jnp.stack([row, row])
    root = lax.rsqrt(sum_tokens(twice(squares[:, 0]), "fsdp", size)[0] / full_inner + EPS)
    normed_low = (gated.astype(F32) * root[:, None]).astype(BF16)
    w_later = w_out
    if fused:
        near = total // 2
        far_out = jnp.dot(gated[near:], w_out, preferred_element_type=F32).astype(BF16)
        normed_low, far_out = lax.optimization_barrier((normed_low, far_out))
        far_out = swap(far_out, "fsdp", size, 1)
        grad_out = contract_rows(normed_low, cot_all).astype(BF16)
        w_later, grad_out = lax.optimization_barrier((w_out, grad_out))
        own_out = lax.psum_scatter(grad_out, "replica", scatter_dimension=0, tiled=True)
    grad_normed = contract_cols(cot_all, w_later)
    cross = jnp.sum(gated.astype(F32) * grad_normed, 1)
    pull = root * root * root * sum_tokens(twice(cross), "fsdp", size)[0] / full_inner

    sequences = total // tokens
    stats = jnp.stack([root, pull], 1)
    if fused:
        early = sequences * 3 // 4
        gp_first, *small_first = mix_backward(dims, operands, stats, grad_normed, scan_out, 0, early)
        tok_out = jnp.dot(gated[:near], w_out, preferred_element_type=F32) + far_out.astype(F32)
        tok_out = tok_out.astype(BF16).reshape(2, own_rows, width)
        head_rows, own_out, small_first[2], tok_out = lax.optimization_barrier(
            (head_rows, own_out, small_first[2], tok_out)
        )
        grad_w_out = lax.all_gather(own_out, "replica", axis=0, tiled=True).astype(F32)
        operands = operands[:4] + (head_rows,) + operands[5:]
        gp_last, *small_last = mix_backward(
            dims, operands, stats, grad_normed, scan_out, early, sequences - early
        )
        grad_conv, grad_chan, grad_head = [first + last for first, last in zip(small_first, small_last)]
    else:
        gp, grad_conv, grad_chan, grad_head = mix_backward(
            dims, operands, stats, grad_normed, scan_out, 0, sequences
        )
    own_wide = own_x.astype(F32)
    own_root = normalise(own_x)

    conv_full = jnp.zeros((8, conv_width), F32)
    conv_full = lax.dynamic_update_slice(conv_full, grad_conv[:, inner:], (0, full_inner))
    conv_full = lax.dynamic_update_slice(conv_full, grad_conv[:, :inner], (0, me * inner))
    conv_full = conv_full[: taps + 1].reshape(-1)
    skip_grad = grad_chan[0].reshape(local_heads, channel).sum(1)
    own_small = jnp.concatenate(
        [grad_head[0, :local_heads], grad_head[1, :local_heads], skip_grad, grad_chan[1]]
    )

    if fused:
        spread = lax.dynamic_update_slice(jnp.zeros((size, own_small.shape[0]), F32), own_small[None], (me, 0))
        norm_row = -(-conv_full.shape[0] // LANES)
        conv_padded = jnp.pad(conv_full, (0, norm_row * LANES - conv_full.shape[0]))
        vector = jnp.concatenate([conv_padded, jnp.zeros((width,), F32), spread.reshape(-1)])
        vector = jnp.pad(vector, (0, -vector.shape[0] % (8 * LANES))).reshape(-1, LANES)
        sum_in, sum_shared, got_out, own_grad, got_grad, vector, _, _ = reduce_gradients(
            size, depth, inner, common, norm_row, gp_first, gp_last, scaled_low, w_cols, tok_out, vector
        )
        grad_w_in = jnp.concatenate([sum_in.reshape(2 * full_inner, depth), sum_shared], 0).astype(F32).T
        out_sum = tok_out[0].astype(F32) + got_out.astype(F32)
        grad_scaled = own_grad.astype(F32) + got_grad.astype(F32)
        vector = vector.reshape(-1)
        conv_full = vector[: conv_full.shape[0]]
        start = norm_row * LANES
        grad_norm = vector[start : start + width] / full_norm[0]
        start = start + width
        own_small = lax.dynamic_slice(vector, (start + me * own_small.shape[0],), own_small.shape)
    else:
        out_part = jnp.dot(gated, w_out, preferred_element_type=F32).astype(BF16)
        out_sum = scatter_relative(out_part.reshape(size, own_rows, width), "fsdp", size)
        grad_w_in, grad_w_out = small_pieces(
            size, copies, depth, inner, columns, me, replica, scaled_low, gp, normed_low, cot_all
        )
        scaled_part = jnp.dot(gp, w_cols, preferred_element_type=F32).astype(BF16)
        grad_scaled = scatter_relative(scaled_part.reshape(size, own_rows, width), "fsdp", size)
        grad_norm = jnp.sum(grad_scaled * own_wide * own_root, 0)
        conv_full, grad_norm = lax.psum((conv_full, grad_norm), ("replica", "fsdp"))
        own_small = lax.psum(own_small, "replica")

    block_out = (own_wide + root[:own_rows, None] * out_sum).astype(BF16).reshape(hidden_in.shape)
    gained = grad_scaled * full_norm
    inner_mean = jnp.mean(gained * own_wide, -1, keepdims=True)
    grad_in = own_cot.astype(F32) + own_root * gained - own_wide * (own_root * own_root * own_root * inner_mean)
    grad_in = grad_in.reshape(hidden_in.shape)
    conv_full = lax.dynamic_slice(conv_full.reshape(taps + 1, conv_width), (0, me * own_conv), (taps + 1, own_conv))
    grad_norm = lax.dynamic_slice(grad_norm, (me * depth,), (depth,))
    return (
        block_out,
        grad_in,
        grad_norm,
        grad_w_in,
        conv_full[:taps],
        conv_full[taps],
        own_small[:local_heads],
        own_small[local_heads : 2 * local_heads],
        own_small[2 * local_heads : 3 * local_heads],
        own_small[3 * local_heads :],
        grad_w_out,
    )


def solution(mesh):
    rows = ("replica", "fsdp")
    placed = (
        P(None, rows, None, None),
        P(None, rows, None),
        P(None, rows, None, None),
        P("fsdp"),
        P("fsdp", None),
        P(None, "fsdp"),
        P("fsdp"),
        P("fsdp"),
        P("fsdp"),
        P("fsdp"),
        P("fsdp"),
        P("fsdp", None),
    )
    return jax.shard_map(
        functools.partial(on_device, mesh.shape["replica"], mesh.shape["fsdp"]),
        mesh=mesh,
        in_specs=placed,
        out_specs=(
            P(None, rows, None, None),
            P(None, rows, None, None),
            P("fsdp"),
            P("fsdp", None),
            P(None, "fsdp"),
            P("fsdp"),
            P("fsdp"),
            P("fsdp"),
            P("fsdp"),
            P("fsdp"),
            P("fsdp", None),
        ),
        check_vma=False,
    )
```
